32 devices in a mesh: space: 4 (over z), member: 8 (over y, x, core).
Axes of the slice: x: 2, y: 2, z: 4, core: 2. Of those that a mesh axis runs over, the one named last changes fastest.
Arguments:
- prior_ensemble: float32 [32, 32, 512], P('member', None, 'space'), may hold values from -12 to 12, as said below
- wind: float32 [32, 512], P(None, 'space'), may hold values from -1 to 1
- obs_value: float32 [32, 512], P(('space', 'member')), may hold values from -6 to 6
- obs_weight: float32 [32, 512], P(('space', 'member')), may hold values from 0.25 to 4
- observed_cell_value: int32 [32, 512], P(('space', 'member')), may hold values from 0 to 511
- obs_count: int32 [32], P(('space', 'member')), may hold values from 64 to 512, as said below
Outputs:
- analysis: float32 [32, 32, 512], P('member', None, 'space')
The draws below stay inside these ranges and needn't reach their ends.
Inputs may be any that keep to these rules, and one draw needn't show every extreme that they name: `prior_ensemble`: member states are rough from cell to cell, member scales differ. `obs_count`: some patch has all 512 slots live and some has 64 live.
All inputs are finite; a program needn't handle non-finite values.
Results may differ from the reference program's by a relative error of at most 0.0003.
Values sent between devices are 32-bit elements; how exact they have to be, the bound alone decides.
No kernel may reach another device: no remote copies, remote signals or barrier semaphores. Data moves between devices by JAX's collectives and lax.ppermute only.
A program may use at most 64 MiB of HBM per device.

```python
import math
import jax
import jax.numpy as jnp
from jax import lax

REGION_HEIGHT = 4
TILE_WIDTH = 128
OBS_MAX = 512
SUBSTEPS = 4
NS_ITERS = 6
ENSEMBLE_SIZE = 32
NY = 32
NX = 512
REGION_COUNT = 32
N_SPACE = 4


def draw_prior_ensemble(key, part):
    first, second = jax.random.split(jax.random.fold_in(key, 11))
    scales = jnp.exp(jax.random.uniform(first, (ENSEMBLE_SIZE, 1, 1), jnp.float32, math.log(0.3), math.log(3.0)))
    base = jnp.clip(jax.random.normal(second, (ENSEMBLE_SIZE, NY, NX), jnp.float32), -4.0, 4.0)
    return base * scales


def draw_obs_count(key, part):
    first, second, third = jax.random.split(jax.random.fold_in(key, 23), 3)
    lowest = OBS_MAX // 8
    raw = jax.random.randint(first, (REGION_COUNT,), 0, 64)
    counts = lowest + (OBS_MAX - lowest) * raw * raw // 3969
    pick = jax.random.randint(second, (), 0, REGION_COUNT)
    other = (pick + 1 + jax.random.randint(third, (), 0, REGION_COUNT - 1)) % REGION_COUNT
    counts = counts.at[pick].set(OBS_MAX)
    counts = counts.at[other].set(lowest)
    return counts.astype(jnp.int32)


def plant(values, rng, least, top_value):
    dims = values.shape
    index_at = [jax.random.randint(jax.random.fold_in(rng, axis), (), 0, dims[axis]) for axis in range(len(dims))]
    values = values.at[tuple(index_at)].set(least)
    longest = dims.index(max(dims))
    index_at[longest] = (index_at[longest] + 1) % dims[longest]
    return values.at[tuple(index_at)].set(top_value)


def levels(key, extent, pieces, low, high):
    factor_of = 1.0
    for position, parts in pieces:
        heights = jax.random.uniform(jax.random.fold_in(jax.random.fold_in(key, 6), position), (parts,), jnp.float32, low / len(pieces), high / len(pieces))
        factor_of = factor_of * jnp.repeat(jnp.exp(heights), extent[position] // parts).reshape((-1,) + (1,) * (len(extent) - 1 - position))
    return factor_of


def gaussian(own_key, shape, spread, bound, shards=(), held_as=jnp.bfloat16):
    entries = spread * jax.random.normal(own_key, shape, jnp.float32)
    if shards:
        entries = entries * levels(own_key, shape, shards, -0.22, 0.18)
    return jnp.clip(entries, -bound, bound).astype(held_as)


def setup_inputs(seed: int = 0) -> dict:
    arg_keys = jax.random.split(jax.random.key(seed), 7)
    return {
        "prior_ensemble": draw_prior_ensemble(jax.random.fold_in(arg_keys[6], 71), 0),
        "wind": jnp.clip(jax.random.uniform(arg_keys[1], (NY, NX), jnp.float32, -1.0, 1.0) * levels(arg_keys[1], (NY, NX), ((1, 4),), -0.4, 0.0), -1.0, 1.0),
        "obs_value": gaussian(arg_keys[2], (REGION_COUNT, OBS_MAX), 1.0, 6.0, ((0, 32),), jnp.float32),
        "obs_weight": jnp.clip(jnp.exp(math.log(4.0) - 2.7725887 * jax.random.uniform(arg_keys[3], (REGION_COUNT, OBS_MAX), jnp.float32) ** levels(arg_keys[3], (REGION_COUNT, OBS_MAX), ((0, 32),), -0.2, 0.2)), 0.25, 4.0),
        "observed_cell_value": plant(jax.random.randint(arg_keys[4], (REGION_COUNT, OBS_MAX), 0, REGION_HEIGHT * TILE_WIDTH), jax.random.fold_in(arg_keys[4], 1), 0, (REGION_HEIGHT * TILE_WIDTH) - 1).astype(jnp.int32),
        "obs_count": draw_obs_count(jax.random.fold_in(arg_keys[6], 71), 0),
    }


def tendency(center, east, west, wind_mid):
    pads = [(0, 0)] * (center.ndim - 2) + [(1, 1), (0, 0)]
    ypad = jnp.pad(center, pads)
    north = ypad[..., 2:, :]
    south = ypad[..., :-2, :]
    speed = wind_mid + 0.25 * jnp.tanh(center)
    return center + 0.2 * (east - 2.0 * center + west) + 0.1 * (north - 2.0 * center + south) - 0.3 * speed * (east - west)

def inverse_root(gram):
    order = gram.shape[0]
    ident = jnp.eye(order, dtype=jnp.float32)
    scale = jnp.sqrt(jnp.sum(gram * gram) + 1e-06)
    upper = gram / scale
    lower = ident
    for step in range(NS_ITERS):
        middle = 1.5 * ident - 0.5 * jnp.dot(lower, upper, precision=lax.Precision.HIGHEST)
        upper = jnp.dot(upper, middle, precision=lax.Precision.HIGHEST)
        lower = jnp.dot(middle, lower, precision=lax.Precision.HIGHEST)
    return lower / jnp.sqrt(scale)

def analyze(xb, cells, value, weight, count):
    order = xb.shape[0]
    mean = lax.optimization_barrier(jnp.sum(xb, axis=0)) / order
    pert = xb - mean
    ypert = jnp.take(pert, cells, axis=1)
    ymean = jnp.take(mean, cells)
    live = (jnp.arange(cells.shape[0], dtype=jnp.int32) < count).astype(jnp.float32)
    wts = weight * live
    gram = (order - 1.0) * jnp.eye(order, dtype=jnp.float32) + jnp.dot(ypert * wts, ypert.T, precision=lax.Precision.HIGHEST)
    rhs = jnp.dot(ypert, wts * (value - ymean), precision=lax.Precision.HIGHEST)
    root = inverse_root(gram)
    wbar = jnp.dot(root, jnp.dot(root, rhs, precision=lax.Precision.HIGHEST), precision=lax.Precision.HIGHEST)
    trans = jnp.sqrt(order - 1.0) * root + wbar[:, None]
    return mean + jnp.dot(trans.T, pert, precision=lax.Precision.HIGHEST)

def reference(prior_ensemble, wind, obs_value, obs_weight, observed_cell_value, obs_count):

    def predicted_ensemble(model_variable):
        for step in range(SUBSTEPS):
            model_variable = tendency(model_variable, jnp.roll(model_variable, -1, axis=1), jnp.roll(model_variable, 1, axis=1), wind)
        return model_variable
    predicted_vector = lax.map(predicted_ensemble, prior_ensemble)
    latitude_lines = NY // REGION_HEIGHT
    local_regions = predicted_vector.reshape(ENSEMBLE_SIZE, latitude_lines, REGION_HEIGHT, N_SPACE, TILE_WIDTH).transpose(3, 1, 0, 2, 4).reshape(REGION_COUNT, ENSEMBLE_SIZE, REGION_HEIGHT * TILE_WIDTH)
    result = lax.map(lambda items: analyze(*items), (local_regions, observed_cell_value, obs_value, obs_weight, obs_count))
    return result.reshape(N_SPACE, latitude_lines, ENSEMBLE_SIZE, REGION_HEIGHT, TILE_WIDTH).transpose(2, 1, 3, 0, 4).reshape(ENSEMBLE_SIZE, NY, NX)
```

```python
import functools

import jax
import jax.numpy as jnp
from jax import lax
from jax.experimental import pallas as pl
from jax.experimental.pallas import tpu as pltpu
from jax.sharding import PartitionSpec as P

SUBSTEPS = 4
NS_ITERS = 6
LANES = 128
STRIP = 32
GATHER_BYTES = 4 << 20


def padded(block, sides, width):
    for axis, dim in sides:
        count = lax.axis_size(axis)
        forward = [(i, i + 1) for i in range(count - 1)]
        forward.append((count - 1, 0))
        backward = [(target, source) for source, target in forward]
        low = lax.ppermute(
            lax.slice_in_dim(block, block.shape[dim] - width, None, axis=dim), axis, forward
        )
        high = lax.ppermute(lax.slice_in_dim(block, 0, width, axis=dim), axis, backward)
        block = jnp.concatenate([low, block, high], axis=dim)
    return block


def tendency(center, east, west, wind_mid):
    pads = [(0, 0)] * (center.ndim - 2) + [(1, 1), (0, 0)]
    ypad = jnp.pad(center, pads)
    north = ypad[..., 2:, :]
    south = ypad[..., :-2, :]
    speed = wind_mid + 0.25 * jnp.tanh(center)
    return (
        center
        + 0.2 * (east - 2.0 * center + west)
        + 0.1 * (north - 2.0 * center + south)
        - 0.3 * speed * (east - west)
    )


def inverse_root(gram):
    order = gram.shape[0]
    ident = jnp.eye(order, dtype=jnp.float32)
    scale = jnp.sqrt(jnp.sum(gram * gram) + 1e-06)
    upper = gram / scale
    lower = ident
    for step in range(NS_ITERS):
        middle = 1.5 * ident - 0.5 * jnp.dot(lower, upper, precision=lax.Precision.HIGHEST)
        upper = jnp.dot(upper, middle, precision=lax.Precision.HIGHEST)
        lower = jnp.dot(middle, lower, precision=lax.Precision.HIGHEST)
    return lower / jnp.sqrt(scale)


def analyze(xb, cells, value, weight, count):
    order = xb.shape[0]
    slots = cells.shape[0]
    mean = jnp.sum(xb, axis=0) / order
    pert = xb - mean
    start_gram = (order - 1.0) * jnp.eye(order, dtype=jnp.float32)
    ypert = jnp.take(pert, cells, axis=1)
    ymean = jnp.take(mean, cells)
    live = (jnp.arange(slots, dtype=jnp.int32) < count).astype(jnp.float32)
    wts = weight * live
    gram = start_gram + jnp.dot(ypert * wts, ypert.T, precision=lax.Precision.HIGHEST)
    rhs = jnp.dot(ypert, wts * (value - ymean), precision=lax.Precision.HIGHEST)
    root = inverse_root(gram)
    wbar = jnp.dot(
        root, jnp.dot(root, rhs, precision=lax.Precision.HIGHEST), precision=lax.Precision.HIGHEST
    )
    trans = jnp.sqrt(order - 1.0) * root + wbar[:, None]
    return mean + jnp.dot(trans.T, pert, precision=lax.Precision.HIGHEST)


def exchanged(prior_ensemble, wind, obs_value, obs_weight, observed_cell_value, obs_count):
    stacked = jnp.concatenate([prior_ensemble, wind[None]], axis=0)
    extended = padded(stacked, (("space", 2),), SUBSTEPS)
    state = extended[:-1]
    wind_ext = extended[-1]
    for step in range(SUBSTEPS):
        edge = step + 1
        wind_mid = wind_ext[:, edge : wind_ext.shape[1] - edge]
        state = tendency(state[..., 1:-1], state[..., 2:], state[..., :-2], wind_mid)
    mem_here, latitude_lines, column_entries = state.shape
    groups = lax.axis_size("member")
    per_dev = obs_count.shape[0]
    cell_count = latitude_lines * column_entries // (groups * per_dev)
    blocks = state.reshape(mem_here, groups, per_dev, cell_count)
    arrived = lax.all_to_all(blocks, "member", split_axis=1, concat_axis=0, tiled=True)
    output_results = [
        analyze(arrived[:, 0, i], observed_cell_value[i], obs_value[i], obs_weight[i], obs_count[i])
        for i in range(per_dev)
    ]
    analysed_state = jnp.stack(output_results, axis=1)[:, None]
    returned = lax.all_to_all(analysed_state, "member", split_axis=0, concat_axis=1, tiled=True)
    return returned.reshape(mem_here, latitude_lines, column_entries)


def strips_kernel(u_ref, q_ref):
    rows = u_ref.shape[1]
    lane = lax.broadcasted_iota(jnp.int32, (rows, LANES), 1)
    west = (lane % STRIP) < STRIP // 2
    total = [jnp.zeros((rows, LANES), jnp.float32)] * 2
    for m in range(u_ref.shape[0] - 1):
        mine = (lane // STRIP) == m
        for k, x in enumerate((u_ref[m], u_ref[u_ref.shape[0] - 1])):
            low = pltpu.roll(x, (STRIP * m + SUBSTEPS) % LANES, 1)
            high = pltpu.roll(x, (STRIP * m + STRIP - SUBSTEPS) % LANES, 1)
            total[k] = jnp.where(mine, jnp.where(west, low, high), total[k])
    q_ref[0:rows, :] = total[0]
    q_ref[rows : 2 * rows, :] = total[1]


def substep(x, wind3):
    rows = x.shape[0]
    row = lax.broadcasted_iota(jnp.int32, x.shape, 0)
    east = pltpu.roll(x, LANES - 1, 1)
    west = pltpu.roll(x, 1, 1)
    north = jnp.where(row == rows - 1, 0.0, pltpu.roll(x, rows - 1, 0))
    south = jnp.where(row == 0, 0.0, pltpu.roll(x, 1, 0))
    speed = wind3 + 0.075 * jnp.tanh(x)
    return 0.4 * x + 0.2 * (east + west) + 0.1 * (north + south) - speed * (east - west)


def pieces(x, count):
    out = []
    for _ in range(count):
        part = x.astype(jnp.bfloat16)
        out.append(part)
        x = x - part.astype(jnp.float32)
    return out


def interior_kernel(count_ref, u_ref, cell_ref, value_ref, weight_ref, f_ref):
    mem_here, rows = u_ref.shape[0] - 1, u_ref.shape[1]
    stride = f_ref.shape[0] // mem_here
    extra = stride - rows
    wind3 = 0.3 * u_ref[mem_here]
    slots = cell_ref.shape[1]
    slot = lax.broadcasted_iota(jnp.int32, (1, slots), 1)
    weight = jnp.where(slot < count_ref[0], weight_ref[...], 0.0)
    parts = pieces(weight, 3) + pieces(weight * value_ref[...], 3)
    sub = lax.broadcasted_iota(jnp.int32, (8, slots), 0)
    lhs = jnp.zeros((8, slots), jnp.float32)
    for k, part in enumerate(parts):
        lhs = jnp.where(sub == k, part.astype(jnp.float32), lhs)
    lhs = lhs.astype(jnp.bfloat16)
    patch_rows = extra * mem_here // 2
    for q in range(patch_rows):
        cell = lax.broadcasted_iota(jnp.int32, (LANES, slots), 0) + LANES * q
        hot = jnp.where(cell == cell_ref[...], 1.0, 0.0).astype(jnp.bfloat16)
        sums = lax.dot_general(
            lhs, hot, (((1,), (1,)), ((), ())), preferred_element_type=jnp.float32
        )
        for which in range(2):
            k = which * patch_rows + q
            line = sums[3 * which : 3 * which + 1] + sums[3 * which + 1 : 3 * which + 2]
            line = line + sums[3 * which + 2 : 3 * which + 3]
            at = (k // extra) * stride + rows + k % extra
            f_ref[at : at + 1, :] = line
    for m in range(mem_here):
        x = u_ref[m]
        for _ in range(SUBSTEPS):
            x = substep(x, wind3)
        f_ref[m * stride : m * stride + rows, :] = x


def edges_kernel(q_ref, east_ref, west_ref, f_in_ref, f_ref):
    rows = q_ref.shape[0] // 2
    lane = lax.broadcasted_iota(jnp.int32, (rows, LANES), 1)
    place = lane % STRIP
    full = []
    for k in range(2):
        at = slice(k * rows, (k + 1) * rows)
        west, east, own = west_ref[at, :], east_ref[at, :], q_ref[at, :]
        full.append(
            jnp.where(place < SUBSTEPS, west, jnp.where(place >= STRIP - SUBSTEPS, east, own))
        )
    x, wind3 = full[0], 0.3 * full[1]
    for _ in range(SUBSTEPS):
        x = substep(x, wind3)
    mem_here = LANES // STRIP
    stride = f_ref.shape[0] // mem_here
    for m in range(mem_here):
        low = pltpu.roll(x, (-STRIP * m - SUBSTEPS) % LANES, 1)
        high = pltpu.roll(x, (-STRIP * m - STRIP + SUBSTEPS) % LANES, 1)
        at = slice(m * stride, m * stride + rows)
        inside = f_in_ref[at, :]
        f_ref[at, :] = jnp.where(
            lane < SUBSTEPS, low, jnp.where(lane >= LANES - SUBSTEPS, high, inside)
        )
        at = slice(m * stride + rows, (m + 1) * stride)
        f_ref[at, :] = f_in_ref[at, :]


def analysis_kernel(dims, me_ref, cat_ref, sib_ref, o_ref, ob_ref, pert_ref, scaled_ref, mean_ref):
    mem_here, rows, groups = dims
    f32, bf16 = jnp.float32, jnp.bfloat16
    order = mem_here * groups
    height = rows // groups
    cells = height * LANES
    wide = order * groups
    stride = cat_ref.shape[0] * 2 // order
    extra = stride - rows
    me = me_ref[0]

    for side, ref in enumerate((cat_ref, sib_ref)):
        for k in range(groups // 2):
            patch = me ^ (2 * k + side)
            base = k * mem_here * stride
            lines = [
                ref[base + m * stride + rows : base + (m + 1) * stride, :] for m in range(mem_here)
            ]
            ob_ref[pl.ds(pl.multiple_of(patch * 2 * height, 2 * height), 2 * height), :] = (
                jnp.concatenate(lines, axis=0)
            )

    for p in range(groups):
        sums = ob_ref[p * 2 * height : (p + 1) * 2 * height, :]
        for q in range(height):
            at = pl.ds(p * height + q, order // 2, stride=stride)
            xb = jnp.concatenate([cat_ref[at, :], sib_ref[at, :]], axis=0)
            mean = jnp.sum(xb, axis=0, keepdims=True) * (1.0 / order)
            pert = xb - mean
            lanes = slice(q * LANES, (q + 1) * LANES)
            weight = sums[q : q + 1, :]
            pert_ref[p * order : (p + 1) * order, lanes] = pert
            scaled_ref[p * order : (p + 1) * order, lanes] = pert * weight
            scaled_ref[wide + p : wide + p + 1, lanes] = (
                sums[height + q : height + q + 1, :] - weight * mean
            )
            mean_ref[p : p + 1, lanes] = mean
    pad = scaled_ref.shape[0] - wide - groups
    if pad:
        scaled_ref[wide + groups :, :] = jnp.zeros((pad, cells), f32)

    def split(x):
        high = x.astype(bf16)
        return high, (x - high.astype(f32)).astype(bf16)

    def product(x, high, low, dims):
        n = x.shape[0]
        xh, xl = split(x)
        dot = functools.partial(
            lax.dot_general, dimension_numbers=(dims, ((), ())), preferred_element_type=f32
        )
        both = dot(jnp.concatenate([xh, xl], axis=0), high)
        return both[:n] + both[n:] + dot(xh, low)

    plain, turned = ((1,), (0,)), ((1,), (1,))

    pert_high, pert_low = split(pert_ref[...])
    full = product(scaled_ref[...], pert_high, pert_low, turned)
    own_row = lax.broadcasted_iota(jnp.int32, (order, wide), 0)
    lane = lax.broadcasted_iota(jnp.int32, (order, wide), 1)
    gram = jnp.where(own_row == lane % order, order - 1.0, 0.0)
    ident = jnp.where(own_row == lane % order, 1.0, 0.0)
    block = lane // order
    total = jnp.zeros((order, wide), f32)
    for p in range(groups):
        total = jnp.where(block == p, full[p * order : (p + 1) * order], total)
    gram = gram + total
    tail = full[wide : wide + 16]
    tail_row = lax.broadcasted_iota(jnp.int32, (16, wide), 0)
    tail_block = lax.broadcasted_iota(jnp.int32, (16, wide), 1) // order
    rhs = jnp.sum(jnp.where(tail_row == tail_block, tail, 0.0), axis=0, keepdims=True)
    first = tail_row == 0

    diag = (
        lax.broadcasted_iota(jnp.int32, (wide, wide), 0) // order
        == lax.broadcasted_iota(jnp.int32, (wide, wide), 1) // order
    )

    def blocks(x):
        return [
            jnp.where(diag, jnp.concatenate([part.astype(f32)] * groups, axis=0), 0.0).astype(bf16)
            for part in split(x)
        ]

    ones = jnp.where(diag, 1.0, 0.0).astype(bf16)
    square = jnp.sum(gram * gram, axis=0, keepdims=True)
    parts = pieces(jnp.where(first, square, 0.0), 3)
    square = sum(
        lax.dot_general(part, ones, (plain, ((), ())), preferred_element_type=f32)[0:1]
        for part in parts
    )
    scale = jnp.sqrt(square + 1e-06)
    inverse = 1.0 / scale

    prod = gram * inverse
    middle = 1.5 * ident - 0.5 * prod
    lower = middle
    vec = jnp.where(first, rhs, 0.0)
    for step in range(NS_ITERS):
        high, low = blocks(middle)
        last = step == NS_ITERS - 1
        if step == 0:
            out = product(jnp.concatenate([prod, vec], axis=0), high, low, plain)
            half, vec = out[:order], out[order:]
        elif not last:
            out = product(jnp.concatenate([prod, lower, vec], axis=0), high, low, plain)
            half, lower, vec = out[:order], out[order : 2 * order], out[2 * order :]
        else:
            out = product(jnp.concatenate([lower, vec], axis=0), high, low, plain)
            lower, vec = out[:order], out[order:]
        if not last:
            prod = product(half, high, low, plain)
            middle = 1.5 * ident - 0.5 * prod
    high, low = blocks(lower)
    wbar = product(vec, high, low, plain)[0:1] * inverse
    eight = lower[0:8] * (jnp.sqrt(inverse) * (order - 1.0) ** 0.5) + wbar

    tall = jnp.concatenate([eight] * groups, axis=0)
    tall_row = lax.broadcasted_iota(jnp.int32, tall.shape, 0) // 8
    tall_block = lax.broadcasted_iota(jnp.int32, tall.shape, 1) // order
    out = product(jnp.where(tall_row == tall_block, tall, 0.0), pert_high, pert_low, plain)
    for p in range(groups):
        for q in range(height):
            lanes = slice(q * LANES, (q + 1) * LANES)
            o_ref[pl.ds(p * height + q, mem_here, stride=rows), :] = (
                out[8 * p : 8 * p + mem_here, lanes] + mean_ref[p : p + 1, lanes]
            )


def kernel_call(body, out_shape, scratch=(), smem=()):
    def call(*args):
        specs = [
            pl.BlockSpec(memory_space=pltpu.SMEM if i in smem else pltpu.VMEM)
            for i in range(len(args))
        ]
        return pl.pallas_call(
            body,
            out_shape=jax.ShapeDtypeStruct(out_shape, jnp.float32),
            in_specs=specs,
            out_specs=pl.BlockSpec(memory_space=pltpu.VMEM),
            scratch_shapes=list(scratch),
            compiler_params=pltpu.CompilerParams(vmem_limit_bytes=32 << 20),
        )(*args)

    return call


def gathered(prior_ensemble, wind, obs_value, obs_weight, observed_cell_value, obs_count):
    mem_here, rows, _ = prior_ensemble.shape
    groups = lax.axis_size("member")
    count = lax.axis_size("space")
    order = mem_here * groups
    height = rows // groups
    extra = 2 * height // mem_here
    stride = rows + extra
    f32, bf16 = jnp.float32, jnp.bfloat16

    both = jnp.concatenate([prior_ensemble, wind[None]], axis=0)
    strips = kernel_call(strips_kernel, (2 * rows, LANES))(both)
    forward = [(i, (i + 1) % count) for i in range(count)]
    backward = [(i, (i - 1) % count) for i in range(count)]
    east = lax.ppermute(strips, "space", backward)
    west = lax.ppermute(strips, "space", forward)
    inside = kernel_call(interior_kernel, (mem_here * stride, LANES), smem=(0,))(
        obs_count, both, observed_cell_value, obs_value, obs_weight
    )
    payload = kernel_call(edges_kernel, (mem_here * stride, LANES))(strips, east, west, inside)

    def swap(x, k):
        return lax.ppermute(x, "member", [(i, i ^ k) for i in range(groups)])

    chips = range(2, groups, 2)
    others = [swap(payload, k) for k in reversed(chips)][::-1]
    cat = jnp.concatenate([payload, *others], axis=0)
    sibling = swap(cat, 1)
    me = lax.axis_index("member").astype(jnp.int32).reshape(1)
    wide = order * groups
    cells = height * LANES
    out = kernel_call(
        functools.partial(analysis_kernel, (mem_here, rows, groups)),
        (mem_here * rows, LANES),
        scratch=[
            pltpu.VMEM((groups * 2 * height, LANES), f32),
            pltpu.VMEM((wide, cells), f32),
            pltpu.VMEM((wide + 16, cells), f32),
            pltpu.VMEM((max(groups, 8), cells), f32),
        ],
        smem=(0,),
    )(me, cat, sibling)
    return out.reshape(mem_here, rows, LANES)


def local(prior_ensemble, *rest):
    mem_here, rows, columns = prior_ensemble.shape
    groups = lax.axis_size("member")
    whole_tile = 4 * mem_here * groups * rows * columns
    fits = (
        columns == LANES
        and mem_here * STRIP == LANES
        and rows % groups == 0
        and 2 * (rows // groups) % mem_here == 0
        and rows % 8 == 0
        and groups & (groups - 1) == 0
        and 2 <= groups <= 16
        and lax.axis_size("space") % 2 == 0
        and rest[-1].shape[0] == 1
        and whole_tile <= GATHER_BYTES
    )
    return (gathered if fits else exchanged)(prior_ensemble, *rest)


def solution(mesh):
    in_specs = (
        P("member", None, "space"),
        P(None, "space"),
        P(("space", "member"), None),
        P(("space", "member"), None),
        P(("space", "member"), None),
        P(("space", "member")),
    )
    out_specs = P("member", None, "space")
    return jax.shard_map(local, mesh=mesh, in_specs=in_specs, out_specs=out_specs, check_vma=False)
```

```python
import functools

import jax
import jax.numpy as jnp
from jax import lax
from jax.experimental import pallas as pl
from jax.experimental.pallas import tpu as pltpu
from jax.sharding import PartitionSpec as P

SUBSTEPS = 4
NS_ITERS = 6
LANES = 128
STRIP = 32
GATHER_BYTES = 4 << 20


def padded(block, sides, width):
    for axis, dim in sides:
        count = lax.axis_size(axis)
        forward = [(i, i + 1) for i in range(count - 1)]
        forward.append((count - 1, 0))
        backward = [(target, source) for source, target in forward]
        low = lax.ppermute(
            lax.slice_in_dim(block, block.shape[dim] - width, None, axis=dim), axis, forward
        )
        high = lax.ppermute(lax.slice_in_dim(block, 0, width, axis=dim), axis, backward)
        block = jnp.concatenate([low, block, high], axis=dim)
    return block


def tendency(center, east, west, wind_mid):
    pads = [(0, 0)] * (center.ndim - 2) + [(1, 1), (0, 0)]
    ypad = jnp.pad(center, pads)
    north = ypad[..., 2:, :]
    south = ypad[..., :-2, :]
    speed = wind_mid + 0.25 * jnp.tanh(center)
    return (
        center
        + 0.2 * (east - 2.0 * center + west)
        + 0.1 * (north - 2.0 * center + south)
        - 0.3 * speed * (east - west)
    )


def inverse_root(gram):
    order = gram.shape[0]
    ident = jnp.eye(order, dtype=jnp.float32)
    scale = jnp.sqrt(jnp.sum(gram * gram) + 1e-06)
    upper = gram / scale
    lower = ident
    for step in range(NS_ITERS):
        middle = 1.5 * ident - 0.5 * jnp.dot(lower, upper, precision=lax.Precision.HIGHEST)
        upper = jnp.dot(upper, middle, precision=lax.Precision.HIGHEST)
        lower = jnp.dot(middle, lower, precision=lax.Precision.HIGHEST)
    return lower / jnp.sqrt(scale)


def analyze(xb, cells, value, weight, count):
    order = xb.shape[0]
    slots = cells.shape[0]
    mean = jnp.sum(xb, axis=0) / order
    pert = xb - mean
    start_gram = (order - 1.0) * jnp.eye(order, dtype=jnp.float32)
    ypert = jnp.take(pert, cells, axis=1)
    ymean = jnp.take(mean, cells)
    live = (jnp.arange(slots, dtype=jnp.int32) < count).astype(jnp.float32)
    wts = weight * live
    gram = start_gram + jnp.dot(ypert * wts, ypert.T, precision=lax.Precision.HIGHEST)
    rhs = jnp.dot(ypert, wts * (value - ymean), precision=lax.Precision.HIGHEST)
    root = inverse_root(gram)
    wbar = jnp.dot(
        root, jnp.dot(root, rhs, precision=lax.Precision.HIGHEST), precision=lax.Precision.HIGHEST
    )
    trans = jnp.sqrt(order - 1.0) * root + wbar[:, None]
    return mean + jnp.dot(trans.T, pert, precision=lax.Precision.HIGHEST)


def exchanged(prior_ensemble, wind, obs_value, obs_weight, observed_cell_value, obs_count):
    stacked = jnp.concatenate([prior_ensemble, wind[None]], axis=0)
    extended = padded(stacked, (("space", 2),), SUBSTEPS)
    state = extended[:-1]
    wind_ext = extended[-1]
    for step in range(SUBSTEPS):
        edge = step + 1
        wind_mid = wind_ext[:, edge : wind_ext.shape[1] - edge]
        state = tendency(state[..., 1:-1], state[..., 2:], state[..., :-2], wind_mid)
    mem_here, latitude_lines, column_entries = state.shape
    groups = lax.axis_size("member")
    per_dev = obs_count.shape[0]
    cell_count = latitude_lines * column_entries // (groups * per_dev)
    blocks = state.reshape(mem_here, groups, per_dev, cell_count)
    arrived = lax.all_to_all(blocks, "member", split_axis=1, concat_axis=0, tiled=True)
    output_results = [
        analyze(arrived[:, 0, i], observed_cell_value[i], obs_value[i], obs_weight[i], obs_count[i])
        for i in range(per_dev)
    ]
    analysed_state = jnp.stack(output_results, axis=1)[:, None]
    returned = lax.all_to_all(analysed_state, "member", split_axis=0, concat_axis=1, tiled=True)
    return returned.reshape(mem_here, latitude_lines, column_entries)


def lane_of(shape):
    return lax.broadcasted_iota(jnp.int32, shape, 1)


def edge_kernel(start, wind_start, u_ref, z_ref):
    members, rows, _ = u_ref.shape
    members = members - 1
    lane = lane_of((rows, LANES))
    place = lane % STRIP
    column = 0 if start > STRIP // 2 else LANES - SUBSTEPS
    total = jnp.zeros((rows, LANES), jnp.float32)
    for m in range(members):
        for x, to in ((u_ref[m], start), (u_ref[members], wind_start)):
            moved = pltpu.roll(x, (STRIP * m + to - column) % LANES, 1)
            keep = (lane // STRIP == m) & (place >= to) & (place < to + SUBSTEPS)
            total = jnp.where(keep, moved, total)
    z_ref[...] = total


def strips(block):
    lane = lane_of(block[0].shape)
    west = (lane % STRIP) < STRIP // 2
    total = jnp.zeros(block[0].shape, jnp.float32)
    for m, x in enumerate(block):
        low = pltpu.roll(x, (STRIP * m + SUBSTEPS) % LANES, 1)
        high = pltpu.roll(x, (STRIP * m + STRIP - SUBSTEPS) % LANES, 1)
        total = jnp.where((lane // STRIP) == m, jnp.where(west, low, high), total)
    return total


def substep(x, wind3):
    rows = x.shape[0]
    row = lax.broadcasted_iota(jnp.int32, x.shape, 0)
    east = pltpu.roll(x, LANES - 1, 1)
    west = pltpu.roll(x, 1, 1)
    north = jnp.where(row == rows - 1, 0.0, pltpu.roll(x, rows - 1, 0))
    south = jnp.where(row == 0, 0.0, pltpu.roll(x, 1, 0))
    speed = wind3 + 0.075 * jnp.tanh(x)
    return 0.4 * x + 0.2 * (east + west) + 0.1 * (north + south) - speed * (east - west)


def pieces(x, count):
    out = []
    for _ in range(count):
        part = x.astype(jnp.bfloat16)
        out.append(part)
        x = x - part.astype(jnp.float32)
    return out


def interior_kernel(count_ref, u_ref, cell_ref, value_ref, weight_ref, f_ref, q_ref):
    mem_here, rows = u_ref.shape[0] - 1, u_ref.shape[1]
    stride = f_ref.shape[0] // mem_here
    extra = stride - rows
    wind3 = 0.3 * u_ref[mem_here]
    slots = cell_ref.shape[1]
    slot = lax.broadcasted_iota(jnp.int32, (1, slots), 1)
    weight = jnp.where(slot < count_ref[...], weight_ref[...], 0.0)
    parts = pieces(weight, 3) + pieces(weight * value_ref[...], 3)
    sub = lax.broadcasted_iota(jnp.int32, (8, slots), 0)
    lhs = jnp.zeros((8, slots), jnp.float32)
    for k, part in enumerate(parts):
        lhs = jnp.where(sub == k, part.astype(jnp.float32), lhs)
    lhs = lhs.astype(jnp.bfloat16)
    patch_rows = extra * mem_here // 2
    for q in range(patch_rows):
        cell = lax.broadcasted_iota(jnp.int32, (LANES, slots), 0) + LANES * q
        hot = jnp.where(cell == cell_ref[...], 1.0, 0.0).astype(jnp.bfloat16)
        sums = lax.dot_general(
            lhs, hot, (((1,), (1,)), ((), ())), preferred_element_type=jnp.float32
        )
        for which in range(2):
            k = which * patch_rows + q
            line = sums[3 * which : 3 * which + 1] + sums[3 * which + 1 : 3 * which + 2]
            line = line + sums[3 * which + 2 : 3 * which + 3]
            at = (k // extra) * stride + rows + k % extra
            f_ref[at : at + 1, :] = line
    q_ref[0:rows, :] = strips([u_ref[m] for m in range(mem_here)])
    q_ref[rows : 2 * rows, :] = strips([u_ref[mem_here]] * mem_here)
    for m in range(mem_here):
        x = u_ref[m]
        for _ in range(SUBSTEPS):
            x = substep(x, wind3)
        f_ref[m * stride : m * stride + rows, :] = x


def edges_kernel(q_ref, west_ref, east_ref, f_in_ref, f_ref):
    rows = q_ref.shape[0] // 2
    lane = lane_of((rows, LANES))
    place = lane % STRIP
    west, east = west_ref[...], east_ref[...]
    full = []
    for k in range(2):
        own = q_ref[k * rows : (k + 1) * rows, :]
        full.append(
            jnp.where(place < SUBSTEPS, west, jnp.where(place >= STRIP - SUBSTEPS, east, own))
        )
        west = pltpu.roll(west, LANES - SUBSTEPS, 1)
        east = pltpu.roll(east, SUBSTEPS, 1)
    x, wind3 = full[0], 0.3 * full[1]
    for _ in range(SUBSTEPS):
        x = substep(x, wind3)
    mem_here = LANES // STRIP
    stride = f_ref.shape[0] // mem_here
    for m in range(mem_here):
        low = pltpu.roll(x, (-STRIP * m - SUBSTEPS) % LANES, 1)
        high = pltpu.roll(x, (-STRIP * m - STRIP + SUBSTEPS) % LANES, 1)
        at = slice(m * stride, m * stride + rows)
        inside = f_in_ref[at, :]
        f_ref[at, :] = jnp.where(
            lane < SUBSTEPS, low, jnp.where(lane >= LANES - SUBSTEPS, high, inside)
        )
        at = slice(m * stride + rows, (m + 1) * stride)
        f_ref[at, :] = f_in_ref[at, :]


def analysis_kernel(dims, me_ref, cat_ref, sib_ref, o_ref, ob_ref, pert_ref, scaled_ref, mean_ref):
    mem_here, rows, groups = dims
    f32, bf16 = jnp.float32, jnp.bfloat16
    order = mem_here * groups
    height = rows // groups
    cells = height * LANES
    wide = order * groups
    stride = cat_ref.shape[0] * 2 // order
    per = LANES // order
    sets = range(groups // per)
    plain, turned = (((1,), (0,)), ((), ())), (((1,), (1,)), ((), ()))
    me = me_ref[0]

    def dot(x, y, how):
        return lax.dot_general(x, y, how, preferred_element_type=f32)

    def split(x):
        high = x.astype(bf16)
        return high, (x - high.astype(f32)).astype(bf16)

    for side, ref in enumerate((cat_ref, sib_ref)):
        for k in range(groups // 2):
            patch = me ^ (2 * k + side)
            base = k * mem_here * stride
            lines = [
                ref[base + m * stride + rows : base + (m + 1) * stride, :] for m in range(mem_here)
            ]
            ob_ref[pl.ds(pl.multiple_of(patch * 2 * height, 2 * height), 2 * height), :] = (
                jnp.concatenate(lines, axis=0)
            )

    for p in range(groups):
        for q in range(height):
            at = pl.ds(p * height + q, order // 2, stride=stride)
            xb = jnp.concatenate([cat_ref[at, :], sib_ref[at, :]], axis=0)
            mean = jnp.sum(xb, axis=0, keepdims=True) * (1.0 / order)
            pert = xb - mean
            lanes = slice(q * LANES, (q + 1) * LANES)
            line = p * 2 * height + q
            pert_ref[p * order : (p + 1) * order, lanes] = pert
            scaled_ref[p * order : (p + 1) * order, lanes] = pert * ob_ref[line : line + 1, :]
            mean_ref[p : p + 1, lanes] = mean
    lift = []
    for q in range(height):
        weight = ob_ref[pl.ds(q, groups, stride=2 * height), :]
        lift.append(
            ob_ref[pl.ds(height + q, groups, stride=2 * height), :]
            - weight * mean_ref[:, q * LANES : (q + 1) * LANES]
        )
    lift = jnp.concatenate(lift, axis=1)
    lift = jnp.concatenate([lift] * (16 // groups), axis=0)
    lift_high, lift_low = split(lift)

    pert_high, pert_low = split(pert_ref[...])
    scaled_high, scaled_low = split(scaled_ref[...])
    own_row = lax.broadcasted_iota(jnp.int32, (order, LANES), 0)
    lane = lax.broadcasted_iota(jnp.int32, (order, LANES), 1)
    ident = jnp.where(own_row == lane % order, 1.0, 0.0)
    tail_row = lax.broadcasted_iota(jnp.int32, (16, LANES), 0)
    tail_block = lax.broadcasted_iota(jnp.int32, (16, LANES), 1) // order
    square_row = lax.broadcasted_iota(jnp.int32, (LANES, LANES), 0) // order
    square_lane = lax.broadcasted_iota(jnp.int32, (LANES, LANES), 1) // order
    diag = jnp.where(square_row == square_lane, 1.0, 0.0).astype(bf16)
    grams, prod, middle, lower, vec, inverse = [], [], [], [], [], []
    for t in sets:
        at = slice(t * LANES, (t + 1) * LANES)
        left_high = jnp.concatenate([scaled_high[at], lift_high], axis=0)
        left_low = jnp.concatenate([scaled_low[at], lift_low], axis=0)
        right = jnp.concatenate([pert_high[at], pert_low[at]], axis=0)
        out = dot(left_high, right, turned)
        full = out[:, :LANES] + out[:, LANES:] + dot(left_low, pert_high[at], turned)
        gram = (order - 1.0) * ident
        for p in range(per):
            gram = gram + jnp.where(lane // order == p, full[p * order : (p + 1) * order], 0.0)
        rhs = jnp.sum(
            jnp.where(tail_row == tail_block + per * t, full[LANES:], 0.0), axis=0, keepdims=True
        )
        grams.append(gram)
        vec.append(jnp.where(tail_row == 0, rhs, 0.0))

    def weights(x):
        high, low = (jnp.concatenate([part] * per, axis=0) * diag for part in split(x))
        top = jnp.concatenate([high, low], axis=1)
        return jnp.concatenate([top, jnp.concatenate([high, jnp.zeros_like(high)], axis=1)], axis=0)

    def product(x, right):
        out = dot(jnp.concatenate(split(x), axis=1), right, plain)
        return out[:, :LANES] + out[:, LANES:]

    twice = []
    for t in sets:
        twice.append(product(jnp.concatenate([grams[t], vec[t]], axis=0), weights(grams[t])))
    for t in sets:
        square = jnp.sum(grams[t] * grams[t], axis=0, keepdims=True)
        group = lane[0:1] // order
        total = jnp.zeros((1, LANES), f32)
        for p in range(per):
            mine = group == p
            total = jnp.where(mine, jnp.sum(jnp.where(mine, square, 0.0), axis=1, keepdims=True), total)
        square = total
        inverse.append(1.0 / jnp.sqrt(square + 1e-06))
        first = grams[t] * inverse[t]
        middle.append(1.5 * ident - 0.5 * first)
        lower.append(middle[t])
        prod.append(1.5 * first - (0.5 * inverse[t]) * (twice[t][:order] * inverse[t]))
        vec[t] = 1.5 * vec[t] - (0.5 * inverse[t]) * twice[t][order:]
    for step in range(NS_ITERS):
        last = step == NS_ITERS - 1
        right = [weights(middle[t]) for t in sets]
        if step:
            for t in sets:
                left = ([] if last else [prod[t]]) + [lower[t], vec[t]]
                out = product(jnp.concatenate(left, axis=0), right[t])
                if not last:
                    prod[t], out = out[:order], out[order:]
                lower[t], vec[t] = out[:order], out[order:]
        if not last:
            for t in sets:
                prod[t] = product(prod[t], right[t])
                middle[t] = 1.5 * ident - 0.5 * prod[t]
    pick = lax.broadcasted_iota(jnp.int32, (groups, LANES), 0)
    tall = []
    for t in sets:
        wbar = product(vec[t], weights(lower[t]))[0:1] * inverse[t]
        own = lower[t][0:mem_here] * (jnp.sqrt(inverse[t]) * (order - 1.0) ** 0.5) + wbar
        keep = pick == lax.broadcasted_iota(jnp.int32, (groups, LANES), 1) // order + per * t
        tall.append(
            jnp.concatenate(
                [jnp.where(keep, own[i : i + 1], 0.0) for i in range(mem_here)], axis=0
            )
        )

    tall_high, tall_low = split(jnp.concatenate(tall, axis=1))
    both = dot(jnp.concatenate([tall_high, tall_low], axis=0), pert_high, plain)
    count = groups * mem_here
    out = both[:count] + both[count:] + dot(tall_high, pert_low, plain)
    for i in range(mem_here):
        for q in range(height):
            lanes = slice(q * LANES, (q + 1) * LANES)
            o_ref[pl.ds(i * rows + q, groups, stride=height), :] = (
                out[i * groups : (i + 1) * groups, lanes] + mean_ref[:, lanes]
            )


def kernel_call(body, *out_shapes, scratch=(), smem=(), work=None):
    def call(*args):
        specs = [
            pl.BlockSpec(memory_space=pltpu.SMEM if i in smem else pltpu.VMEM)
            for i in range(len(args))
        ]
        out = pl.pallas_call(
            body,
            out_shape=[jax.ShapeDtypeStruct(shape, jnp.float32) for shape in out_shapes],
            in_specs=specs,
            out_specs=[pl.BlockSpec(memory_space=pltpu.VMEM) for _ in out_shapes],
            scratch_shapes=list(scratch),
            compiler_params=pltpu.CompilerParams(vmem_limit_bytes=32 << 20),
            cost_estimate=work
            and pl.CostEstimate(flops=work, bytes_accessed=work, transcendentals=0),
        )(*args)
        return out[0] if len(out_shapes) == 1 else out

    return call


def gathered(prior_ensemble, wind, obs_value, obs_weight, observed_cell_value, obs_count):
    mem_here, rows, _ = prior_ensemble.shape
    groups = lax.axis_size("member")
    count = lax.axis_size("space")
    order = mem_here * groups
    height = rows // groups
    stride = rows + 2 * height // mem_here
    wide, cells = order * groups, height * LANES
    f32 = jnp.float32

    both = jnp.concatenate([prior_ensemble, wind[None]], axis=0)
    forward = [(i, (i + 1) % count) for i in range(count)]
    backward = [(i, (i - 1) % count) for i in range(count)]
    eastern = kernel_call(functools.partial(edge_kernel, 0, SUBSTEPS), (rows, LANES))(both)
    western = kernel_call(
        functools.partial(edge_kernel, STRIP - SUBSTEPS, STRIP - 2 * SUBSTEPS), (rows, LANES), work=None
    )(both)
    east = lax.ppermute(western, "space", backward)
    west = lax.ppermute(eastern, "space", forward)
    inside, near = kernel_call(interior_kernel, (mem_here * stride, LANES), (2 * rows, LANES))(
        obs_count.reshape(1, 1), both, observed_cell_value, obs_value, obs_weight
    )
    payload = kernel_call(edges_kernel, (mem_here * stride, LANES))(near, west, east, inside)

    def swap(x, k):
        return lax.ppermute(x, "member", [(i, i ^ k) for i in range(groups)])

    others = [swap(payload, k) for k in range(2, groups, 2)]
    cat = jnp.concatenate([payload, *others], axis=0)
    first = swap(jnp.concatenate([payload, others[-1]], axis=0), 1)
    size = payload.shape[0]
    sibling = jnp.concatenate(
        [first[:size], *[swap(x, 1) for x in others[:-1]], first[size:]], axis=0
    )
    me = lax.axis_index("member").astype(jnp.int32).reshape(1)
    out = kernel_call(
        functools.partial(analysis_kernel, (mem_here, rows, groups)),
        (mem_here * rows, LANES),
        scratch=[
            pltpu.VMEM((groups * 2 * height, LANES), f32),
            pltpu.VMEM((wide, cells), f32),
            pltpu.VMEM((wide, cells), f32),
            pltpu.VMEM((groups, cells), f32),
        ],
        smem=(0,),
    )(me, cat, sibling)
    return out.reshape(mem_here, rows, LANES)


def local(prior_ensemble, *rest):
    mem_here, rows, columns = prior_ensemble.shape
    groups = lax.axis_size("member")
    whole_tile = 4 * mem_here * groups * rows * columns
    fits = (
        columns == LANES
        and mem_here * STRIP == LANES
        and rows % groups == 0
        and 2 * (rows // groups) % mem_here == 0
        and rows % 8 == 0
        and groups & (groups - 1) == 0
        and groups in (8, 16)
        and LANES % (mem_here * groups) == 0
        and lax.axis_size("space") % 2 == 0
        and rest[-1].shape[0] == 1
        and whole_tile <= GATHER_BYTES
    )
    return (gathered if fits else exchanged)(prior_ensemble, *rest)


def solution(mesh):
    in_specs = (
        P("member", None, "space"),
        P(None, "space"),
        P(("space", "member"), None),
        P(("space", "member"), None),
        P(("space", "member"), None),
        P(("space", "member")),
    )
    out_specs = P("member", None, "space")
    return jax.shard_map(local, mesh=mesh, in_specs=in_specs, out_specs=out_specs, check_vma=False)
```

```python
import functools

import jax
import jax.numpy as jnp
from jax import lax
from jax.experimental import pallas as pl
from jax.experimental.pallas import tpu as pltpu
from jax.sharding import PartitionSpec as P

SUBSTEPS = 4
NS_ITERS = 6
LANES = 128
STRIP = 32
GATHER_BYTES = 4 << 20


def padded(block, sides, width):
    for axis, dim in sides:
        count = lax.axis_size(axis)
        forward = [(i, i + 1) for i in range(count - 1)]
        forward.append((count - 1, 0))
        backward = [(target, source) for source, target in forward]
        low = lax.ppermute(
            lax.slice_in_dim(block, block.shape[dim] - width, None, axis=dim), axis, forward
        )
        high = lax.ppermute(lax.slice_in_dim(block, 0, width, axis=dim), axis, backward)
        block = jnp.concatenate([low, block, high], axis=dim)
    return block


def tendency(center, east, west, wind_mid):
    pads = [(0, 0)] * (center.ndim - 2) + [(1, 1), (0, 0)]
    ypad = jnp.pad(center, pads)
    north = ypad[..., 2:, :]
    south = ypad[..., :-2, :]
    speed = wind_mid + 0.25 * jnp.tanh(center)
    return (
        center
        + 0.2 * (east - 2.0 * center + west)
        + 0.1 * (north - 2.0 * center + south)
        - 0.3 * speed * (east - west)
    )


def inverse_root(gram):
    order = gram.shape[0]
    ident = jnp.eye(order, dtype=jnp.float32)
    scale = jnp.sqrt(jnp.sum(gram * gram) + 1e-06)
    upper = gram / scale
    lower = ident
    for step in range(NS_ITERS):
        middle = 1.5 * ident - 0.5 * jnp.dot(lower, upper, precision=lax.Precision.HIGHEST)
        upper = jnp.dot(upper, middle, precision=lax.Precision.HIGHEST)
        lower = jnp.dot(middle, lower, precision=lax.Precision.HIGHEST)
    return lower / jnp.sqrt(scale)


def analyze(xb, cells, value, weight, count):
    order = xb.shape[0]
    slots = cells.shape[0]
    mean = jnp.sum(xb, axis=0) / order
    pert = xb - mean
    start_gram = (order - 1.0) * jnp.eye(order, dtype=jnp.float32)
    ypert = jnp.take(pert, cells, axis=1)
    ymean = jnp.take(mean, cells)
    live = (jnp.arange(slots, dtype=jnp.int32) < count).astype(jnp.float32)
    wts = weight * live
    gram = start_gram + jnp.dot(ypert * wts, ypert.T, precision=lax.Precision.HIGHEST)
    rhs = jnp.dot(ypert, wts * (value - ymean), precision=lax.Precision.HIGHEST)
    root = inverse_root(gram)
    wbar = jnp.dot(
        root, jnp.dot(root, rhs, precision=lax.Precision.HIGHEST), precision=lax.Precision.HIGHEST
    )
    trans = jnp.sqrt(order - 1.0) * root + wbar[:, None]
    return mean + jnp.dot(trans.T, pert, precision=lax.Precision.HIGHEST)


def exchanged(prior_ensemble, wind, obs_value, obs_weight, observed_cell_value, obs_count):
    stacked = jnp.concatenate([prior_ensemble, wind[None]], axis=0)
    extended = padded(stacked, (("space", 2),), SUBSTEPS)
    state = extended[:-1]
    wind_ext = extended[-1]
    for step in range(SUBSTEPS):
        edge = step + 1
        wind_mid = wind_ext[:, edge : wind_ext.shape[1] - edge]
        state = tendency(state[..., 1:-1], state[..., 2:], state[..., :-2], wind_mid)
    mem_here, latitude_lines, column_entries = state.shape
    groups = lax.axis_size("member")
    per_dev = obs_count.shape[0]
    cell_count = latitude_lines * column_entries // (groups * per_dev)
    blocks = state.reshape(mem_here, groups, per_dev, cell_count)
    arrived = lax.all_to_all(blocks, "member", split_axis=1, concat_axis=0, tiled=True)
    output_results = [
        analyze(arrived[:, 0, i], observed_cell_value[i], obs_value[i], obs_weight[i], obs_count[i])
        for i in range(per_dev)
    ]
    analysed_state = jnp.stack(output_results, axis=1)[:, None]
    returned = lax.all_to_all(analysed_state, "member", split_axis=0, concat_axis=1, tiled=True)
    return returned.reshape(mem_here, latitude_lines, column_entries)


def lane_of(shape):
    return lax.broadcasted_iota(jnp.int32, shape, 1)


def edge_kernel(start, wind_start, u_ref, z_ref):
    members, rows, _ = u_ref.shape
    members = members - 1
    lane = lane_of((rows, LANES))
    place = lane % STRIP
    column = 0 if start > STRIP // 2 else LANES - SUBSTEPS
    total = jnp.zeros((rows, LANES), jnp.float32)
    for m in range(members):
        for x, to in ((u_ref[m], start), (u_ref[members], wind_start)):
            moved = pltpu.roll(x, (STRIP * m + to - column) % LANES, 1)
            keep = (lane // STRIP == m) & (place >= to) & (place < to + SUBSTEPS)
            total = jnp.where(keep, moved, total)
    z_ref[...] = total


def strips(block):
    lane = lane_of(block[0].shape)
    west = (lane % STRIP) < STRIP // 2
    total = jnp.zeros(block[0].shape, jnp.float32)
    for m, x in enumerate(block):
        low = pltpu.roll(x, (STRIP * m + SUBSTEPS) % LANES, 1)
        high = pltpu.roll(x, (STRIP * m + STRIP - SUBSTEPS) % LANES, 1)
        total = jnp.where((lane // STRIP) == m, jnp.where(west, low, high), total)
    return total


def substep(x, wind3):
    rows = x.shape[0]
    row = lax.broadcasted_iota(jnp.int32, x.shape, 0)
    east = pltpu.roll(x, LANES - 1, 1)
    west = pltpu.roll(x, 1, 1)
    north = jnp.where(row == rows - 1, 0.0, pltpu.roll(x, rows - 1, 0))
    south = jnp.where(row == 0, 0.0, pltpu.roll(x, 1, 0))
    speed = wind3 + 0.075 * jnp.tanh(x)
    return 0.4 * x + 0.2 * (east + west) + 0.1 * (north + south) - speed * (east - west)


def pieces(x, count):
    out = []
    for _ in range(count):
        part = x.astype(jnp.bfloat16)
        out.append(part)
        x = x - part.astype(jnp.float32)
    return out


def interior_kernel(count_ref, u_ref, cell_ref, value_ref, weight_ref, f_ref, q_ref):
    mem_here, rows = u_ref.shape[0] - 1, u_ref.shape[1]
    stride = f_ref.shape[0] // mem_here
    extra = stride - rows
    wind3 = 0.3 * u_ref[mem_here]
    slots = cell_ref.shape[1]
    slot = lax.broadcasted_iota(jnp.int32, (1, slots), 1)
    weight = jnp.where(slot < count_ref[...], weight_ref[...], 0.0)
    parts = pieces(weight, 3) + pieces(weight * value_ref[...], 3)
    sub = lax.broadcasted_iota(jnp.int32, (8, slots), 0)
    lhs = jnp.zeros((8, slots), jnp.float32)
    for k, part in enumerate(parts):
        lhs = jnp.where(sub == k, part.astype(jnp.float32), lhs)
    lhs = lhs.astype(jnp.bfloat16)
    patch_rows = extra * mem_here // 2
    for q in range(patch_rows):
        cell = lax.broadcasted_iota(jnp.int32, (LANES, slots), 0) + LANES * q
        hot = jnp.where(cell == cell_ref[...], 1.0, 0.0).astype(jnp.bfloat16)
        sums = lax.dot_general(
            lhs, hot, (((1,), (1,)), ((), ())), preferred_element_type=jnp.float32
        )
        for which in range(2):
            k = which * patch_rows + q
            line = sums[3 * which : 3 * which + 1] + sums[3 * which + 1 : 3 * which + 2]
            line = line + sums[3 * which + 2 : 3 * which + 3]
            at = (k // extra) * stride + rows + k % extra
            f_ref[at : at + 1, :] = line
    q_ref[0:rows, :] = strips([u_ref[m] for m in range(mem_here)])
    q_ref[rows : 2 * rows, :] = strips([u_ref[mem_here]] * mem_here)
    for m in range(mem_here):
        x = u_ref[m]
        for _ in range(SUBSTEPS):
            x = substep(x, wind3)
        f_ref[m * stride : m * stride + rows, :] = x


def edges_kernel(q_ref, west_ref, east_ref, f_in_ref, f_ref):
    rows = q_ref.shape[0] // 2
    lane = lane_of((rows, LANES))
    place = lane % STRIP
    west, east = west_ref[...], east_ref[...]
    full = []
    for k in range(2):
        own = q_ref[k * rows : (k + 1) * rows, :]
        full.append(
            jnp.where(place < SUBSTEPS, west, jnp.where(place >= STRIP - SUBSTEPS, east, own))
        )
        west = pltpu.roll(west, LANES - SUBSTEPS, 1)
        east = pltpu.roll(east, SUBSTEPS, 1)
    x, wind3 = full[0], 0.3 * full[1]
    for _ in range(SUBSTEPS):
        x = substep(x, wind3)
    mem_here = LANES // STRIP
    stride = f_ref.shape[0] // mem_here
    for m in range(mem_here):
        low = pltpu.roll(x, (-STRIP * m - SUBSTEPS) % LANES, 1)
        high = pltpu.roll(x, (-STRIP * m - STRIP + SUBSTEPS) % LANES, 1)
        at = slice(m * stride, m * stride + rows)
        inside = f_in_ref[at, :]
        f_ref[at, :] = jnp.where(
            lane < SUBSTEPS, low, jnp.where(lane >= LANES - SUBSTEPS, high, inside)
        )
        at = slice(m * stride + rows, (m + 1) * stride)
        f_ref[at, :] = f_in_ref[at, :]


def visits(groups):
    chips = [groups - 2, *range(2, groups - 2, 2)]
    return [0, *[chip + (i + 1) % 2 for i, chip in enumerate(chips)]]


def analysis_kernel(dims, me_ref, cat_ref, sib_ref, o_ref, ob_ref, pert_ref, scaled_ref, mean_ref):
    mem_here, rows, groups = dims
    f32, bf16 = jnp.float32, jnp.bfloat16
    order = mem_here * groups
    height = rows // groups
    cells = height * LANES
    wide = order * groups
    stride = cat_ref.shape[0] * 2 // order
    per = LANES // order
    sets = range(groups // per)
    plain, turned = (((1,), (0,)), ((), ())), (((1,), (1,)), ((), ()))
    me = me_ref[0]

    def dot(x, y, how):
        return lax.dot_general(x, y, how, preferred_element_type=f32)

    def split(x):
        high = x.astype(bf16)
        return high, (x - high.astype(f32)).astype(bf16)

    for side, ref in enumerate((cat_ref, sib_ref)):
        for k in range(groups // 2):
            patch = me ^ (visits(groups)[k] ^ side)
            base = k * mem_here * stride
            lines = [
                ref[base + m * stride + rows : base + (m + 1) * stride, :] for m in range(mem_here)
            ]
            ob_ref[pl.ds(pl.multiple_of(patch * 2 * height, 2 * height), 2 * height), :] = (
                jnp.concatenate(lines, axis=0)
            )

    for p in range(groups):
        for q in range(height):
            at = pl.ds(p * height + q, order // 2, stride=stride)
            xb = jnp.concatenate([cat_ref[at, :], sib_ref[at, :]], axis=0)
            mean = jnp.sum(xb, axis=0, keepdims=True) * (1.0 / order)
            pert = xb - mean
            lanes = slice(q * LANES, (q + 1) * LANES)
            line = p * 2 * height + q
            pert_ref[p * order : (p + 1) * order, lanes] = pert
            scaled_ref[p * order : (p + 1) * order, lanes] = pert * ob_ref[line : line + 1, :]
            mean_ref[p : p + 1, lanes] = mean
    lift = []
    for q in range(height):
        weight = ob_ref[pl.ds(q, groups, stride=2 * height), :]
        lift.append(
            ob_ref[pl.ds(height + q, groups, stride=2 * height), :]
            - weight * mean_ref[:, q * LANES : (q + 1) * LANES]
        )
    lift = jnp.concatenate(lift, axis=1)
    lift = jnp.concatenate([lift] * (16 // groups), axis=0)
    lift_high, lift_low = split(lift)

    pert_high, pert_low = split(pert_ref[...])
    scaled_high, scaled_low = split(scaled_ref[...])
    own_row = lax.broadcasted_iota(jnp.int32, (order, LANES), 0)
    lane = lax.broadcasted_iota(jnp.int32, (order, LANES), 1)
    ident = jnp.where(own_row == lane % order, 1.0, 0.0)
    tail_row = lax.broadcasted_iota(jnp.int32, (16, LANES), 0)
    tail_block = lax.broadcasted_iota(jnp.int32, (16, LANES), 1) // order
    square_row = lax.broadcasted_iota(jnp.int32, (LANES, LANES), 0) // order
    square_lane = lax.broadcasted_iota(jnp.int32, (LANES, LANES), 1) // order
    diag = jnp.where(square_row == square_lane, 1.0, 0.0).astype(bf16)
    grams, prod, middle, lower, vec, inverse = [], [], [], [], [], []
    for t in sets:
        at = slice(t * LANES, (t + 1) * LANES)
        left_high = jnp.concatenate([scaled_high[at], lift_high], axis=0)
        left_low = jnp.concatenate([scaled_low[at], lift_low], axis=0)
        right = jnp.concatenate([pert_high[at], pert_low[at]], axis=0)
        out = dot(left_high, right, turned)
        full = out[:, :LANES] + out[:, LANES:] + dot(left_low, pert_high[at], turned)
        gram = (order - 1.0) * ident
        for p in range(per):
            gram = gram + jnp.where(lane // order == p, full[p * order : (p + 1) * order], 0.0)
        rhs = jnp.sum(
            jnp.where(tail_row == tail_block + per * t, full[LANES:], 0.0), axis=0, keepdims=True
        )
        grams.append(gram)
        vec.append(jnp.where(tail_row == 0, rhs, 0.0))

    def weights(x):
        high, low = (jnp.concatenate([part] * per, axis=0) * diag for part in split(x))
        top = jnp.concatenate([high, low], axis=1)
        return jnp.concatenate([top, jnp.concatenate([high, jnp.zeros_like(high)], axis=1)], axis=0)

    def product(x, right):
        out = dot(jnp.concatenate(split(x), axis=1), right, plain)
        return out[:, :LANES] + out[:, LANES:]

    twice = []
    for t in sets:
        twice.append(product(jnp.concatenate([grams[t], vec[t]], axis=0), weights(grams[t])))
    for t in sets:
        square = jnp.sum(grams[t] * grams[t], axis=0, keepdims=True)
        group = lane[0:1] // order
        total = jnp.zeros((1, LANES), f32)
        for p in range(per):
            mine = group == p
            total = jnp.where(mine, jnp.sum(jnp.where(mine, square, 0.0), axis=1, keepdims=True), total)
        square = total
        inverse.append(1.0 / jnp.sqrt(square + 1e-06))
        first = grams[t] * inverse[t]
        middle.append(1.5 * ident - 0.5 * first)
        lower.append(middle[t])
        prod.append(1.5 * first - (0.5 * inverse[t]) * (twice[t][:order] * inverse[t]))
        vec[t] = 1.5 * vec[t] - (0.5 * inverse[t]) * twice[t][order:]
    for step in range(NS_ITERS):
        last = step == NS_ITERS - 1
        right = [weights(middle[t]) for t in sets]
        if step:
            for t in sets:
                left = ([] if last else [prod[t]]) + [lower[t], vec[t]]
                out = product(jnp.concatenate(left, axis=0), right[t])
                if not last:
                    prod[t], out = out[:order], out[order:]
                lower[t], vec[t] = out[:order], out[order:]
        if not last:
            for t in sets:
                prod[t] = product(prod[t], right[t])
                middle[t] = 1.5 * ident - 0.5 * prod[t]
    pick = lax.broadcasted_iota(jnp.int32, (groups, LANES), 0)
    tall = []
    for t in sets:
        wbar = product(vec[t], weights(lower[t]))[0:1] * inverse[t]
        own = lower[t][0:mem_here] * (jnp.sqrt(inverse[t]) * (order - 1.0) ** 0.5) + wbar
        keep = pick == lax.broadcasted_iota(jnp.int32, (groups, LANES), 1) // order + per * t
        tall.append(
            jnp.concatenate(
                [jnp.where(keep, own[i : i + 1], 0.0) for i in range(mem_here)], axis=0
            )
        )

    tall_high, tall_low = split(jnp.concatenate(tall, axis=1))
    both = dot(jnp.concatenate([tall_high, tall_low], axis=0), pert_high, plain)
    count = groups * mem_here
    out = both[:count] + both[count:] + dot(tall_high, pert_low, plain)
    for i in range(mem_here):
        for q in range(height):
            lanes = slice(q * LANES, (q + 1) * LANES)
            o_ref[pl.ds(i * rows + q, groups, stride=height), :] = (
                out[i * groups : (i + 1) * groups, lanes] + mean_ref[:, lanes]
            )


def kernel_call(body, *out_shapes, scratch=(), smem=(), work=None):
    def call(*args):
        specs = [
            pl.BlockSpec(memory_space=pltpu.SMEM if i in smem else pltpu.VMEM)
            for i in range(len(args))
        ]
        out = pl.pallas_call(
            body,
            out_shape=[jax.ShapeDtypeStruct(shape, jnp.float32) for shape in out_shapes],
            in_specs=specs,
            out_specs=[pl.BlockSpec(memory_space=pltpu.VMEM) for _ in out_shapes],
            scratch_shapes=list(scratch),
            compiler_params=pltpu.CompilerParams(vmem_limit_bytes=32 << 20),
            cost_estimate=work
            and pl.CostEstimate(flops=work, bytes_accessed=work, transcendentals=0),
        )(*args)
        return out[0] if len(out_shapes) == 1 else out

    return call


def gathered(prior_ensemble, wind, obs_value, obs_weight, observed_cell_value, obs_count):
    mem_here, rows, _ = prior_ensemble.shape
    groups = lax.axis_size("member")
    count = lax.axis_size("space")
    order = mem_here * groups
    height = rows // groups
    stride = rows + 2 * height // mem_here
    wide, cells = order * groups, height * LANES
    f32 = jnp.float32

    both = jnp.concatenate([prior_ensemble, wind[None]], axis=0)
    forward = [(i, (i + 1) % count) for i in range(count)]
    backward = [(i, (i - 1) % count) for i in range(count)]
    eastern = kernel_call(functools.partial(edge_kernel, 0, SUBSTEPS), (rows, LANES))(both)
    western = kernel_call(
        functools.partial(edge_kernel, STRIP - SUBSTEPS, STRIP - 2 * SUBSTEPS), (rows, LANES), work=None
    )(both)
    east = lax.ppermute(western, "space", backward)
    west = lax.ppermute(eastern, "space", forward)
    inside, near = kernel_call(interior_kernel, (mem_here * stride, LANES), (2 * rows, LANES))(
        obs_count.reshape(1, 1), both, observed_cell_value, obs_value, obs_weight
    )
    payload = kernel_call(edges_kernel, (mem_here * stride, LANES))(near, west, east, inside)

    def swap(x, k):
        return lax.ppermute(x, "member", [(i, i ^ k) for i in range(groups)])

    held = [payload] + [swap(payload, k) for k in visits(groups)[1:]]
    cat = jnp.concatenate(held, axis=0)
    first = jnp.concatenate(held[:2], axis=0)
    sibling = jnp.concatenate([swap(x, 1) for x in [first, *held[2:]]], axis=0)
    me = lax.axis_index("member").astype(jnp.int32).reshape(1)
    out = kernel_call(
        functools.partial(analysis_kernel, (mem_here, rows, groups)),
        (mem_here * rows, LANES),
        scratch=[
            pltpu.VMEM((groups * 2 * height, LANES), f32),
            pltpu.VMEM((wide, cells), f32),
            pltpu.VMEM((wide, cells), f32),
            pltpu.VMEM((groups, cells), f32),
        ],
        smem=(0,),
    )(me, cat, sibling)
    return out.reshape(mem_here, rows, LANES)


def local(prior_ensemble, *rest):
    mem_here, rows, columns = prior_ensemble.shape
    groups = lax.axis_size("member")
    whole_tile = 4 * mem_here * groups * rows * columns
    fits = (
        columns == LANES
        and mem_here * STRIP == LANES
        and rows % groups == 0
        and 2 * (rows // groups) % mem_here == 0
        and rows % 8 == 0
        and groups & (groups - 1) == 0
        and groups in (8, 16)
        and LANES % (mem_here * groups) == 0
        and lax.axis_size("space") % 2 == 0
        and rest[-1].shape[0] == 1
        and whole_tile <= GATHER_BYTES
    )
    return (gathered if fits else exchanged)(prior_ensemble, *rest)


def solution(mesh):
    in_specs = (
        P("member", None, "space"),
        P(None, "space"),
        P(("space", "member"), None),
        P(("space", "member"), None),
        P(("space", "member"), None),
        P(("space", "member")),
    )
    out_specs = P("member", None, "space")
    return jax.shard_map(local, mesh=mesh, in_specs=in_specs, out_specs=out_specs, check_vma=False)
```

```python
import functools

import jax
import jax.numpy as jnp
from jax import lax
from jax.experimental import pallas as pl
from jax.experimental.pallas import tpu as pltpu
from jax.sharding import PartitionSpec as P

SUBSTEPS = 4
NS_ITERS = 6
LANES = 128
STRIP = 32
GATHER_BYTES = 4 << 20


def padded(block, sides, width):
    for axis, dim in sides:
        count = lax.axis_size(axis)
        forward = [(i, i + 1) for i in range(count - 1)]
        forward.append((count - 1, 0))
        backward = [(target, source) for source, target in forward]
        low = lax.ppermute(
            lax.slice_in_dim(block, block.shape[dim] - width, None, axis=dim), axis, forward
        )
        high = lax.ppermute(lax.slice_in_dim(block, 0, width, axis=dim), axis, backward)
        block = jnp.concatenate([low, block, high], axis=dim)
    return block


def tendency(center, east, west, wind_mid):
    pads = [(0, 0)] * (center.ndim - 2) + [(1, 1), (0, 0)]
    ypad = jnp.pad(center, pads)
    north = ypad[..., 2:, :]
    south = ypad[..., :-2, :]
    speed = wind_mid + 0.25 * jnp.tanh(center)
    return (
        center
        + 0.2 * (east - 2.0 * center + west)
        + 0.1 * (north - 2.0 * center + south)
        - 0.3 * speed * (east - west)
    )


def inverse_root(gram):
    order = gram.shape[0]
    ident = jnp.eye(order, dtype=jnp.float32)
    scale = jnp.sqrt(jnp.sum(gram * gram) + 1e-06)
    upper = gram / scale
    lower = ident
    for step in range(NS_ITERS):
        middle = 1.5 * ident - 0.5 * jnp.dot(lower, upper, precision=lax.Precision.HIGHEST)
        upper = jnp.dot(upper, middle, precision=lax.Precision.HIGHEST)
        lower = jnp.dot(middle, lower, precision=lax.Precision.HIGHEST)
    return lower / jnp.sqrt(scale)


def analyze(xb, cells, value, weight, count):
    order = xb.shape[0]
    slots = cells.shape[0]
    mean = jnp.sum(xb, axis=0) / order
    pert = xb - mean
    start_gram = (order - 1.0) * jnp.eye(order, dtype=jnp.float32)
    ypert = jnp.take(pert, cells, axis=1)
    ymean = jnp.take(mean, cells)
    live = (jnp.arange(slots, dtype=jnp.int32) < count).astype(jnp.float32)
    wts = weight * live
    gram = start_gram + jnp.dot(ypert * wts, ypert.T, precision=lax.Precision.HIGHEST)
    rhs = jnp.dot(ypert, wts * (value - ymean), precision=lax.Precision.HIGHEST)
    root = inverse_root(gram)
    wbar = jnp.dot(
        root, jnp.dot(root, rhs, precision=lax.Precision.HIGHEST), precision=lax.Precision.HIGHEST
    )
    trans = jnp.sqrt(order - 1.0) * root + wbar[:, None]
    return mean + jnp.dot(trans.T, pert, precision=lax.Precision.HIGHEST)


def exchanged(prior_ensemble, wind, obs_value, obs_weight, observed_cell_value, obs_count):
    stacked = jnp.concatenate([prior_ensemble, wind[None]], axis=0)
    extended = padded(stacked, (("space", 2),), SUBSTEPS)
    state = extended[:-1]
    wind_ext = extended[-1]
    for step in range(SUBSTEPS):
        edge = step + 1
        wind_mid = wind_ext[:, edge : wind_ext.shape[1] - edge]
        state = tendency(state[..., 1:-1], state[..., 2:], state[..., :-2], wind_mid)
    mem_here, latitude_lines, column_entries = state.shape
    groups = lax.axis_size("member")
    per_dev = obs_count.shape[0]
    cell_count = latitude_lines * column_entries // (groups * per_dev)
    blocks = state.reshape(mem_here, groups, per_dev, cell_count)
    arrived = lax.all_to_all(blocks, "member", split_axis=1, concat_axis=0, tiled=True)
    output_results = [
        analyze(arrived[:, 0, i], observed_cell_value[i], obs_value[i], obs_weight[i], obs_count[i])
        for i in range(per_dev)
    ]
    analysed_state = jnp.stack(output_results, axis=1)[:, None]
    returned = lax.all_to_all(analysed_state, "member", split_axis=0, concat_axis=1, tiled=True)
    return returned.reshape(mem_here, latitude_lines, column_entries)


def lane_of(shape):
    return lax.broadcasted_iota(jnp.int32, shape, 1)


def edge_kernel(start, wind_start, u_ref, z_ref):
    members, rows, _ = u_ref.shape
    members = members - 1
    lane = lane_of((rows, LANES))
    place = lane % STRIP
    column = 0 if start > STRIP // 2 else LANES - SUBSTEPS
    total = jnp.zeros((rows, LANES), jnp.float32)
    for m in range(members):
        for x, to in ((u_ref[m], start), (u_ref[members], wind_start)):
            moved = pltpu.roll(x, (STRIP * m + to - column) % LANES, 1)
            keep = (lane // STRIP == m) & (place >= to) & (place < to + SUBSTEPS)
            total = jnp.where(keep, moved, total)
    z_ref[...] = total


def strips(block):
    lane = lane_of(block[0].shape)
    west = (lane % STRIP) < STRIP // 2
    total = jnp.zeros(block[0].shape, jnp.float32)
    for m, x in enumerate(block):
        low = pltpu.roll(x, (STRIP * m + SUBSTEPS) % LANES, 1)
        high = pltpu.roll(x, (STRIP * m + STRIP - SUBSTEPS) % LANES, 1)
        total = jnp.where((lane // STRIP) == m, jnp.where(west, low, high), total)
    return total


def stencil(x, east, west, wind3):
    rows = x.shape[0]
    row = lax.broadcasted_iota(jnp.int32, x.shape, 0)
    north = jnp.where(row == rows - 1, 0.0, pltpu.roll(x, rows - 1, 0))
    south = jnp.where(row == 0, 0.0, pltpu.roll(x, 1, 0))
    speed = wind3 + 0.075 * jnp.tanh(x)
    return 0.4 * x + 0.2 * (east + west) + 0.1 * (north + south) - speed * (east - west)


def shifted(x, by):
    return pltpu.roll(x, -by % LANES, 1) if by else x


def substep(x, wind3):
    return stencil(x, shifted(x, 1), shifted(x, -1), wind3)


def substeps(x, wind3, count):
    at = {k: shifted(x, k) for k in range(-count, count + 1)}
    winds = {k: shifted(wind3, k) for k in range(1 - count, count)}
    for reach in range(count - 1, -1, -1):
        at = {
            k: stencil(at[k], at[k + 1], at[k - 1], winds[k]) for k in range(-reach, reach + 1)
        }
    return at[0]


def pieces(x, count):
    out = []
    for _ in range(count):
        part = x.astype(jnp.bfloat16)
        out.append(part)
        x = x - part.astype(jnp.float32)
    return out


def interior_kernel(count_ref, u_ref, cell_ref, value_ref, weight_ref, f_ref, q_ref):
    mem_here, rows = u_ref.shape[0] - 1, u_ref.shape[1]
    stride = f_ref.shape[0] // mem_here
    extra = stride - rows
    wind3 = 0.3 * u_ref[mem_here]
    slots = cell_ref.shape[1]
    slot = lax.broadcasted_iota(jnp.int32, (1, slots), 1)
    weight = jnp.where(slot < count_ref[...], weight_ref[...], 0.0)
    parts = pieces(weight, 3) + pieces(weight * value_ref[...], 3)
    sub = lax.broadcasted_iota(jnp.int32, (8, slots), 0)
    lhs = jnp.zeros((8, slots), jnp.float32)
    for k, part in enumerate(parts):
        lhs = jnp.where(sub == k, part.astype(jnp.float32), lhs)
    lhs = lhs.astype(jnp.bfloat16)
    patch_rows = extra * mem_here // 2
    for q in range(patch_rows):
        cell = lax.broadcasted_iota(jnp.int32, (LANES, slots), 0) + LANES * q
        hot = jnp.where(cell == cell_ref[...], 1.0, 0.0).astype(jnp.bfloat16)
        sums = lax.dot_general(
            lhs, hot, (((1,), (1,)), ((), ())), preferred_element_type=jnp.float32
        )
        for which in range(2):
            k = which * patch_rows + q
            line = sums[3 * which : 3 * which + 1] + sums[3 * which + 1 : 3 * which + 2]
            line = line + sums[3 * which + 2 : 3 * which + 3]
            at = (k // extra) * stride + rows + k % extra
            f_ref[at : at + 1, :] = line
    q_ref[0:rows, :] = strips([u_ref[m] for m in range(mem_here)])
    q_ref[rows : 2 * rows, :] = strips([u_ref[mem_here]] * mem_here)
    for m in range(mem_here):
        x = u_ref[m]
        for _ in range(SUBSTEPS):
            x = substep(x, wind3)
        f_ref[m * stride : m * stride + rows, :] = x


def edges_kernel(q_ref, west_ref, east_ref, f_in_ref, f_ref):
    rows = q_ref.shape[0] // 2
    lane = lane_of((rows, LANES))
    place = lane % STRIP
    west, east = west_ref[...], east_ref[...]
    full = []
    for k in range(2):
        own = q_ref[k * rows : (k + 1) * rows, :]
        full.append(
            jnp.where(place < SUBSTEPS, west, jnp.where(place >= STRIP - SUBSTEPS, east, own))
        )
        west = pltpu.roll(west, LANES - SUBSTEPS, 1)
        east = pltpu.roll(east, SUBSTEPS, 1)
    x, wind3 = full[0], 0.3 * full[1]
    x = substeps(x, wind3, SUBSTEPS)
    mem_here = LANES // STRIP
    stride = f_ref.shape[0] // mem_here
    for m in range(mem_here):
        low = pltpu.roll(x, (-STRIP * m - SUBSTEPS) % LANES, 1)
        high = pltpu.roll(x, (-STRIP * m - STRIP + SUBSTEPS) % LANES, 1)
        at = slice(m * stride, m * stride + rows)
        inside = f_in_ref[at, :]
        f_ref[at, :] = jnp.where(
            lane < SUBSTEPS, low, jnp.where(lane >= LANES - SUBSTEPS, high, inside)
        )
        at = slice(m * stride + rows, (m + 1) * stride)
        f_ref[at, :] = f_in_ref[at, :]


def visits(groups):
    chips = [groups - 2, *range(2, groups - 2, 2)]
    return [0, *[chip + (i + 1) % 2 for i, chip in enumerate(chips)]]


def analysis_kernel(dims, me_ref, cat_ref, sib_ref, o_ref, ob_ref, pert_ref, scaled_ref, mean_ref, done_ref, sems):
    mem_here, rows, groups = dims
    f32, bf16 = jnp.float32, jnp.bfloat16
    order = mem_here * groups
    height = rows // groups
    cells = height * LANES
    wide = order * groups
    stride = cat_ref.shape[0] * 2 // order
    per = LANES // order
    sets = range(groups // per)
    plain, turned = (((1,), (0,)), ((), ())), (((1,), (1,)), ((), ()))
    me = me_ref[0]

    def dot(x, y, how):
        return lax.dot_general(x, y, how, preferred_element_type=f32)

    def split(x):
        high = x.astype(bf16)
        return high, (x - high.astype(f32)).astype(bf16)

    for side, ref in enumerate((cat_ref, sib_ref)):
        for k in range(groups // 2):
            patch = me ^ (visits(groups)[k] ^ side)
            base = k * mem_here * stride
            lines = [
                ref[base + m * stride + rows : base + (m + 1) * stride, :] for m in range(mem_here)
            ]
            ob_ref[pl.ds(pl.multiple_of(patch * 2 * height, 2 * height), 2 * height), :] = (
                jnp.concatenate(lines, axis=0)
            )

    for p in range(groups):
        for q in range(height):
            at = pl.ds(p * height + q, order // 2, stride=stride)
            xb = jnp.concatenate([cat_ref[at, :], sib_ref[at, :]], axis=0)
            mean = jnp.sum(xb, axis=0, keepdims=True) * (1.0 / order)
            pert = xb - mean
            lanes = slice(q * LANES, (q + 1) * LANES)
            line = p * 2 * height + q
            pert_ref[p * order : (p + 1) * order, lanes] = pert
            scaled_ref[p * order : (p + 1) * order, lanes] = pert * ob_ref[line : line + 1, :]
            mean_ref[p : p + 1, lanes] = mean
    lift = []
    for q in range(height):
        weight = ob_ref[pl.ds(q, groups, stride=2 * height), :]
        lift.append(
            ob_ref[pl.ds(height + q, groups, stride=2 * height), :]
            - weight * mean_ref[:, q * LANES : (q + 1) * LANES]
        )
    lift = jnp.concatenate(lift, axis=1)
    lift = jnp.concatenate([lift] * (16 // groups), axis=0)
    lift_high, lift_low = split(lift)

    pert_high, pert_low = split(pert_ref[...])
    scaled_high, scaled_low = split(scaled_ref[...])
    own_row = lax.broadcasted_iota(jnp.int32, (order, LANES), 0)
    lane = lax.broadcasted_iota(jnp.int32, (order, LANES), 1)
    ident = jnp.where(own_row == lane % order, 1.0, 0.0)
    tail_row = lax.broadcasted_iota(jnp.int32, (16, LANES), 0)
    tail_block = lax.broadcasted_iota(jnp.int32, (16, LANES), 1) // order
    square_row = lax.broadcasted_iota(jnp.int32, (LANES, LANES), 0) // order
    square_lane = lax.broadcasted_iota(jnp.int32, (LANES, LANES), 1) // order
    diag = jnp.where(square_row == square_lane, 1.0, 0.0).astype(bf16)
    grams, prod, middle, lower, vec, inverse = [], [], [], [], [], []
    for t in sets:
        at = slice(t * LANES, (t + 1) * LANES)
        left_high = jnp.concatenate([scaled_high[at], lift_high], axis=0)
        left_low = jnp.concatenate([scaled_low[at], lift_low], axis=0)
        right = jnp.concatenate([pert_high[at], pert_low[at]], axis=0)
        out = dot(left_high, right, turned)
        full = out[:, :LANES] + out[:, LANES:] + dot(left_low, pert_high[at], turned)
        gram = (order - 1.0) * ident
        for p in range(per):
            gram = gram + jnp.where(lane // order == p, full[p * order : (p + 1) * order], 0.0)
        rhs = jnp.sum(
            jnp.where(tail_row == tail_block + per * t, full[LANES:], 0.0), axis=0, keepdims=True
        )
        grams.append(gram)
        vec.append(jnp.where(tail_row == 0, rhs, 0.0))

    def weights(x):
        high, low = (jnp.concatenate([part] * per, axis=0) * diag for part in split(x))
        top = jnp.concatenate([high, low], axis=1)
        return jnp.concatenate([top, jnp.concatenate([high, jnp.zeros_like(high)], axis=1)], axis=0)

    def product(x, right):
        out = dot(jnp.concatenate(split(x), axis=1), right, plain)
        return out[:, :LANES] + out[:, LANES:]

    twice = []
    for t in sets:
        twice.append(product(jnp.concatenate([grams[t], vec[t]], axis=0), weights(grams[t])))
    for t in sets:
        square = jnp.sum(grams[t] * grams[t], axis=0, keepdims=True)
        group = lane[0:1] // order
        total = jnp.zeros((1, LANES), f32)
        for p in range(per):
            mine = group == p
            total = jnp.where(mine, jnp.sum(jnp.where(mine, square, 0.0), axis=1, keepdims=True), total)
        inverse.append(1.0 / jnp.sqrt(total + 1e-06))
        first = grams[t] * inverse[t]
        middle.append(1.5 * ident - 0.5 * first)
        prod.append(1.5 * first - (0.5 * inverse[t]) * (twice[t][:order] * inverse[t]))
        vec[t] = 1.5 * vec[t] - (0.5 * inverse[t]) * twice[t][order:]
        lower.append(middle[t][0:8])
    for step in range(NS_ITERS):
        right = [weights(middle[t]) for t in sets]
        last = step == NS_ITERS - 1
        if step:
            for t in sets:
                left = ([] if last else [prod[t]]) + [vec[t][0:8], lower[t]]
                out = product(jnp.concatenate(left, axis=0), right[t])
                if not last:
                    prod[t], out = out[:order], out[order:]
                vec[t], lower[t] = out, out[8:16]
        for t in sets:
            left = [vec[t]] if last else [prod[t], vec[t]]
            out = product(jnp.concatenate(left, axis=0), right[t])
            if not last:
                prod[t], out = out[:order], out[order:]
                middle[t] = 1.5 * ident - 0.5 * prod[t]
            vec[t] = out
    pick = lax.broadcasted_iota(jnp.int32, (groups, LANES), 0)
    tall = []
    for t in sets:
        own = lower[t] * (jnp.sqrt(inverse[t]) * (order - 1.0) ** 0.5) + vec[t][0:1] * inverse[t]
        keep = pick == lax.broadcasted_iota(jnp.int32, (groups, LANES), 1) // order + per * t
        tall.append(
            jnp.concatenate(
                [jnp.where(keep, own[i : i + 1], 0.0) for i in range(mem_here)], axis=0
            )
        )

    tall_high, tall_low = split(jnp.concatenate(tall, axis=1))
    both = dot(jnp.concatenate([tall_high, tall_low], axis=0), pert_high, plain)
    count = groups * mem_here
    out = both[:count] + both[count:] + dot(tall_high, pert_low, plain)
    copies = []
    for i in range(mem_here):
        for q in range(height):
            lanes = slice(q * LANES, (q + 1) * LANES)
            done_ref[pl.ds(i * rows + q, groups, stride=height), :] = (
                out[i * groups : (i + 1) * groups, lanes] + mean_ref[:, lanes]
            )
        at = pl.ds(i * rows, rows)
        copies.append(pltpu.make_async_copy(done_ref.at[at], o_ref.at[at], sems.at[i]))
        copies[i].start()
    for copy in copies:
        copy.wait()


def kernel_call(body, *out_shapes, scratch=(), smem=(), out_space=pltpu.VMEM):
    def call(*args):
        specs = [
            pl.BlockSpec(memory_space=pltpu.SMEM if i in smem else pltpu.VMEM)
            for i in range(len(args))
        ]
        out = pl.pallas_call(
            body,
            out_shape=[jax.ShapeDtypeStruct(shape, jnp.float32) for shape in out_shapes],
            in_specs=specs,
            out_specs=[pl.BlockSpec(memory_space=out_space) for _ in out_shapes],
            scratch_shapes=list(scratch),
            compiler_params=pltpu.CompilerParams(vmem_limit_bytes=32 << 20),
        )(*args)
        return out[0] if len(out_shapes) == 1 else out

    return call


def gathered(prior_ensemble, wind, obs_value, obs_weight, observed_cell_value, obs_count):
    mem_here, rows, _ = prior_ensemble.shape
    groups = lax.axis_size("member")
    count = lax.axis_size("space")
    order = mem_here * groups
    height = rows // groups
    stride = rows + 2 * height // mem_here
    wide, cells = order * groups, height * LANES
    f32 = jnp.float32

    both = jnp.concatenate([prior_ensemble, wind[None]], axis=0)
    forward = [(i, (i + 1) % count) for i in range(count)]
    backward = [(i, (i - 1) % count) for i in range(count)]
    eastern = kernel_call(functools.partial(edge_kernel, 0, SUBSTEPS), (rows, LANES))(both)
    western = kernel_call(
        functools.partial(edge_kernel, STRIP - SUBSTEPS, STRIP - 2 * SUBSTEPS), (rows, LANES)
    )(both)
    east = lax.ppermute(western, "space", backward)
    west = lax.ppermute(eastern, "space", forward)
    inside, near = kernel_call(interior_kernel, (mem_here * stride, LANES), (2 * rows, LANES))(
        obs_count.reshape(1, 1), both, observed_cell_value, obs_value, obs_weight
    )
    payload = kernel_call(edges_kernel, (mem_here * stride, LANES))(near, west, east, inside)

    def swap(x, k):
        return lax.ppermute(x, "member", [(i, i ^ k) for i in range(groups)])

    held = [payload] + [swap(payload, k) for k in visits(groups)[1:]]
    cat = jnp.concatenate(held, axis=0)
    first = jnp.concatenate(held[:2], axis=0)
    sibling = jnp.concatenate([swap(x, 1) for x in [first, *held[2:]]], axis=0)
    me = lax.axis_index("member").astype(jnp.int32).reshape(1)
    out = kernel_call(
        functools.partial(analysis_kernel, (mem_here, rows, groups)),
        (mem_here * rows, LANES),
        scratch=[
            pltpu.VMEM((groups * 2 * height, LANES), f32),
            pltpu.VMEM((wide, cells), f32),
            pltpu.VMEM((wide, cells), f32),
            pltpu.VMEM((groups, cells), f32),
            pltpu.VMEM((mem_here * rows, LANES), f32),
            pltpu.SemaphoreType.DMA((mem_here,)),
        ],
        smem=(0,),
        out_space=pl.ANY,
    )(me, cat, sibling)
    return out.reshape(mem_here, rows, LANES)


def local(prior_ensemble, *rest):
    mem_here, rows, columns = prior_ensemble.shape
    groups = lax.axis_size("member")
    whole_tile = 4 * mem_here * groups * rows * columns
    fits = (
        columns == LANES
        and mem_here * STRIP == LANES
        and rows % groups == 0
        and 2 * (rows // groups) % mem_here == 0
        and rows % 8 == 0
        and groups & (groups - 1) == 0
        and groups in (8, 16)
        and LANES % (mem_here * groups) == 0
        and lax.axis_size("space") % 2 == 0
        and rest[-1].shape[0] == 1
        and whole_tile <= GATHER_BYTES
    )
    return (gathered if fits else exchanged)(prior_ensemble, *rest)


def solution(mesh):
    in_specs = (
        P("member", None, "space"),
        P(None, "space"),
        P(("space", "member"), None),
        P(("space", "member"), None),
        P(("space", "member"), None),
        P(("space", "member")),
    )
    out_specs = P("member", None, "space")
    return jax.shard_map(local, mesh=mesh, in_specs=in_specs, out_specs=out_specs, check_vma=False)
```

```python
import functools

import jax
import jax.numpy as jnp
from jax import lax
from jax.experimental import pallas as pl
from jax.experimental.pallas import tpu as pltpu
from jax.sharding import PartitionSpec as P

SUBSTEPS = 4
NS_ITERS = 6
LANES = 128
STRIP = 32
GATHER_BYTES = 4 << 20


def padded(block, sides, width):
    for axis, dim in sides:
        count = lax.axis_size(axis)
        forward = [(i, i + 1) for i in range(count - 1)]
        forward.append((count - 1, 0))
        backward = [(target, source) for source, target in forward]
        low = lax.ppermute(
            lax.slice_in_dim(block, block.shape[dim] - width, None, axis=dim), axis, forward
        )
        high = lax.ppermute(lax.slice_in_dim(block, 0, width, axis=dim), axis, backward)
        block = jnp.concatenate([low, block, high], axis=dim)
    return block


def tendency(center, east, west, wind_mid):
    pads = [(0, 0)] * (center.ndim - 2) + [(1, 1), (0, 0)]
    ypad = jnp.pad(center, pads)
    north = ypad[..., 2:, :]
    south = ypad[..., :-2, :]
    speed = wind_mid + 0.25 * jnp.tanh(center)
    return (
        center
        + 0.2 * (east - 2.0 * center + west)
        + 0.1 * (north - 2.0 * center + south)
        - 0.3 * speed * (east - west)
    )


def inverse_root(gram):
    order = gram.shape[0]
    ident = jnp.eye(order, dtype=jnp.float32)
    scale = jnp.sqrt(jnp.sum(gram * gram) + 1e-06)
    upper = gram / scale
    lower = ident
    for step in range(NS_ITERS):
        middle = 1.5 * ident - 0.5 * jnp.dot(lower, upper, precision=lax.Precision.HIGHEST)
        upper = jnp.dot(upper, middle, precision=lax.Precision.HIGHEST)
        lower = jnp.dot(middle, lower, precision=lax.Precision.HIGHEST)
    return lower / jnp.sqrt(scale)


def analyze(xb, cells, value, weight, count):
    order = xb.shape[0]
    slots = cells.shape[0]
    mean = jnp.sum(xb, axis=0) / order
    pert = xb - mean
    start_gram = (order - 1.0) * jnp.eye(order, dtype=jnp.float32)
    ypert = jnp.take(pert, cells, axis=1)
    ymean = jnp.take(mean, cells)
    live = (jnp.arange(slots, dtype=jnp.int32) < count).astype(jnp.float32)
    wts = weight * live
    gram = start_gram + jnp.dot(ypert * wts, ypert.T, precision=lax.Precision.HIGHEST)
    rhs = jnp.dot(ypert, wts * (value - ymean), precision=lax.Precision.HIGHEST)
    root = inverse_root(gram)
    wbar = jnp.dot(
        root, jnp.dot(root, rhs, precision=lax.Precision.HIGHEST), precision=lax.Precision.HIGHEST
    )
    trans = jnp.sqrt(order - 1.0) * root + wbar[:, None]
    return mean + jnp.dot(trans.T, pert, precision=lax.Precision.HIGHEST)


def exchanged(prior_ensemble, wind, obs_value, obs_weight, observed_cell_value, obs_count):
    stacked = jnp.concatenate([prior_ensemble, wind[None]], axis=0)
    extended = padded(stacked, (("space", 2),), SUBSTEPS)
    state = extended[:-1]
    wind_ext = extended[-1]
    for step in range(SUBSTEPS):
        edge = step + 1
        wind_mid = wind_ext[:, edge : wind_ext.shape[1] - edge]
        state = tendency(state[..., 1:-1], state[..., 2:], state[..., :-2], wind_mid)
    mem_here, latitude_lines, column_entries = state.shape
    groups = lax.axis_size("member")
    per_dev = obs_count.shape[0]
    cell_count = latitude_lines * column_entries // (groups * per_dev)
    blocks = state.reshape(mem_here, groups, per_dev, cell_count)
    arrived = lax.all_to_all(blocks, "member", split_axis=1, concat_axis=0, tiled=True)
    output_results = [
        analyze(arrived[:, 0, i], observed_cell_value[i], obs_value[i], obs_weight[i], obs_count[i])
        for i in range(per_dev)
    ]
    analysed_state = jnp.stack(output_results, axis=1)[:, None]
    returned = lax.all_to_all(analysed_state, "member", split_axis=0, concat_axis=1, tiled=True)
    return returned.reshape(mem_here, latitude_lines, column_entries)


def lane_of(shape):
    return lax.broadcasted_iota(jnp.int32, shape, 1)


def edge_kernel(column, u_ref, z_ref):
    members, rows, _ = u_ref.shape
    members = members - 1
    lane = lane_of((8, LANES))
    total = jnp.zeros((8, LANES), jnp.float32)
    for m in range(members):
        for g in range(rows // 8):
            for x, to in ((u_ref[m], 0), (u_ref[members], SUBSTEPS)):
                to = STRIP * m + 2 * SUBSTEPS * g + to
                moved = pltpu.roll(x[8 * g : 8 * g + 8], (to - column) % LANES, 1)
                total = jnp.where((lane >= to) & (lane < to + SUBSTEPS), moved, total)
    z_ref[...] = total


def unfolded(packet, rows, to):
    parts = [shifted(packet, 2 * SUBSTEPS * g - to) for g in range(rows // 8)]
    return jnp.concatenate(parts, axis=0)


def strips(block):
    lane = lane_of(block[0].shape)
    west = (lane % STRIP) < STRIP // 2
    total = jnp.zeros(block[0].shape, jnp.float32)
    for m, x in enumerate(block):
        low = pltpu.roll(x, (STRIP * m + SUBSTEPS) % LANES, 1)
        high = pltpu.roll(x, (STRIP * m + STRIP - SUBSTEPS) % LANES, 1)
        total = jnp.where((lane // STRIP) == m, jnp.where(west, low, high), total)
    return total


def stencil(x, east, west, wind3):
    rows = x.shape[0]
    row = lax.broadcasted_iota(jnp.int32, x.shape, 0)
    north = jnp.where(row == rows - 1, 0.0, pltpu.roll(x, rows - 1, 0))
    south = jnp.where(row == 0, 0.0, pltpu.roll(x, 1, 0))
    speed = wind3 + 0.075 * jnp.tanh(x)
    return 0.4 * x + 0.2 * (east + west) + 0.1 * (north + south) - speed * (east - west)


def shifted(x, by):
    return pltpu.roll(x, -by % LANES, 1) if by else x


def substep(x, wind3):
    return stencil(x, shifted(x, 1), shifted(x, -1), wind3)


def substeps(x, wind3, count):
    at = {k: shifted(x, k) for k in range(-count, count + 1)}
    winds = {k: shifted(wind3, k) for k in range(1 - count, count)}
    for reach in range(count - 1, -1, -1):
        at = {
            k: stencil(at[k], at[k + 1], at[k - 1], winds[k]) for k in range(-reach, reach + 1)
        }
    return at[0]


def pieces(x, count):
    out = []
    for _ in range(count):
        part = x.astype(jnp.bfloat16)
        out.append(part)
        x = x - part.astype(jnp.float32)
    return out


def interior_kernel(count_ref, u_ref, cell_ref, value_ref, weight_ref, f_ref, q_ref):
    mem_here, rows = u_ref.shape[0] - 1, u_ref.shape[1]
    stride = f_ref.shape[0] // mem_here
    extra = stride - rows
    wind3 = 0.3 * u_ref[mem_here]
    slots = cell_ref.shape[1]
    slot = lax.broadcasted_iota(jnp.int32, (1, slots), 1)
    weight = jnp.where(slot < count_ref[...], weight_ref[...], 0.0)
    parts = pieces(weight, 3) + pieces(weight * value_ref[...], 3)
    sub = lax.broadcasted_iota(jnp.int32, (8, slots), 0)
    lhs = jnp.zeros((8, slots), jnp.float32)
    for k, part in enumerate(parts):
        lhs = jnp.where(sub == k, part.astype(jnp.float32), lhs)
    lhs = lhs.astype(jnp.bfloat16)
    patch_rows = extra * mem_here // 2
    for q in range(patch_rows):
        cell = lax.broadcasted_iota(jnp.int32, (LANES, slots), 0) + LANES * q
        hot = jnp.where(cell == cell_ref[...], 1.0, 0.0).astype(jnp.bfloat16)
        sums = lax.dot_general(
            lhs, hot, (((1,), (1,)), ((), ())), preferred_element_type=jnp.float32
        )
        for which in range(2):
            k = which * patch_rows + q
            line = sums[3 * which : 3 * which + 1] + sums[3 * which + 1 : 3 * which + 2]
            line = line + sums[3 * which + 2 : 3 * which + 3]
            at = (k // extra) * stride + rows + k % extra
            f_ref[at : at + 1, :] = line
    q_ref[0:rows, :] = strips([u_ref[m] for m in range(mem_here)])
    q_ref[rows : 2 * rows, :] = strips([u_ref[mem_here]] * mem_here)
    for m in range(mem_here):
        x = u_ref[m]
        for _ in range(SUBSTEPS):
            x = substep(x, wind3)
        f_ref[m * stride : m * stride + rows, :] = x


def edges_kernel(q_ref, west_ref, east_ref, f_in_ref, f_ref):
    rows = q_ref.shape[0] // 2
    lane = lane_of((rows, LANES))
    place = lane % STRIP
    full = []
    for k in range(2):
        own = q_ref[k * rows : (k + 1) * rows, :]
        west = unfolded(west_ref[...], rows, -SUBSTEPS * k)
        east = unfolded(east_ref[...], rows, STRIP - SUBSTEPS - SUBSTEPS * k)
        full.append(
            jnp.where(place < SUBSTEPS, west, jnp.where(place >= STRIP - SUBSTEPS, east, own))
        )
    x, wind3 = full[0], 0.3 * full[1]
    x = substeps(x, wind3, SUBSTEPS)
    mem_here = LANES // STRIP
    stride = f_ref.shape[0] // mem_here
    for m in range(mem_here):
        low = pltpu.roll(x, (-STRIP * m - SUBSTEPS) % LANES, 1)
        high = pltpu.roll(x, (-STRIP * m - STRIP + SUBSTEPS) % LANES, 1)
        at = slice(m * stride, m * stride + rows)
        inside = f_in_ref[at, :]
        f_ref[at, :] = jnp.where(
            lane < SUBSTEPS, low, jnp.where(lane >= LANES - SUBSTEPS, high, inside)
        )
        at = slice(m * stride + rows, (m + 1) * stride)
        f_ref[at, :] = f_in_ref[at, :]


def visits(groups):
    chips = [groups - 2, *range(2, groups - 2, 2)]
    return [0, *[chip + (i + 1) % 2 for i, chip in enumerate(chips)]]


def analysis_kernel(dims, me_ref, cat_ref, sib_ref, o_ref, ob_ref, pert_ref, scaled_ref, mean_ref, done_ref, sems):
    mem_here, rows, groups = dims
    f32, bf16 = jnp.float32, jnp.bfloat16
    order = mem_here * groups
    height = rows // groups
    cells = height * LANES
    wide = order * groups
    stride = cat_ref.shape[0] * 2 // order
    per = LANES // order
    sets = range(groups // per)
    plain, turned = (((1,), (0,)), ((), ())), (((1,), (1,)), ((), ()))
    me = me_ref[0]

    def dot(x, y, how):
        return lax.dot_general(x, y, how, preferred_element_type=f32)

    def split(x):
        high = x.astype(bf16)
        return high, (x - high.astype(f32)).astype(bf16)

    for side, ref in enumerate((cat_ref, sib_ref)):
        for k in range(groups // 2):
            patch = me ^ (visits(groups)[k] ^ side)
            base = k * mem_here * stride
            lines = [
                ref[base + m * stride + rows : base + (m + 1) * stride, :] for m in range(mem_here)
            ]
            ob_ref[pl.ds(pl.multiple_of(patch * 2 * height, 2 * height), 2 * height), :] = (
                jnp.concatenate(lines, axis=0)
            )

    for p in range(groups):
        for q in range(height):
            at = pl.ds(p * height + q, order // 2, stride=stride)
            xb = jnp.concatenate([cat_ref[at, :], sib_ref[at, :]], axis=0)
            mean = jnp.sum(xb, axis=0, keepdims=True) * (1.0 / order)
            pert = xb - mean
            lanes = slice(q * LANES, (q + 1) * LANES)
            line = p * 2 * height + q
            pert_ref[p * order : (p + 1) * order, lanes] = pert
            scaled_ref[p * order : (p + 1) * order, lanes] = pert * ob_ref[line : line + 1, :]
            mean_ref[p : p + 1, lanes] = mean
    lift = []
    for q in range(height):
        weight = ob_ref[pl.ds(q, groups, stride=2 * height), :]
        lift.append(
            ob_ref[pl.ds(height + q, groups, stride=2 * height), :]
            - weight * mean_ref[:, q * LANES : (q + 1) * LANES]
        )
    lift = jnp.concatenate(lift, axis=1)
    lift = jnp.concatenate([lift] * (16 // groups), axis=0)
    lift_high, lift_low = split(lift)

    pert_high, pert_low = split(pert_ref[...])
    scaled_high, scaled_low = split(scaled_ref[...])
    own_row = lax.broadcasted_iota(jnp.int32, (order, LANES), 0)
    lane = lax.broadcasted_iota(jnp.int32, (order, LANES), 1)
    ident = jnp.where(own_row == lane % order, 1.0, 0.0)
    tail_row = lax.broadcasted_iota(jnp.int32, (16, LANES), 0)
    tail_block = lax.broadcasted_iota(jnp.int32, (16, LANES), 1) // order
    square_row = lax.broadcasted_iota(jnp.int32, (LANES, LANES), 0) // order
    square_lane = lax.broadcasted_iota(jnp.int32, (LANES, LANES), 1) // order
    diag = jnp.where(square_row == square_lane, 1.0, 0.0).astype(bf16)
    grams, prod, middle, lower, vec, inverse = [], [], [], [], [], []
    for t in sets:
        at = slice(t * LANES, (t + 1) * LANES)
        left_high = jnp.concatenate([scaled_high[at], lift_high], axis=0)
        left_low = jnp.concatenate([scaled_low[at], lift_low], axis=0)
        right = jnp.concatenate([pert_high[at], pert_low[at]], axis=0)
        out = dot(left_high, right, turned)
        full = out[:, :LANES] + out[:, LANES:] + dot(left_low, pert_high[at], turned)
        gram = (order - 1.0) * ident
        for p in range(per):
            gram = gram + jnp.where(lane // order == p, full[p * order : (p + 1) * order], 0.0)
        rhs = jnp.sum(
            jnp.where(tail_row == tail_block + per * t, full[LANES:], 0.0), axis=0, keepdims=True
        )
        grams.append(gram)
        vec.append(jnp.where(tail_row == 0, rhs, 0.0))

    def weights(x):
        high, low = (jnp.concatenate([part] * per, axis=0) * diag for part in split(x))
        return jnp.concatenate([high, high], axis=0), low

    def product(x, right):
        xh, xl = split(x)
        return dot(jnp.concatenate([xh, xl], axis=1), right[0], plain) + dot(xh, right[1], plain)

    twice = []
    for t in sets:
        twice.append(product(jnp.concatenate([grams[t], vec[t]], axis=0), weights(grams[t])))
    for t in sets:
        square = jnp.sum(grams[t] * grams[t], axis=0, keepdims=True)
        group = lane[0:1] // order
        total = jnp.zeros((1, LANES), f32)
        for p in range(per):
            mine = group == p
            total = jnp.where(mine, jnp.sum(jnp.where(mine, square, 0.0), axis=1, keepdims=True), total)
        inverse.append(1.0 / jnp.sqrt(total + 1e-06))
        first = grams[t] * inverse[t]
        middle.append(1.5 * ident - 0.5 * first)
        prod.append(1.5 * first - (0.5 * inverse[t]) * (twice[t][:order] * inverse[t]))
        vec[t] = 1.5 * vec[t] - (0.5 * inverse[t]) * twice[t][order:]
        lower.append(middle[t][0:8])
    for step in range(NS_ITERS):
        right = [weights(middle[t]) for t in sets]
        last = step == NS_ITERS - 1
        if step:
            for t in sets:
                left = ([] if last else [prod[t]]) + [vec[t][0:8], lower[t]]
                out = product(jnp.concatenate(left, axis=0), right[t])
                if not last:
                    prod[t], out = out[:order], out[order:]
                vec[t], lower[t] = out, out[8:16]
        for t in sets:
            left = [vec[t]] if last else [prod[t], vec[t]]
            out = product(jnp.concatenate(left, axis=0), right[t])
            if not last:
                prod[t], out = out[:order], out[order:]
                middle[t] = 1.5 * ident - 0.5 * prod[t]
            vec[t] = out
    pick = lax.broadcasted_iota(jnp.int32, (groups, LANES), 0)
    tall = []
    for t in sets:
        own = lower[t] * (jnp.sqrt(inverse[t]) * (order - 1.0) ** 0.5) + vec[t][0:1] * inverse[t]
        keep = pick == lax.broadcasted_iota(jnp.int32, (groups, LANES), 1) // order + per * t
        tall.append(
            jnp.concatenate(
                [jnp.where(keep, own[i : i + 1], 0.0) for i in range(mem_here)], axis=0
            )
        )

    tall_high, tall_low = split(jnp.concatenate(tall, axis=1))
    both = dot(jnp.concatenate([tall_high, tall_low], axis=0), pert_high, plain)
    count = groups * mem_here
    out = both[:count] + both[count:] + dot(tall_high, pert_low, plain)
    copies = []
    for i in range(mem_here):
        for q in range(height):
            lanes = slice(q * LANES, (q + 1) * LANES)
            done_ref[pl.ds(i * rows + q, groups, stride=height), :] = (
                out[i * groups : (i + 1) * groups, lanes] + mean_ref[:, lanes]
            )
        at = pl.ds(i * rows, rows)
        copies.append(pltpu.make_async_copy(done_ref.at[at], o_ref.at[at], sems.at[i]))
        copies[i].start()
    for copy in copies:
        copy.wait()


def kernel_call(body, *out_shapes, scratch=(), smem=(), out_space=pltpu.VMEM):
    def call(*args):
        specs = [
            pl.BlockSpec(memory_space=pltpu.SMEM if i in smem else pltpu.VMEM)
            for i in range(len(args))
        ]
        out = pl.pallas_call(
            body,
            out_shape=[jax.ShapeDtypeStruct(shape, jnp.float32) for shape in out_shapes],
            in_specs=specs,
            out_specs=[pl.BlockSpec(memory_space=out_space) for _ in out_shapes],
            scratch_shapes=list(scratch),
            compiler_params=pltpu.CompilerParams(vmem_limit_bytes=32 << 20),
        )(*args)
        return out[0] if len(out_shapes) == 1 else out

    return call


def gathered(prior_ensemble, wind, obs_value, obs_weight, observed_cell_value, obs_count):
    mem_here, rows, _ = prior_ensemble.shape
    groups = lax.axis_size("member")
    count = lax.axis_size("space")
    order = mem_here * groups
    height = rows // groups
    stride = rows + 2 * height // mem_here
    wide, cells = order * groups, height * LANES
    f32 = jnp.float32

    both = jnp.concatenate([prior_ensemble, wind[None]], axis=0)
    forward = [(i, (i + 1) % count) for i in range(count)]
    backward = [(i, (i - 1) % count) for i in range(count)]
    eastern = kernel_call(functools.partial(edge_kernel, LANES - SUBSTEPS), (8, LANES))(both)
    western = kernel_call(functools.partial(edge_kernel, 0), (8, LANES))(both)
    east = lax.ppermute(western, "space", backward)
    west = lax.ppermute(eastern, "space", forward)
    inside, near = kernel_call(interior_kernel, (mem_here * stride, LANES), (2 * rows, LANES))(
        obs_count.reshape(1, 1), both, observed_cell_value, obs_value, obs_weight
    )
    payload = kernel_call(edges_kernel, (mem_here * stride, LANES))(near, west, east, inside)

    def swap(x, k):
        return lax.ppermute(x, "member", [(i, i ^ k) for i in range(groups)])

    held = [payload] + [swap(payload, k) for k in visits(groups)[1:]]
    cat = jnp.concatenate(held, axis=0)
    first = jnp.concatenate(held[:2], axis=0)
    sibling = jnp.concatenate([swap(x, 1) for x in [first, *held[2:]]], axis=0)
    me = lax.axis_index("member").astype(jnp.int32).reshape(1)
    out = kernel_call(
        functools.partial(analysis_kernel, (mem_here, rows, groups)),
        (mem_here * rows, LANES),
        scratch=[
            pltpu.VMEM((groups * 2 * height, LANES), f32),
            pltpu.VMEM((wide, cells), f32),
            pltpu.VMEM((wide, cells), f32),
            pltpu.VMEM((groups, cells), f32),
            pltpu.VMEM((mem_here * rows, LANES), f32),
            pltpu.SemaphoreType.DMA((mem_here,)),
        ],
        smem=(0,),
        out_space=pl.ANY,
    )(me, cat, sibling)
    return out.reshape(mem_here, rows, LANES)


def local(prior_ensemble, *rest):
    mem_here, rows, columns = prior_ensemble.shape
    groups = lax.axis_size("member")
    whole_tile = 4 * mem_here * groups * rows * columns
    fits = (
        columns == LANES
        and mem_here * STRIP == LANES
        and rows % groups == 0
        and 2 * (rows // groups) % mem_here == 0
        and rows % 8 == 0
        and rows * 2 * SUBSTEPS <= 8 * STRIP
        and groups & (groups - 1) == 0
        and groups in (8, 16)
        and LANES % (mem_here * groups) == 0
        and lax.axis_size("space") % 2 == 0
        and rest[-1].shape[0] == 1
        and whole_tile <= GATHER_BYTES
    )
    return (gathered if fits else exchanged)(prior_ensemble, *rest)


def solution(mesh):
    in_specs = (
        P("member", None, "space"),
        P(None, "space"),
        P(("space", "member"), None),
        P(("space", "member"), None),
        P(("space", "member"), None),
        P(("space", "member")),
    )
    out_specs = P("member", None, "space")
    return jax.shard_map(local, mesh=mesh, in_specs=in_specs, out_specs=out_specs, check_vma=False)
```

```python
import functools

import jax
import jax.numpy as jnp
from jax import lax
from jax.experimental import pallas as pl
from jax.experimental.pallas import tpu as pltpu
from jax.sharding import PartitionSpec as P

SUBSTEPS = 4
NS_ITERS = 6
LANES = 128
STRIP = 32
GATHER_BYTES = 4 << 20


def padded(block, sides, width):
    for axis, dim in sides:
        count = lax.axis_size(axis)
        forward = [(i, i + 1) for i in range(count - 1)]
        forward.append((count - 1, 0))
        backward = [(target, source) for source, target in forward]
        low = lax.ppermute(
            lax.slice_in_dim(block, block.shape[dim] - width, None, axis=dim), axis, forward
        )
        high = lax.ppermute(lax.slice_in_dim(block, 0, width, axis=dim), axis, backward)
        block = jnp.concatenate([low, block, high], axis=dim)
    return block


def tendency(center, east, west, wind_mid):
    pads = [(0, 0)] * (center.ndim - 2) + [(1, 1), (0, 0)]
    ypad = jnp.pad(center, pads)
    north = ypad[..., 2:, :]
    south = ypad[..., :-2, :]
    speed = wind_mid + 0.25 * jnp.tanh(center)
    return (
        center
        + 0.2 * (east - 2.0 * center + west)
        + 0.1 * (north - 2.0 * center + south)
        - 0.3 * speed * (east - west)
    )


def inverse_root(gram):
    order = gram.shape[0]
    ident = jnp.eye(order, dtype=jnp.float32)
    scale = jnp.sqrt(jnp.sum(gram * gram) + 1e-06)
    upper = gram / scale
    lower = ident
    for step in range(NS_ITERS):
        middle = 1.5 * ident - 0.5 * jnp.dot(lower, upper, precision=lax.Precision.HIGHEST)
        upper = jnp.dot(upper, middle, precision=lax.Precision.HIGHEST)
        lower = jnp.dot(middle, lower, precision=lax.Precision.HIGHEST)
    return lower / jnp.sqrt(scale)


def analyze(xb, cells, value, weight, count):
    order = xb.shape[0]
    slots = cells.shape[0]
    mean = jnp.sum(xb, axis=0) / order
    pert = xb - mean
    start_gram = (order - 1.0) * jnp.eye(order, dtype=jnp.float32)
    ypert = jnp.take(pert, cells, axis=1)
    ymean = jnp.take(mean, cells)
    live = (jnp.arange(slots, dtype=jnp.int32) < count).astype(jnp.float32)
    wts = weight * live
    gram = start_gram + jnp.dot(ypert * wts, ypert.T, precision=lax.Precision.HIGHEST)
    rhs = jnp.dot(ypert, wts * (value - ymean), precision=lax.Precision.HIGHEST)
    root = inverse_root(gram)
    wbar = jnp.dot(
        root, jnp.dot(root, rhs, precision=lax.Precision.HIGHEST), precision=lax.Precision.HIGHEST
    )
    trans = jnp.sqrt(order - 1.0) * root + wbar[:, None]
    return mean + jnp.dot(trans.T, pert, precision=lax.Precision.HIGHEST)


def exchanged(prior_ensemble, wind, obs_value, obs_weight, observed_cell_value, obs_count):
    stacked = jnp.concatenate([prior_ensemble, wind[None]], axis=0)
    extended = padded(stacked, (("space", 2),), SUBSTEPS)
    state = extended[:-1]
    wind_ext = extended[-1]
    for step in range(SUBSTEPS):
        edge = step + 1
        wind_mid = wind_ext[:, edge : wind_ext.shape[1] - edge]
        state = tendency(state[..., 1:-1], state[..., 2:], state[..., :-2], wind_mid)
    mem_here, latitude_lines, column_entries = state.shape
    groups = lax.axis_size("member")
    per_dev = obs_count.shape[0]
    cell_count = latitude_lines * column_entries // (groups * per_dev)
    blocks = state.reshape(mem_here, groups, per_dev, cell_count)
    arrived = lax.all_to_all(blocks, "member", split_axis=1, concat_axis=0, tiled=True)
    output_results = [
        analyze(arrived[:, 0, i], observed_cell_value[i], obs_value[i], obs_weight[i], obs_count[i])
        for i in range(per_dev)
    ]
    analysed_state = jnp.stack(output_results, axis=1)[:, None]
    returned = lax.all_to_all(analysed_state, "member", split_axis=0, concat_axis=1, tiled=True)
    return returned.reshape(mem_here, latitude_lines, column_entries)


def lane_of(shape):
    return lax.broadcasted_iota(jnp.int32, shape, 1)


def packet(u_ref, column):
    members, rows, _ = u_ref.shape
    members = members - 1
    lane = lane_of((8, LANES))
    parts = []
    for m in range(members):
        for g in range(rows // 8):
            for x, to in ((u_ref[m], 0), (u_ref[members], SUBSTEPS)):
                to = STRIP * m + 2 * SUBSTEPS * g + to
                moved = pltpu.roll(x[8 * g : 8 * g + 8], (to - column) % LANES, 1)
                parts.append(jnp.where((lane >= to) & (lane < to + SUBSTEPS), moved, 0.0))
    while len(parts) > 1:
        parts = [sum(parts[i : i + 2]) for i in range(0, len(parts), 2)]
    return parts[0]


def packets_kernel(u_hbm, wind_hbm, *refs):
    obs_hbm, (east_ref, west_ref, u_ref), obs_ref, sems = refs[:3], refs[3:6], refs[6:9], refs[9]
    members = u_hbm.shape[0]
    pairs = [(u_hbm.at[m], u_ref.at[m]) for m in range(members)]
    pairs += [(wind_hbm, u_ref.at[members]), *zip(obs_hbm, obs_ref)]
    copies = [pltpu.make_async_copy(a, b, sems.at[i]) for i, (a, b) in enumerate(pairs)]
    for copy in copies:
        copy.start()
    for copy in copies:
        copy.wait()
    east_ref[...] = packet(u_ref, LANES - SUBSTEPS)
    west_ref[...] = packet(u_ref, 0)


def unfolded(packet, rows, to):
    parts = [shifted(packet, 2 * SUBSTEPS * g - to) for g in range(rows // 8)]
    return jnp.concatenate(parts, axis=0)


def strips(block):
    lane = lane_of(block[0].shape)
    west = (lane % STRIP) < STRIP // 2
    total = jnp.zeros(block[0].shape, jnp.float32)
    for m, x in enumerate(block):
        low = pltpu.roll(x, (STRIP * m + SUBSTEPS) % LANES, 1)
        high = pltpu.roll(x, (STRIP * m + STRIP - SUBSTEPS) % LANES, 1)
        total = jnp.where((lane // STRIP) == m, jnp.where(west, low, high), total)
    return total


def stencil(x, east, west, wind3):
    rows = x.shape[0]
    row = lax.broadcasted_iota(jnp.int32, x.shape, 0)
    north = jnp.where(row == rows - 1, 0.0, pltpu.roll(x, rows - 1, 0))
    south = jnp.where(row == 0, 0.0, pltpu.roll(x, 1, 0))
    speed = wind3 + 0.075 * jnp.tanh(x)
    return 0.4 * x + 0.2 * (east + west) + 0.1 * (north + south) - speed * (east - west)


def shifted(x, by):
    return pltpu.roll(x, -by % LANES, 1) if by else x


def substep(x, wind3):
    return stencil(x, shifted(x, 1), shifted(x, -1), wind3)


def substeps(x, wind3, count):
    at = {k: shifted(x, k) for k in range(-count, count + 1)}
    winds = {k: shifted(wind3, k) for k in range(1 - count, count)}
    for reach in range(count - 1, -1, -1):
        at = {
            k: stencil(at[k], at[k + 1], at[k - 1], winds[k]) for k in range(-reach, reach + 1)
        }
    return at[0]


def pieces(x, count):
    out = []
    for _ in range(count):
        part = x.astype(jnp.bfloat16)
        out.append(part)
        x = x - part.astype(jnp.float32)
    return out


def interior_kernel(count_ref, u_ref, cell_ref, value_ref, weight_ref, f_ref, q_ref):
    mem_here, rows = u_ref.shape[0] - 1, u_ref.shape[1]
    stride = f_ref.shape[0] // mem_here
    extra = stride - rows
    wind3 = 0.3 * u_ref[mem_here]
    slots = cell_ref.shape[1]
    slot = lax.broadcasted_iota(jnp.int32, (1, slots), 1)
    weight = jnp.where(slot < count_ref[...], weight_ref[...], 0.0)
    parts = pieces(weight, 3) + pieces(weight * value_ref[...], 3)
    sub = lax.broadcasted_iota(jnp.int32, (8, slots), 0)
    lhs = jnp.zeros((8, slots), jnp.float32)
    for k, part in enumerate(parts):
        lhs = jnp.where(sub == k, part.astype(jnp.float32), lhs)
    lhs = lhs.astype(jnp.bfloat16)
    patch_rows = extra * mem_here // 2
    for q in range(patch_rows):
        cell = lax.broadcasted_iota(jnp.int32, (LANES, slots), 0) + LANES * q
        hot = jnp.where(cell == cell_ref[...], 1.0, 0.0).astype(jnp.bfloat16)
        sums = lax.dot_general(
            lhs, hot, (((1,), (1,)), ((), ())), preferred_element_type=jnp.float32
        )
        for which in range(2):
            k = which * patch_rows + q
            line = sums[3 * which : 3 * which + 1] + sums[3 * which + 1 : 3 * which + 2]
            line = line + sums[3 * which + 2 : 3 * which + 3]
            at = (k // extra) * stride + rows + k % extra
            f_ref[at : at + 1, :] = line
    q_ref[0:rows, :] = strips([u_ref[m] for m in range(mem_here)])
    q_ref[rows : 2 * rows, :] = strips([u_ref[mem_here]] * mem_here)
    for m in range(mem_here):
        x = u_ref[m]
        for _ in range(SUBSTEPS):
            x = substep(x, wind3)
        f_ref[m * stride : m * stride + rows, :] = x


def edges_kernel(q_ref, west_ref, east_ref, f_in_ref, f_ref):
    rows = q_ref.shape[0] // 2
    lane = lane_of((rows, LANES))
    place = lane % STRIP
    full = []
    for k in range(2):
        own = q_ref[k * rows : (k + 1) * rows, :]
        west = unfolded(west_ref[...], rows, -SUBSTEPS * k)
        east = unfolded(east_ref[...], rows, STRIP - SUBSTEPS - SUBSTEPS * k)
        full.append(
            jnp.where(place < SUBSTEPS, west, jnp.where(place >= STRIP - SUBSTEPS, east, own))
        )
    x, wind3 = full[0], 0.3 * full[1]
    for _ in range(2):
        x = substeps(x, wind3, SUBSTEPS // 2)
    mem_here = LANES // STRIP
    stride = f_ref.shape[0] // mem_here
    for m in range(mem_here):
        low = pltpu.roll(x, (-STRIP * m - SUBSTEPS) % LANES, 1)
        high = pltpu.roll(x, (-STRIP * m - STRIP + SUBSTEPS) % LANES, 1)
        at = slice(m * stride, m * stride + rows)
        inside = f_in_ref[at, :]
        f_ref[at, :] = jnp.where(
            lane < SUBSTEPS, low, jnp.where(lane >= LANES - SUBSTEPS, high, inside)
        )
        at = slice(m * stride + rows, (m + 1) * stride)
        f_ref[at, :] = f_in_ref[at, :]


def visits(groups):
    chips = [groups - 2, *range(2, groups - 2, 2)]
    return [0, *[chip + (i + 1) % 2 for i, chip in enumerate(chips)]]


def analysis_kernel(dims, me_ref, cat_ref, sib_ref, o_ref, ob_ref, pert_ref, scaled_ref, mean_ref, done_ref, sems):
    mem_here, rows, groups = dims
    f32, bf16 = jnp.float32, jnp.bfloat16
    order = mem_here * groups
    height = rows // groups
    cells = height * LANES
    wide = order * groups
    stride = cat_ref.shape[0] * 2 // order
    per = LANES // order
    sets = range(groups // per)
    plain, turned = (((1,), (0,)), ((), ())), (((1,), (1,)), ((), ()))
    me = me_ref[0]

    def dot(x, y, how):
        return lax.dot_general(x, y, how, preferred_element_type=f32)

    def split(x):
        high = x.astype(bf16)
        return high, (x - high.astype(f32)).astype(bf16)

    for side, ref in enumerate((cat_ref, sib_ref)):
        for k in range(groups // 2):
            patch = me ^ (visits(groups)[k] ^ side)
            base = k * mem_here * stride
            lines = [
                ref[base + m * stride + rows : base + (m + 1) * stride, :] for m in range(mem_here)
            ]
            ob_ref[pl.ds(pl.multiple_of(patch * 2 * height, 2 * height), 2 * height), :] = (
                jnp.concatenate(lines, axis=0)
            )

    for p in range(groups):
        for q in range(height):
            at = pl.ds(p * height + q, order // 2, stride=stride)
            xb = jnp.concatenate([cat_ref[at, :], sib_ref[at, :]], axis=0)
            mean = jnp.sum(xb, axis=0, keepdims=True) * (1.0 / order)
            pert = xb - mean
            lanes = slice(q * LANES, (q + 1) * LANES)
            line = p * 2 * height + q
            pert_ref[p * order : (p + 1) * order, lanes] = pert
            scaled_ref[p * order : (p + 1) * order, lanes] = pert * ob_ref[line : line + 1, :]
            mean_ref[p : p + 1, lanes] = mean
    lift = []
    for q in range(height):
        weight = ob_ref[pl.ds(q, groups, stride=2 * height), :]
        lift.append(
            ob_ref[pl.ds(height + q, groups, stride=2 * height), :]
            - weight * mean_ref[:, q * LANES : (q + 1) * LANES]
        )
    lift = jnp.concatenate(lift, axis=1)
    lift = jnp.concatenate([lift] * (16 // groups), axis=0)
    lift_high, lift_low = split(lift)

    pert_high, pert_low = split(pert_ref[...])
    scaled_high, scaled_low = split(scaled_ref[...])
    own_row = lax.broadcasted_iota(jnp.int32, (order, LANES), 0)
    lane = lax.broadcasted_iota(jnp.int32, (order, LANES), 1)
    ident = jnp.where(own_row == lane % order, 1.0, 0.0)
    tail_row = lax.broadcasted_iota(jnp.int32, (16, LANES), 0)
    tail_block = lax.broadcasted_iota(jnp.int32, (16, LANES), 1) // order
    square_row = lax.broadcasted_iota(jnp.int32, (LANES, LANES), 0) // order
    square_lane = lax.broadcasted_iota(jnp.int32, (LANES, LANES), 1) // order
    diag = jnp.where(square_row == square_lane, 1.0, 0.0).astype(bf16)
    grams, prod, middle, lower, vec, inverse = [], [], [], [], [], []
    for t in sets:
        at = slice(t * LANES, (t + 1) * LANES)
        left_high = jnp.concatenate([scaled_high[at], lift_high], axis=0)
        left_low = jnp.concatenate([scaled_low[at], lift_low], axis=0)
        right = jnp.concatenate([pert_high[at], pert_low[at]], axis=0)
        out = dot(left_high, right, turned)
        full = out[:, :LANES] + out[:, LANES:] + dot(left_low, pert_high[at], turned)
        gram = (order - 1.0) * ident
        for p in range(per):
            gram = gram + jnp.where(lane // order == p, full[p * order : (p + 1) * order], 0.0)
        rhs = jnp.sum(
            jnp.where(tail_row == tail_block + per * t, full[LANES:], 0.0), axis=0, keepdims=True
        )
        grams.append(gram)
        vec.append(jnp.where(tail_row == 0, rhs, 0.0))

    def weights(x):
        high, low = (jnp.concatenate([part] * per, axis=0) * diag for part in split(x))
        return jnp.concatenate([high, high], axis=0), low

    def product(x, right):
        xh, xl = split(x)
        return dot(jnp.concatenate([xh, xl], axis=1), right[0], plain) + dot(xh, right[1], plain)

    twice = []
    for t in sets:
        twice.append(product(jnp.concatenate([grams[t], vec[t]], axis=0), weights(grams[t])))
    for t in sets:
        square = jnp.sum(grams[t] * grams[t], axis=0, keepdims=True)
        group = lane[0:1] // order
        total = jnp.zeros((1, LANES), f32)
        for p in range(per):
            mine = group == p
            total = jnp.where(mine, jnp.sum(jnp.where(mine, square, 0.0), axis=1, keepdims=True), total)
        inverse.append(1.0 / jnp.sqrt(total + 1e-06))
        first = grams[t] * inverse[t]
        middle.append(1.5 * ident - 0.5 * first)
        prod.append(1.5 * first - (0.5 * inverse[t]) * (twice[t][:order] * inverse[t]))
        vec[t] = 1.5 * vec[t] - (0.5 * inverse[t]) * twice[t][order:]
        lower.append(middle[t][0:8])
    for step in range(NS_ITERS):
        right = [weights(middle[t]) for t in sets]
        last = step == NS_ITERS - 1
        if step:
            for t in sets:
                left = ([] if last else [prod[t]]) + [vec[t][0:8], lower[t]]
                out = product(jnp.concatenate(left, axis=0), right[t])
                if not last:
                    prod[t], out = out[:order], out[order:]
                vec[t], lower[t] = out, out[8:16]
        for t in sets:
            left = [vec[t]] if last else [prod[t], vec[t]]
            out = product(jnp.concatenate(left, axis=0), right[t])
            if not last:
                prod[t], out = out[:order], out[order:]
                middle[t] = 1.5 * ident - 0.5 * prod[t]
            vec[t] = out
    pick = lax.broadcasted_iota(jnp.int32, (groups, LANES), 0)
    tall = []
    for t in sets:
        own = lower[t] * (jnp.sqrt(inverse[t]) * (order - 1.0) ** 0.5) + vec[t][0:1] * inverse[t]
        keep = pick == lax.broadcasted_iota(jnp.int32, (groups, LANES), 1) // order + per * t
        tall.append(
            jnp.concatenate(
                [jnp.where(keep, own[i : i + 1], 0.0) for i in range(mem_here)], axis=0
            )
        )

    tall_high, tall_low = split(jnp.concatenate(tall, axis=1))
    both = dot(jnp.concatenate([tall_high, tall_low], axis=0), pert_high, plain)
    count = groups * mem_here
    out = both[:count] + both[count:] + dot(tall_high, pert_low, plain)
    copies = []
    for i in range(mem_here):
        for q in range(height):
            lanes = slice(q * LANES, (q + 1) * LANES)
            done_ref[pl.ds(i * rows + q, groups, stride=height), :] = (
                out[i * groups : (i + 1) * groups, lanes] + mean_ref[:, lanes]
            )
        at = pl.ds(i * rows, rows)
        copies.append(pltpu.make_async_copy(done_ref.at[at], o_ref.at[at], sems.at[i]))
        copies[i].start()
    for copy in copies:
        copy.wait()


def typed(shape):
    shape, dtype = shape if isinstance(shape[0], tuple) else (shape, jnp.float32)
    return jax.ShapeDtypeStruct(shape, dtype)


def kernel_call(body, *out_shapes, scratch=(), smem=(), far=(), out_space=pltpu.VMEM):
    def call(*args):
        args = [
            pltpu.with_memory_space_constraint(x, pltpu.HBM) if i in far else x
            for i, x in enumerate(args)
        ]
        specs = [
            pl.BlockSpec(
                memory_space=pltpu.SMEM if i in smem else pl.ANY if i in far else pltpu.VMEM
            )
            for i in range(len(args))
        ]
        out = pl.pallas_call(
            body,
            out_shape=[typed(shape) for shape in out_shapes],
            in_specs=specs,
            out_specs=[pl.BlockSpec(memory_space=out_space) for _ in out_shapes],
            scratch_shapes=list(scratch),
            compiler_params=pltpu.CompilerParams(vmem_limit_bytes=32 << 20),
        )(*args)
        return out[0] if len(out_shapes) == 1 else out

    return call


def gathered(prior_ensemble, wind, obs_value, obs_weight, observed_cell_value, obs_count):
    mem_here, rows, _ = prior_ensemble.shape
    groups = lax.axis_size("member")
    count = lax.axis_size("space")
    order = mem_here * groups
    height = rows // groups
    stride = rows + 2 * height // mem_here
    wide, cells = order * groups, height * LANES
    f32 = jnp.float32

    forward = [(i, (i + 1) % count) for i in range(count)]
    backward = [(i, (i - 1) % count) for i in range(count)]
    observed = (observed_cell_value, obs_value, obs_weight)
    eastern, western, both, *observed = kernel_call(
        packets_kernel,
        (8, LANES),
        (8, LANES),
        (mem_here + 1, rows, LANES),
        *[(x.shape, x.dtype) for x in observed],
        scratch=[pltpu.SemaphoreType.DMA((mem_here + 1 + len(observed),))],
        far=range(5),
    )(prior_ensemble, wind, *observed)
    east = lax.ppermute(western, "space", backward)
    west = lax.ppermute(eastern, "space", forward)
    inside, near = kernel_call(interior_kernel, (mem_here * stride, LANES), (2 * rows, LANES))(
        obs_count.reshape(1, 1), both, *observed
    )
    payload = kernel_call(edges_kernel, (mem_here * stride, LANES))(near, west, east, inside)

    def swap(x, k):
        return lax.ppermute(x, "member", [(i, i ^ k) for i in range(groups)])

    held = [payload] + [swap(payload, k) for k in visits(groups)[1:]]
    cat = jnp.concatenate(held, axis=0)
    first = jnp.concatenate(held[:2], axis=0)
    sibling = jnp.concatenate([swap(x, 1) for x in [first, *held[2:]]], axis=0)
    me = lax.axis_index("member").astype(jnp.int32).reshape(1)
    out = kernel_call(
        functools.partial(analysis_kernel, (mem_here, rows, groups)),
        (mem_here * rows, LANES),
        scratch=[
            pltpu.VMEM((groups * 2 * height, LANES), f32),
            pltpu.VMEM((wide, cells), f32),
            pltpu.VMEM((wide, cells), f32),
            pltpu.VMEM((groups, cells), f32),
            pltpu.VMEM((mem_here * rows, LANES), f32),
            pltpu.SemaphoreType.DMA((mem_here,)),
        ],
        smem=(0,),
        out_space=pl.ANY,
    )(me, cat, sibling)
    return out.reshape(mem_here, rows, LANES)


def local(prior_ensemble, *rest):
    mem_here, rows, columns = prior_ensemble.shape
    groups = lax.axis_size("member")
    whole_tile = 4 * mem_here * groups * rows * columns
    fits = (
        columns == LANES
        and mem_here * STRIP == LANES
        and rows % groups == 0
        and 2 * (rows // groups) % mem_here == 0
        and rows % 8 == 0
        and rows * 2 * SUBSTEPS <= 8 * STRIP
        and groups & (groups - 1) == 0
        and groups in (8, 16)
        and LANES % (mem_here * groups) == 0
        and lax.axis_size("space") % 2 == 0
        and rest[-1].shape[0] == 1
        and whole_tile <= GATHER_BYTES
    )
    return (gathered if fits else exchanged)(prior_ensemble, *rest)


def solution(mesh):
    in_specs = (
        P("member", None, "space"),
        P(None, "space"),
        P(("space", "member"), None),
        P(("space", "member"), None),
        P(("space", "member"), None),
        P(("space", "member")),
    )
    out_specs = P("member", None, "space")
    return jax.shard_map(local, mesh=mesh, in_specs=in_specs, out_specs=out_specs, check_vma=False)
```

```python
import functools

import jax
import jax.numpy as jnp
from jax import lax
from jax.experimental import pallas as pl
from jax.experimental.pallas import tpu as pltpu
from jax.sharding import PartitionSpec as P

SUBSTEPS = 4
NS_ITERS = 6
LANES = 128
STRIP = 32
GATHER_BYTES = 4 << 20


def padded(block, sides, width):
    for axis, dim in sides:
        count = lax.axis_size(axis)
        forward = [(i, i + 1) for i in range(count - 1)]
        forward.append((count - 1, 0))
        backward = [(target, source) for source, target in forward]
        low = lax.ppermute(
            lax.slice_in_dim(block, block.shape[dim] - width, None, axis=dim), axis, forward
        )
        high = lax.ppermute(lax.slice_in_dim(block, 0, width, axis=dim), axis, backward)
        block = jnp.concatenate([low, block, high], axis=dim)
    return block


def tendency(center, east, west, wind_mid):
    pads = [(0, 0)] * (center.ndim - 2) + [(1, 1), (0, 0)]
    ypad = jnp.pad(center, pads)
    north = ypad[..., 2:, :]
    south = ypad[..., :-2, :]
    speed = wind_mid + 0.25 * jnp.tanh(center)
    return (
        center
        + 0.2 * (east - 2.0 * center + west)
        + 0.1 * (north - 2.0 * center + south)
        - 0.3 * speed * (east - west)
    )


def inverse_root(gram):
    order = gram.shape[0]
    ident = jnp.eye(order, dtype=jnp.float32)
    scale = jnp.sqrt(jnp.sum(gram * gram) + 1e-06)
    upper = gram / scale
    lower = ident
    for step in range(NS_ITERS):
        middle = 1.5 * ident - 0.5 * jnp.dot(lower, upper, precision=lax.Precision.HIGHEST)
        upper = jnp.dot(upper, middle, precision=lax.Precision.HIGHEST)
        lower = jnp.dot(middle, lower, precision=lax.Precision.HIGHEST)
    return lower / jnp.sqrt(scale)


def analyze(xb, cells, value, weight, count):
    order = xb.shape[0]
    slots = cells.shape[0]
    mean = jnp.sum(xb, axis=0) / order
    pert = xb - mean
    start_gram = (order - 1.0) * jnp.eye(order, dtype=jnp.float32)
    ypert = jnp.take(pert, cells, axis=1)
    ymean = jnp.take(mean, cells)
    live = (jnp.arange(slots, dtype=jnp.int32) < count).astype(jnp.float32)
    wts = weight * live
    gram = start_gram + jnp.dot(ypert * wts, ypert.T, precision=lax.Precision.HIGHEST)
    rhs = jnp.dot(ypert, wts * (value - ymean), precision=lax.Precision.HIGHEST)
    root = inverse_root(gram)
    wbar = jnp.dot(
        root, jnp.dot(root, rhs, precision=lax.Precision.HIGHEST), precision=lax.Precision.HIGHEST
    )
    trans = jnp.sqrt(order - 1.0) * root + wbar[:, None]
    return mean + jnp.dot(trans.T, pert, precision=lax.Precision.HIGHEST)


def exchanged(prior_ensemble, wind, obs_value, obs_weight, observed_cell_value, obs_count):
    stacked = jnp.concatenate([prior_ensemble, wind[None]], axis=0)
    extended = padded(stacked, (("space", 2),), SUBSTEPS)
    state = extended[:-1]
    wind_ext = extended[-1]
    for step in range(SUBSTEPS):
        edge = step + 1
        wind_mid = wind_ext[:, edge : wind_ext.shape[1] - edge]
        state = tendency(state[..., 1:-1], state[..., 2:], state[..., :-2], wind_mid)
    mem_here, latitude_lines, column_entries = state.shape
    groups = lax.axis_size("member")
    per_dev = obs_count.shape[0]
    cell_count = latitude_lines * column_entries // (groups * per_dev)
    blocks = state.reshape(mem_here, groups, per_dev, cell_count)
    arrived = lax.all_to_all(blocks, "member", split_axis=1, concat_axis=0, tiled=True)
    output_results = [
        analyze(arrived[:, 0, i], observed_cell_value[i], obs_value[i], obs_weight[i], obs_count[i])
        for i in range(per_dev)
    ]
    analysed_state = jnp.stack(output_results, axis=1)[:, None]
    returned = lax.all_to_all(analysed_state, "member", split_axis=0, concat_axis=1, tiled=True)
    return returned.reshape(mem_here, latitude_lines, column_entries)


def lane_of(shape):
    return lax.broadcasted_iota(jnp.int32, shape, 1)


def packet(u_ref, moved_wind, column):
    members, rows, _ = u_ref.shape
    lane = lane_of((8, LANES))
    beside = (lane - column) % LANES // SUBSTEPS == 1
    parts = []
    for m in range(members - 1):
        for g in range(rows // 8):
            at, to = slice(8 * g, 8 * g + 8), STRIP * m + 2 * SUBSTEPS * g
            both = jnp.where(beside, moved_wind[at], u_ref[m, at, :])
            moved = pltpu.roll(both, (to - column) % LANES, 1)
            parts.append(jnp.where(lane // (2 * SUBSTEPS) == to // (2 * SUBSTEPS), moved, 0.0))
    while len(parts) > 1:
        parts = [sum(parts[i : i + 2]) for i in range(0, len(parts), 2)]
    return parts[0]


def packets_kernel(u_hbm, wind_hbm, *refs):
    obs_hbm, (east_ref, west_ref, u_ref), obs_ref, sems = refs[:3], refs[3:6], refs[6:9], refs[9]
    members = u_hbm.shape[0]
    pairs = [(wind_hbm, u_ref.at[members])]
    pairs += [(u_hbm.at[m], u_ref.at[m]) for m in range(members)]
    pairs += [*zip(obs_hbm, obs_ref)]
    copies = [pltpu.make_async_copy(a, b, sems.at[i]) for i, (a, b) in enumerate(pairs)]
    for copy in copies:
        copy.start()
    copies[0].wait()
    moved_wind = pltpu.roll(u_ref[members], SUBSTEPS, 1)
    for copy in copies[1 : 1 + members]:
        copy.wait()
    east_ref[...] = packet(u_ref, moved_wind, LANES - SUBSTEPS)
    west_ref[...] = packet(u_ref, moved_wind, 0)
    for copy in copies[1 + members :]:
        copy.wait()


def unfolded(packet, rows, to):
    parts = [shifted(packet, 2 * SUBSTEPS * g - to) for g in range(rows // 8)]
    return jnp.concatenate(parts, axis=0)


def strips(block):
    lane = lane_of(block[0].shape)
    west = (lane % STRIP) < STRIP // 2
    parts = []
    for m, x in enumerate(block):
        low = pltpu.roll(x, (STRIP * m + SUBSTEPS) % LANES, 1)
        high = pltpu.roll(x, (STRIP * m + STRIP - SUBSTEPS) % LANES, 1)
        parts.append(jnp.where((lane // STRIP) == m, jnp.where(west, low, high), 0.0))
    return sum(parts)


def stencil(x, east, west, wind3):
    rows = x.shape[0]
    row = lax.broadcasted_iota(jnp.int32, x.shape, 0)
    north = jnp.where(row == rows - 1, 0.0, pltpu.roll(x, rows - 1, 0))
    south = jnp.where(row == 0, 0.0, pltpu.roll(x, 1, 0))
    speed = wind3 + 0.075 * jnp.tanh(x)
    return 0.4 * x + 0.2 * (east + west) + 0.1 * (north + south) - speed * (east - west)


def shifted(x, by):
    return pltpu.roll(x, -by % LANES, 1) if by else x


def substep(x, wind3):
    return stencil(x, shifted(x, 1), shifted(x, -1), wind3)


def substeps(x, wind3, count):
    at = {k: shifted(x, k) for k in range(-count, count + 1)}
    winds = {k: shifted(wind3, k) for k in range(1 - count, count)}
    for reach in range(count - 1, -1, -1):
        at = {
            k: stencil(at[k], at[k + 1], at[k - 1], winds[k]) for k in range(-reach, reach + 1)
        }
    return at[0]


def pieces(x, count):
    out = []
    for _ in range(count):
        part = x.astype(jnp.bfloat16)
        out.append(part)
        x = x - part.astype(jnp.float32)
    return out


def interior_kernel(count_ref, u_ref, cell_ref, value_ref, weight_ref, f_ref, q_ref):
    mem_here, rows = u_ref.shape[0] - 1, u_ref.shape[1]
    stride = f_ref.shape[0] // mem_here
    extra = stride - rows
    wind3 = 0.3 * u_ref[mem_here]
    slots = cell_ref.shape[1]
    slot = lax.broadcasted_iota(jnp.int32, (1, slots), 1)
    weight = jnp.where(slot < count_ref[0], weight_ref[...], 0.0)
    parts = pieces(weight, 3) + pieces(weight * value_ref[...], 3)
    sub = lax.broadcasted_iota(jnp.int32, (8, slots), 0)
    lhs = jnp.zeros((8, slots), jnp.float32)
    for k, part in enumerate(parts):
        lhs = jnp.where(sub == k, part.astype(jnp.float32), lhs)
    lhs = lhs.astype(jnp.bfloat16)
    patch_rows = extra * mem_here // 2
    for q in range(patch_rows):
        cell = lax.broadcasted_iota(jnp.int32, (LANES, slots), 0) + LANES * q
        hot = jnp.where(cell == cell_ref[...], 1.0, 0.0).astype(jnp.bfloat16)
        sums = lax.dot_general(
            lhs, hot, (((1,), (1,)), ((), ())), preferred_element_type=jnp.float32
        )
        for which in range(2):
            k = which * patch_rows + q
            line = sums[3 * which : 3 * which + 1] + sums[3 * which + 1 : 3 * which + 2]
            line = line + sums[3 * which + 2 : 3 * which + 3]
            at = (k // extra) * stride + rows + k % extra
            f_ref[at : at + 1, :] = line
    q_ref[0:rows, :] = strips([u_ref[m] for m in range(mem_here)])
    q_ref[rows : 2 * rows, :] = strips([u_ref[mem_here]] * mem_here)
    state = [u_ref[m] for m in range(mem_here)]
    for _ in range(SUBSTEPS):
        state = [substep(x, wind3) for x in state]
    for m, x in enumerate(state):
        f_ref[m * stride : m * stride + rows, :] = x


def edges_kernel(q_ref, west_ref, east_ref, f_in_ref, f_ref):
    rows = q_ref.shape[0] // 2
    lane = lane_of((rows, LANES))
    place = lane % STRIP
    full = []
    for k in range(2):
        own = q_ref[k * rows : (k + 1) * rows, :]
        west = unfolded(west_ref[...], rows, -SUBSTEPS * k)
        east = unfolded(east_ref[...], rows, STRIP - SUBSTEPS - SUBSTEPS * k)
        full.append(
            jnp.where(place < SUBSTEPS, west, jnp.where(place >= STRIP - SUBSTEPS, east, own))
        )
    x, wind3 = full[0], 0.3 * full[1]
    for _ in range(2):
        x = substeps(x, wind3, SUBSTEPS // 2)
    mem_here = LANES // STRIP
    stride = f_ref.shape[0] // mem_here
    for m in range(mem_here):
        low = pltpu.roll(x, (-STRIP * m - SUBSTEPS) % LANES, 1)
        high = pltpu.roll(x, (-STRIP * m - STRIP + SUBSTEPS) % LANES, 1)
        at = slice(m * stride, m * stride + rows)
        inside = f_in_ref[at, :]
        f_ref[at, :] = jnp.where(
            lane < SUBSTEPS, low, jnp.where(lane >= LANES - SUBSTEPS, high, inside)
        )
        at = slice(m * stride + rows, (m + 1) * stride)
        f_ref[at, :] = f_in_ref[at, :]


def visits(groups):
    chips = [groups - 2, *range(2, groups - 2, 2)]
    return [0, *[chip + (i + 1) % 2 for i, chip in enumerate(chips)]]


def analysis_kernel(dims, me_ref, cat_ref, sib_ref, o_ref, ob_ref, pert_ref, scaled_ref, mean_ref, done_ref, sems):
    mem_here, rows, groups = dims
    f32, bf16 = jnp.float32, jnp.bfloat16
    order = mem_here * groups
    height = rows // groups
    cells = height * LANES
    wide = order * groups
    stride = cat_ref.shape[0] * 2 // order
    per = LANES // order
    sets = range(groups // per)
    plain, turned = (((1,), (0,)), ((), ())), (((1,), (1,)), ((), ()))
    me = me_ref[0]

    def dot(x, y, how):
        return lax.dot_general(x, y, how, preferred_element_type=f32)

    def split(x):
        high = x.astype(bf16)
        return high, (x - high.astype(f32)).astype(bf16)

    for side, ref in enumerate((cat_ref, sib_ref)):
        for k in range(groups // 2):
            patch = me ^ (visits(groups)[k] ^ side)
            base = k * mem_here * stride
            lines = [
                ref[base + m * stride + rows : base + (m + 1) * stride, :] for m in range(mem_here)
            ]
            ob_ref[pl.ds(pl.multiple_of(patch * 2 * height, 2 * height), 2 * height), :] = (
                jnp.concatenate(lines, axis=0)
            )

    for p in range(groups):
        for q in range(height):
            at = pl.ds(p * height + q, order // 2, stride=stride)
            xb = jnp.concatenate([cat_ref[at, :], sib_ref[at, :]], axis=0)
            mean = jnp.sum(xb, axis=0, keepdims=True) * (1.0 / order)
            pert = xb - mean
            lanes = slice(q * LANES, (q + 1) * LANES)
            line = p * 2 * height + q
            pert_ref[p * order : (p + 1) * order, lanes] = pert
            scaled_ref[p * order : (p + 1) * order, lanes] = pert * ob_ref[line : line + 1, :]
            mean_ref[p : p + 1, lanes] = mean
    lift = []
    for q in range(height):
        weight = ob_ref[pl.ds(q, groups, stride=2 * height), :]
        lift.append(
            ob_ref[pl.ds(height + q, groups, stride=2 * height), :]
            - weight * mean_ref[:, q * LANES : (q + 1) * LANES]
        )
    lift = jnp.concatenate(lift, axis=1)
    lift = jnp.concatenate([lift] * (16 // groups), axis=0)
    lift_high, lift_low = split(lift)

    pert_high, pert_low = split(pert_ref[...])
    scaled_high, scaled_low = split(scaled_ref[...])
    own_row = lax.broadcasted_iota(jnp.int32, (order, LANES), 0)
    lane = lax.broadcasted_iota(jnp.int32, (order, LANES), 1)
    ident = jnp.where(own_row == lane % order, 1.0, 0.0)
    tail_row = lax.broadcasted_iota(jnp.int32, (16, LANES), 0)
    tail_block = lax.broadcasted_iota(jnp.int32, (16, LANES), 1) // order
    square_row = lax.broadcasted_iota(jnp.int32, (LANES, LANES), 0) // order
    square_lane = lax.broadcasted_iota(jnp.int32, (LANES, LANES), 1) // order
    diag = jnp.where(square_row == square_lane, 1.0, 0.0).astype(bf16)
    grams, prod, middle, lower, vec, inverse = [], [], [], [], [], []
    for t in sets:
        at = slice(t * LANES, (t + 1) * LANES)
        left_high = jnp.concatenate([scaled_high[at], lift_high], axis=0)
        left_low = jnp.concatenate([scaled_low[at], lift_low], axis=0)
        right = jnp.concatenate([pert_high[at], pert_low[at]], axis=0)
        out = dot(left_high, right, turned)
        full = out[:, :LANES] + out[:, LANES:] + dot(left_low, pert_high[at], turned)
        gram = (order - 1.0) * ident
        for p in range(per):
            gram = gram + jnp.where(lane // order == p, full[p * order : (p + 1) * order], 0.0)
        rhs = jnp.sum(
            jnp.where(tail_row == tail_block + per * t, full[LANES:], 0.0), axis=0, keepdims=True
        )
        grams.append(gram)
        vec.append(jnp.where(tail_row == 0, rhs, 0.0))

    def weights(x):
        high, low = (jnp.concatenate([part] * per, axis=0) * diag for part in split(x))
        return jnp.concatenate([high, high], axis=0), low

    def product(x, right):
        xh, xl = split(x)
        return dot(jnp.concatenate([xh, xl], axis=1), right[0], plain) + dot(xh, right[1], plain)

    twice = []
    for t in sets:
        twice.append(product(jnp.concatenate([grams[t], vec[t]], axis=0), weights(grams[t])))
    for t in sets:
        square = jnp.sum(grams[t] * grams[t], axis=0, keepdims=True)
        group = lane[0:1] // order
        total = jnp.zeros((1, LANES), f32)
        for p in range(per):
            mine = group == p
            total = jnp.where(mine, jnp.sum(jnp.where(mine, square, 0.0), axis=1, keepdims=True), total)
        inverse.append(1.0 / jnp.sqrt(total + 1e-06))
        first = grams[t] * inverse[t]
        middle.append(1.5 * ident - 0.5 * first)
        prod.append(1.5 * first - (0.5 * inverse[t]) * (twice[t][:order] * inverse[t]))
        vec[t] = 1.5 * vec[t] - (0.5 * inverse[t]) * twice[t][order:]
        lower.append(middle[t][0:8])
    for step in range(NS_ITERS):
        right = [weights(middle[t]) for t in sets]
        last = step == NS_ITERS - 1
        if step:
            for t in sets:
                left = ([] if last else [prod[t]]) + [vec[t][0:8], lower[t]]
                out = product(jnp.concatenate(left, axis=0), right[t])
                if not last:
                    prod[t], out = out[:order], out[order:]
                vec[t], lower[t] = out, out[8:16]
        for t in sets:
            left = [vec[t]] if last else [prod[t], vec[t]]
            out = product(jnp.concatenate(left, axis=0), right[t])
            if not last:
                prod[t], out = out[:order], out[order:]
                middle[t] = 1.5 * ident - 0.5 * prod[t]
            vec[t] = out
    pick = lax.broadcasted_iota(jnp.int32, (groups, LANES), 0)
    tall = []
    for t in sets:
        own = lower[t] * (jnp.sqrt(inverse[t]) * (order - 1.0) ** 0.5) + vec[t][0:1] * inverse[t]
        keep = pick == lax.broadcasted_iota(jnp.int32, (groups, LANES), 1) // order + per * t
        tall.append(
            jnp.concatenate(
                [jnp.where(keep, own[i : i + 1], 0.0) for i in range(mem_here)], axis=0
            )
        )

    tall_high, tall_low = split(jnp.concatenate(tall, axis=1))
    both = dot(jnp.concatenate([tall_high, tall_low], axis=0), pert_high, plain)
    count = groups * mem_here
    out = both[:count] + both[count:] + dot(tall_high, pert_low, plain)
    copies = []
    for i in range(mem_here):
        for q in range(height):
            lanes = slice(q * LANES, (q + 1) * LANES)
            done_ref[pl.ds(i * rows + q, groups, stride=height), :] = (
                out[i * groups : (i + 1) * groups, lanes] + mean_ref[:, lanes]
            )
        at = pl.ds(i * rows, rows)
        copies.append(pltpu.make_async_copy(done_ref.at[at], o_ref.at[at], sems.at[i]))
        copies[i].start()
    for copy in copies:
        copy.wait()


def typed(shape):
    shape, dtype = shape if isinstance(shape[0], tuple) else (shape, jnp.float32)
    return jax.ShapeDtypeStruct(shape, dtype)


def kernel_call(body, *out_shapes, scratch=(), smem=(), far=(), out_space=pltpu.VMEM):
    def call(*args):
        args = [
            pltpu.with_memory_space_constraint(x, pltpu.HBM) if i in far else x
            for i, x in enumerate(args)
        ]
        specs = [
            pl.BlockSpec(
                memory_space=pltpu.SMEM if i in smem else pl.ANY if i in far else pltpu.VMEM
            )
            for i in range(len(args))
        ]
        out = pl.pallas_call(
            body,
            out_shape=[typed(shape) for shape in out_shapes],
            in_specs=specs,
            out_specs=[pl.BlockSpec(memory_space=out_space) for _ in out_shapes],
            scratch_shapes=list(scratch),
            compiler_params=pltpu.CompilerParams(vmem_limit_bytes=32 << 20),
        )(*args)
        return out[0] if len(out_shapes) == 1 else out

    return call


def gathered(prior_ensemble, wind, obs_value, obs_weight, observed_cell_value, obs_count):
    mem_here, rows, _ = prior_ensemble.shape
    groups = lax.axis_size("member")
    count = lax.axis_size("space")
    order = mem_here * groups
    height = rows // groups
    stride = rows + 2 * height // mem_here
    wide, cells = order * groups, height * LANES
    f32 = jnp.float32

    forward = [(i, (i + 1) % count) for i in range(count)]
    backward = [(i, (i - 1) % count) for i in range(count)]
    observed = (observed_cell_value, obs_value, obs_weight)
    eastern, western, both, *observed = kernel_call(
        packets_kernel,
        (8, LANES),
        (8, LANES),
        (mem_here + 1, rows, LANES),
        *[(x.shape, x.dtype) for x in observed],
        scratch=[pltpu.SemaphoreType.DMA((mem_here + 1 + len(observed),))],
        far=range(5),
    )(prior_ensemble, wind, *observed)
    east = lax.ppermute(western, "space", backward)
    west = lax.ppermute(eastern, "space", forward)
    inside, near = kernel_call(
        interior_kernel, (mem_here * stride, LANES), (2 * rows, LANES), smem=(0,)
    )(obs_count, both, *observed)
    payload = kernel_call(edges_kernel, (mem_here * stride, LANES))(near, west, east, inside)

    def swap(x, k):
        return lax.ppermute(x, "member", [(i, i ^ k) for i in range(groups)])

    held = [payload] + [swap(payload, k) for k in visits(groups)[1:]]
    cat = jnp.concatenate(held, axis=0)
    first = jnp.concatenate(held[:2], axis=0)
    sibling = jnp.concatenate([swap(x, 1) for x in [first, *held[2:]]], axis=0)
    me = lax.axis_index("member").astype(jnp.int32).reshape(1)
    out = kernel_call(
        functools.partial(analysis_kernel, (mem_here, rows, groups)),
        (mem_here * rows, LANES),
        scratch=[
            pltpu.VMEM((groups * 2 * height, LANES), f32),
            pltpu.VMEM((wide, cells), f32),
            pltpu.VMEM((wide, cells), f32),
            pltpu.VMEM((groups, cells), f32),
            pltpu.VMEM((mem_here * rows, LANES), f32),
            pltpu.SemaphoreType.DMA((mem_here,)),
        ],
        smem=(0,),
        out_space=pl.ANY,
    )(me, cat, sibling)
    return out.reshape(mem_here, rows, LANES)


def local(prior_ensemble, *rest):
    mem_here, rows, columns = prior_ensemble.shape
    groups = lax.axis_size("member")
    whole_tile = 4 * mem_here * groups * rows * columns
    fits = (
        columns == LANES
        and mem_here * STRIP == LANES
        and rows % groups == 0
        and 2 * (rows // groups) % mem_here == 0
        and rows % 8 == 0
        and rows * 2 * SUBSTEPS <= 8 * STRIP
        and groups & (groups - 1) == 0
        and groups in (8, 16)
        and LANES % (mem_here * groups) == 0
        and lax.axis_size("space") % 2 == 0
        and rest[-1].shape[0] == 1
        and whole_tile <= GATHER_BYTES
    )
    return (gathered if fits else exchanged)(prior_ensemble, *rest)


def solution(mesh):
    in_specs = (
        P("member", None, "space"),
        P(None, "space"),
        P(("space", "member"), None),
        P(("space", "member"), None),
        P(("space", "member"), None),
        P(("space", "member")),
    )
    out_specs = P("member", None, "space")
    return jax.shard_map(local, mesh=mesh, in_specs=in_specs, out_specs=out_specs, check_vma=False)
```

```python
import functools

import jax
import jax.numpy as jnp
from jax import lax
from jax.experimental import pallas as pl
from jax.experimental.pallas import tpu as pltpu
from jax.sharding import PartitionSpec as P

SUBSTEPS = 4
NS_ITERS = 6
LANES = 128
STRIP = 32
GATHER_BYTES = 4 << 20


def padded(block, sides, width):
    for axis, dim in sides:
        count = lax.axis_size(axis)
        forward = [(i, i + 1) for i in range(count - 1)]
        forward.append((count - 1, 0))
        backward = [(target, source) for source, target in forward]
        low = lax.ppermute(
            lax.slice_in_dim(block, block.shape[dim] - width, None, axis=dim), axis, forward
        )
        high = lax.ppermute(lax.slice_in_dim(block, 0, width, axis=dim), axis, backward)
        block = jnp.concatenate([low, block, high], axis=dim)
    return block


def tendency(center, east, west, wind_mid):
    pads = [(0, 0)] * (center.ndim - 2) + [(1, 1), (0, 0)]
    ypad = jnp.pad(center, pads)
    north = ypad[..., 2:, :]
    south = ypad[..., :-2, :]
    speed = wind_mid + 0.25 * jnp.tanh(center)
    return (
        center
        + 0.2 * (east - 2.0 * center + west)
        + 0.1 * (north - 2.0 * center + south)
        - 0.3 * speed * (east - west)
    )


def inverse_root(gram):
    order = gram.shape[0]
    ident = jnp.eye(order, dtype=jnp.float32)
    scale = jnp.sqrt(jnp.sum(gram * gram) + 1e-06)
    upper = gram / scale
    lower = ident
    for step in range(NS_ITERS):
        middle = 1.5 * ident - 0.5 * jnp.dot(lower, upper, precision=lax.Precision.HIGHEST)
        upper = jnp.dot(upper, middle, precision=lax.Precision.HIGHEST)
        lower = jnp.dot(middle, lower, precision=lax.Precision.HIGHEST)
    return lower / jnp.sqrt(scale)


def analyze(xb, cells, value, weight, count):
    order = xb.shape[0]
    slots = cells.shape[0]
    mean = jnp.sum(xb, axis=0) / order
    pert = xb - mean
    start_gram = (order - 1.0) * jnp.eye(order, dtype=jnp.float32)
    ypert = jnp.take(pert, cells, axis=1)
    ymean = jnp.take(mean, cells)
    live = (jnp.arange(slots, dtype=jnp.int32) < count).astype(jnp.float32)
    wts = weight * live
    gram = start_gram + jnp.dot(ypert * wts, ypert.T, precision=lax.Precision.HIGHEST)
    rhs = jnp.dot(ypert, wts * (value - ymean), precision=lax.Precision.HIGHEST)
    root = inverse_root(gram)
    wbar = jnp.dot(
        root, jnp.dot(root, rhs, precision=lax.Precision.HIGHEST), precision=lax.Precision.HIGHEST
    )
    trans = jnp.sqrt(order - 1.0) * root + wbar[:, None]
    return mean + jnp.dot(trans.T, pert, precision=lax.Precision.HIGHEST)


def exchanged(prior_ensemble, wind, obs_value, obs_weight, observed_cell_value, obs_count):
    stacked = jnp.concatenate([prior_ensemble, wind[None]], axis=0)
    extended = padded(stacked, (("space", 2),), SUBSTEPS)
    state = extended[:-1]
    wind_ext = extended[-1]
    for step in range(SUBSTEPS):
        edge = step + 1
        wind_mid = wind_ext[:, edge : wind_ext.shape[1] - edge]
        state = tendency(state[..., 1:-1], state[..., 2:], state[..., :-2], wind_mid)
    mem_here, latitude_lines, column_entries = state.shape
    groups = lax.axis_size("member")
    per_dev = obs_count.shape[0]
    cell_count = latitude_lines * column_entries // (groups * per_dev)
    blocks = state.reshape(mem_here, groups, per_dev, cell_count)
    arrived = lax.all_to_all(blocks, "member", split_axis=1, concat_axis=0, tiled=True)
    output_results = [
        analyze(arrived[:, 0, i], observed_cell_value[i], obs_value[i], obs_weight[i], obs_count[i])
        for i in range(per_dev)
    ]
    analysed_state = jnp.stack(output_results, axis=1)[:, None]
    returned = lax.all_to_all(analysed_state, "member", split_axis=0, concat_axis=1, tiled=True)
    return returned.reshape(mem_here, latitude_lines, column_entries)


def lane_of(shape):
    return lax.broadcasted_iota(jnp.int32, shape, 1)


def packet(u_ref, moved_wind, column):
    members, rows, _ = u_ref.shape
    lane = lane_of((8, LANES))
    beside = (lane - column) % LANES // SUBSTEPS == 1
    parts = []
    for m in range(members - 1):
        for g in range(rows // 8):
            at, to = slice(8 * g, 8 * g + 8), STRIP * m + 2 * SUBSTEPS * g
            both = jnp.where(beside, moved_wind[at], u_ref[m, at, :])
            moved = pltpu.roll(both, (to - column) % LANES, 1)
            parts.append(jnp.where(lane // (2 * SUBSTEPS) == to // (2 * SUBSTEPS), moved, 0.0))
    while len(parts) > 1:
        parts = [sum(parts[i : i + 2]) for i in range(0, len(parts), 2)]
    return parts[0]


def packets_kernel(u_hbm, wind_hbm, *refs):
    obs_hbm, (east_ref, west_ref, u_ref), obs_ref, sems = refs[:3], refs[3:6], refs[6:9], refs[9]
    members = u_hbm.shape[0]
    pairs = [(wind_hbm, u_ref.at[members])]
    pairs += [(u_hbm.at[m], u_ref.at[m]) for m in range(members)]
    pairs += [*zip(obs_hbm, obs_ref)]
    copies = [pltpu.make_async_copy(a, b, sems.at[i]) for i, (a, b) in enumerate(pairs)]
    for copy in copies:
        copy.start()
    copies[0].wait()
    moved_wind = pltpu.roll(u_ref[members], SUBSTEPS, 1)
    for copy in copies[1 : 1 + members]:
        copy.wait()
    east_ref[...] = packet(u_ref, moved_wind, LANES - SUBSTEPS)
    west_ref[...] = packet(u_ref, moved_wind, 0)
    for copy in copies[1 + members :]:
        copy.wait()


def unfolded(packet, rows, to):
    parts = [shifted(packet, 2 * SUBSTEPS * g - to) for g in range(rows // 8)]
    return jnp.concatenate(parts, axis=0)


def strips(block):
    lane = lane_of(block[0].shape)
    west = (lane % STRIP) < STRIP // 2
    parts = []
    for m, x in enumerate(block):
        low = pltpu.roll(x, (STRIP * m + SUBSTEPS) % LANES, 1)
        high = pltpu.roll(x, (STRIP * m + STRIP - SUBSTEPS) % LANES, 1)
        parts.append(jnp.where((lane // STRIP) == m, jnp.where(west, low, high), 0.0))
    return sum(parts)


def stencil(x, east, west, wind3):
    rows = x.shape[0]
    row = lax.broadcasted_iota(jnp.int32, x.shape, 0)
    north = jnp.where(row == rows - 1, 0.0, pltpu.roll(x, rows - 1, 0))
    south = jnp.where(row == 0, 0.0, pltpu.roll(x, 1, 0))
    speed = wind3 + 0.075 * jnp.tanh(x)
    return 0.4 * x + 0.2 * (east + west) + 0.1 * (north + south) - speed * (east - west)


def shifted(x, by):
    return pltpu.roll(x, -by % LANES, 1) if by else x


def substep(x, wind3):
    return stencil(x, shifted(x, 1), shifted(x, -1), wind3)


def substeps(x, wind3, count):
    at = {k: shifted(x, k) for k in range(-count, count + 1)}
    winds = {k: shifted(wind3, k) for k in range(1 - count, count)}
    for reach in range(count - 1, -1, -1):
        at = {
            k: stencil(at[k], at[k + 1], at[k - 1], winds[k]) for k in range(-reach, reach + 1)
        }
    return at[0]


def pieces(x, count):
    out = []
    for _ in range(count):
        part = x.astype(jnp.bfloat16)
        out.append(part)
        x = x - part.astype(jnp.float32)
    return out


def interior_kernel(count_ref, u_ref, cell_ref, value_ref, weight_ref, f_ref, q_ref):
    mem_here, rows = u_ref.shape[0] - 1, u_ref.shape[1]
    stride = f_ref.shape[0] // mem_here
    extra = stride - rows
    wind3 = 0.3 * u_ref[mem_here]
    slots = cell_ref.shape[1]
    slot = lax.broadcasted_iota(jnp.int32, (1, slots), 1)
    weight = jnp.where(slot < count_ref[0], weight_ref[...], 0.0)
    parts = pieces(weight, 3) + pieces(weight * value_ref[...], 3)
    sub = lax.broadcasted_iota(jnp.int32, (8, slots), 0)
    lhs = jnp.zeros((8, slots), jnp.float32)
    for k, part in enumerate(parts):
        lhs = jnp.where(sub == k, part.astype(jnp.float32), lhs)
    lhs = lhs.astype(jnp.bfloat16)
    patch_rows = extra * mem_here // 2
    for q in range(patch_rows):
        cell = lax.broadcasted_iota(jnp.int32, (LANES, slots), 0) + LANES * q
        hot = jnp.where(cell == cell_ref[...], 1.0, 0.0).astype(jnp.bfloat16)
        sums = lax.dot_general(
            lhs, hot, (((1,), (1,)), ((), ())), preferred_element_type=jnp.float32
        )
        for which in range(2):
            k = which * patch_rows + q
            line = sums[3 * which : 3 * which + 1] + sums[3 * which + 1 : 3 * which + 2]
            line = line + sums[3 * which + 2 : 3 * which + 3]
            at = (k // extra) * stride + rows + k % extra
            f_ref[at : at + 1, :] = line
    q_ref[0:rows, :] = strips([u_ref[m] for m in range(mem_here)])
    q_ref[rows : 2 * rows, :] = strips([u_ref[mem_here]] * mem_here)
    state = [u_ref[m] for m in range(mem_here)]
    for _ in range(SUBSTEPS):
        state = [substep(x, wind3) for x in state]
    for m, x in enumerate(state):
        f_ref[m * stride : m * stride + rows, :] = x


def edges_kernel(q_ref, west_ref, east_ref, f_in_ref, f_ref):
    rows = q_ref.shape[0] // 2
    lane = lane_of((rows, LANES))
    place = lane % STRIP
    full = []
    for k in range(2):
        own = q_ref[k * rows : (k + 1) * rows, :]
        west = unfolded(west_ref[...], rows, -SUBSTEPS * k)
        east = unfolded(east_ref[...], rows, STRIP - SUBSTEPS - SUBSTEPS * k)
        full.append(
            jnp.where(place < SUBSTEPS, west, jnp.where(place >= STRIP - SUBSTEPS, east, own))
        )
    x, wind3 = full[0], 0.3 * full[1]
    for _ in range(2):
        x = substeps(x, wind3, SUBSTEPS // 2)
    mem_here = LANES // STRIP
    stride = f_ref.shape[0] // mem_here
    for m in range(mem_here):
        low = pltpu.roll(x, (-STRIP * m - SUBSTEPS) % LANES, 1)
        high = pltpu.roll(x, (-STRIP * m - STRIP + SUBSTEPS) % LANES, 1)
        at = slice(m * stride, m * stride + rows)
        inside = f_in_ref[at, :]
        f_ref[at, :] = jnp.where(
            lane < SUBSTEPS, low, jnp.where(lane >= LANES - SUBSTEPS, high, inside)
        )
        at = slice(m * stride + rows, (m + 1) * stride)
        f_ref[at, :] = f_in_ref[at, :]


def visits(groups):
    near = range(2, groups - 2, 2)
    pairs = [(one + i % 2, two + i % 2) for i, (one, two) in enumerate(zip(near, reversed(near)))]
    return [(groups - 1, groups - 1), *pairs]


def sources(groups):
    taken = [(odd, even) if even % 2 else (even, odd) for even, odd in visits(groups)]
    return [(0, 0), *taken]


def analysis_kernel(dims, me_ref, cat_ref, sib_ref, o_ref, ob_ref, pert_ref, scaled_ref, mean_ref, done_ref, sems):
    mem_here, rows, groups = dims
    f32, bf16 = jnp.float32, jnp.bfloat16
    order = mem_here * groups
    height = rows // groups
    cells = height * LANES
    wide = order * groups
    stride = cat_ref.shape[0] * 2 // order
    per = LANES // order
    sets = range(groups // per)
    plain, turned = (((1,), (0,)), ((), ())), (((1,), (1,)), ((), ()))
    me = me_ref[0]

    def dot(x, y, how):
        return lax.dot_general(x, y, how, preferred_element_type=f32)

    def split(x):
        high = x.astype(bf16)
        return high, (x - high.astype(f32)).astype(bf16)

    for side, ref in enumerate((cat_ref, sib_ref)):
        for k in range(groups // 2):
            source = sources(groups)[k]
            patch = me ^ side ^ jnp.where(((me & 1) ^ side) == 0, source[0], source[1])
            base = k * mem_here * stride
            lines = [
                ref[base + m * stride + rows : base + (m + 1) * stride, :] for m in range(mem_here)
            ]
            ob_ref[pl.ds(pl.multiple_of(patch * 2 * height, 2 * height), 2 * height), :] = (
                jnp.concatenate(lines, axis=0)
            )

    for p in range(groups):
        for q in range(height):
            at = pl.ds(p * height + q, order // 2, stride=stride)
            xb = jnp.concatenate([cat_ref[at, :], sib_ref[at, :]], axis=0)
            mean = jnp.sum(xb, axis=0, keepdims=True) * (1.0 / order)
            pert = xb - mean
            lanes = slice(q * LANES, (q + 1) * LANES)
            line = p * 2 * height + q
            pert_ref[p * order : (p + 1) * order, lanes] = pert
            scaled_ref[p * order : (p + 1) * order, lanes] = pert * ob_ref[line : line + 1, :]
            mean_ref[p : p + 1, lanes] = mean
    lift = []
    for q in range(height):
        weight = ob_ref[pl.ds(q, groups, stride=2 * height), :]
        lift.append(
            ob_ref[pl.ds(height + q, groups, stride=2 * height), :]
            - weight * mean_ref[:, q * LANES : (q + 1) * LANES]
        )
    lift = jnp.concatenate(lift, axis=1)
    lift = jnp.concatenate([lift] * (16 // groups), axis=0)
    lift_high, lift_low = split(lift)

    pert_high, pert_low = split(pert_ref[...])
    scaled_high, scaled_low = split(scaled_ref[...])
    own_row = lax.broadcasted_iota(jnp.int32, (order, LANES), 0)
    lane = lax.broadcasted_iota(jnp.int32, (order, LANES), 1)
    ident = jnp.where(own_row == lane % order, 1.0, 0.0)
    tail_row = lax.broadcasted_iota(jnp.int32, (16, LANES), 0)
    tail_block = lax.broadcasted_iota(jnp.int32, (16, LANES), 1) // order
    square_row = lax.broadcasted_iota(jnp.int32, (LANES, LANES), 0) // order
    square_lane = lax.broadcasted_iota(jnp.int32, (LANES, LANES), 1) // order
    diag = jnp.where(square_row == square_lane, 1.0, 0.0).astype(bf16)
    grams, prod, middle, lower, vec, inverse = [], [], [], [], [], []
    for t in sets:
        at = slice(t * LANES, (t + 1) * LANES)
        left_high = jnp.concatenate([scaled_high[at], lift_high], axis=0)
        left_low = jnp.concatenate([scaled_low[at], lift_low], axis=0)
        right = jnp.concatenate([pert_high[at], pert_low[at]], axis=0)
        out = dot(left_high, right, turned)
        full = out[:, :LANES] + out[:, LANES:] + dot(left_low, pert_high[at], turned)
        gram = (order - 1.0) * ident
        for p in range(per):
            gram = gram + jnp.where(lane // order == p, full[p * order : (p + 1) * order], 0.0)
        rhs = jnp.sum(
            jnp.where(tail_row == tail_block + per * t, full[LANES:], 0.0), axis=0, keepdims=True
        )
        grams.append(gram)
        vec.append(jnp.where(tail_row == 0, rhs, 0.0))

    def weights(x):
        high, low = (jnp.concatenate([part] * per, axis=0) * diag for part in split(x))
        return jnp.concatenate([high, high], axis=0), low

    def product(x, right):
        xh, xl = split(x)
        return dot(jnp.concatenate([xh, xl], axis=1), right[0], plain) + dot(xh, right[1], plain)

    twice = []
    for t in sets:
        twice.append(product(jnp.concatenate([grams[t], vec[t]], axis=0), weights(grams[t])))
    for t in sets:
        square = jnp.sum(grams[t] * grams[t], axis=0, keepdims=True)
        group = lane[0:1] // order
        total = jnp.zeros((1, LANES), f32)
        for p in range(per):
            mine = group == p
            total = jnp.where(mine, jnp.sum(jnp.where(mine, square, 0.0), axis=1, keepdims=True), total)
        inverse.append(1.0 / jnp.sqrt(total + 1e-06))
        first = grams[t] * inverse[t]
        middle.append(1.5 * ident - 0.5 * first)
        prod.append(1.5 * first - (0.5 * inverse[t]) * (twice[t][:order] * inverse[t]))
        vec[t] = 1.5 * vec[t] - (0.5 * inverse[t]) * twice[t][order:]
        lower.append(middle[t][0:8])
    for step in range(NS_ITERS):
        right = [weights(middle[t]) for t in sets]
        last = step == NS_ITERS - 1
        if step:
            for t in sets:
                left = ([] if last else [prod[t]]) + [vec[t][0:8], lower[t]]
                out = product(jnp.concatenate(left, axis=0), right[t])
                if not last:
                    prod[t], out = out[:order], out[order:]
                vec[t], lower[t] = out, out[8:16]
        for t in sets:
            left = [vec[t]] if last else [prod[t], vec[t]]
            out = product(jnp.concatenate(left, axis=0), right[t])
            if not last:
                prod[t], out = out[:order], out[order:]
                middle[t] = 1.5 * ident - 0.5 * prod[t]
            vec[t] = out
    pick = lax.broadcasted_iota(jnp.int32, (groups, LANES), 0)
    tall = []
    for t in sets:
        own = lower[t] * (jnp.sqrt(inverse[t]) * (order - 1.0) ** 0.5) + vec[t][0:1] * inverse[t]
        keep = pick == lax.broadcasted_iota(jnp.int32, (groups, LANES), 1) // order + per * t
        tall.append(
            jnp.concatenate(
                [jnp.where(keep, own[i : i + 1], 0.0) for i in range(mem_here)], axis=0
            )
        )

    tall_high, tall_low = split(jnp.concatenate(tall, axis=1))
    both = dot(jnp.concatenate([tall_high, tall_low], axis=0), pert_high, plain)
    count = groups * mem_here
    out = both[:count] + both[count:] + dot(tall_high, pert_low, plain)
    copies = []
    for i in range(mem_here):
        for q in range(height):
            lanes = slice(q * LANES, (q + 1) * LANES)
            done_ref[pl.ds(i * rows + q, groups, stride=height), :] = (
                out[i * groups : (i + 1) * groups, lanes] + mean_ref[:, lanes]
            )
        at = pl.ds(i * rows, rows)
        copies.append(pltpu.make_async_copy(done_ref.at[at], o_ref.at[at], sems.at[i]))
        copies[i].start()
    for copy in copies:
        copy.wait()


def typed(shape):
    shape, dtype = shape if isinstance(shape[0], tuple) else (shape, jnp.float32)
    return jax.ShapeDtypeStruct(shape, dtype)


def kernel_call(body, *out_shapes, scratch=(), smem=(), far=(), out_space=pltpu.VMEM):
    def call(*args):
        args = [
            pltpu.with_memory_space_constraint(x, pltpu.HBM) if i in far else x
            for i, x in enumerate(args)
        ]
        specs = [
            pl.BlockSpec(
                memory_space=pltpu.SMEM if i in smem else pl.ANY if i in far else pltpu.VMEM
            )
            for i in range(len(args))
        ]
        out = pl.pallas_call(
            body,
            out_shape=[typed(shape) for shape in out_shapes],
            in_specs=specs,
            out_specs=[pl.BlockSpec(memory_space=out_space) for _ in out_shapes],
            scratch_shapes=list(scratch),
            compiler_params=pltpu.CompilerParams(vmem_limit_bytes=32 << 20),
        )(*args)
        return out[0] if len(out_shapes) == 1 else out

    return call


def gathered(prior_ensemble, wind, obs_value, obs_weight, observed_cell_value, obs_count):
    mem_here, rows, _ = prior_ensemble.shape
    groups = lax.axis_size("member")
    count = lax.axis_size("space")
    order = mem_here * groups
    height = rows // groups
    stride = rows + 2 * height // mem_here
    wide, cells = order * groups, height * LANES
    f32 = jnp.float32

    forward = [(i, (i + 1) % count) for i in range(count)]
    backward = [(i, (i - 1) % count) for i in range(count)]
    observed = (observed_cell_value, obs_value, obs_weight)
    eastern, western, both, *observed = kernel_call(
        packets_kernel,
        (8, LANES),
        (8, LANES),
        (mem_here + 1, rows, LANES),
        *[(x.shape, x.dtype) for x in observed],
        scratch=[pltpu.SemaphoreType.DMA((mem_here + 1 + len(observed),))],
        far=range(5),
    )(prior_ensemble, wind, *observed)
    east = lax.ppermute(western, "space", backward)
    west = lax.ppermute(eastern, "space", forward)
    inside, near = kernel_call(
        interior_kernel, (mem_here * stride, LANES), (2 * rows, LANES), smem=(0,)
    )(obs_count, both, *observed)
    payload = kernel_call(edges_kernel, (mem_here * stride, LANES))(near, west, east, inside)

    def swap(x, k):
        return lax.ppermute(x, "member", [(i, i ^ k) for i in range(groups)])

    held = [payload]
    for visit in visits(groups):
        move = [(i, i ^ visit[i % 2]) for i in range(groups)]
        held.append(lax.ppermute(payload, "member", move))
    cat = jnp.concatenate(held, axis=0)
    first = jnp.concatenate(held[:2], axis=0)
    sibling = jnp.concatenate([swap(x, 1) for x in [first, *held[2:]]], axis=0)
    me = lax.axis_index("member").astype(jnp.int32).reshape(1)
    out = kernel_call(
        functools.partial(analysis_kernel, (mem_here, rows, groups)),
        (mem_here * rows, LANES),
        scratch=[
            pltpu.VMEM((groups * 2 * height, LANES), f32),
            pltpu.VMEM((wide, cells), f32),
            pltpu.VMEM((wide, cells), f32),
            pltpu.VMEM((groups, cells), f32),
            pltpu.VMEM((mem_here * rows, LANES), f32),
            pltpu.SemaphoreType.DMA((mem_here,)),
        ],
        smem=(0,),
        out_space=pl.ANY,
    )(me, cat, sibling)
    return out.reshape(mem_here, rows, LANES)


def local(prior_ensemble, *rest):
    mem_here, rows, columns = prior_ensemble.shape
    groups = lax.axis_size("member")
    whole_tile = 4 * mem_here * groups * rows * columns
    fits = (
        columns == LANES
        and mem_here * STRIP == LANES
        and rows % groups == 0
        and 2 * (rows // groups) % mem_here == 0
        and rows % 8 == 0
        and rows * 2 * SUBSTEPS <= 8 * STRIP
        and groups & (groups - 1) == 0
        and groups in (8, 16)
        and LANES % (mem_here * groups) == 0
        and lax.axis_size("space") % 2 == 0
        and rest[-1].shape[0] == 1
        and whole_tile <= GATHER_BYTES
    )
    return (gathered if fits else exchanged)(prior_ensemble, *rest)


def solution(mesh):
    in_specs = (
        P("member", None, "space"),
        P(None, "space"),
        P(("space", "member"), None),
        P(("space", "member"), None),
        P(("space", "member"), None),
        P(("space", "member")),
    )
    out_specs = P("member", None, "space")
    return jax.shard_map(local, mesh=mesh, in_specs=in_specs, out_specs=out_specs, check_vma=False)
```

```python
import functools

import jax
import jax.numpy as jnp
from jax import lax
from jax.experimental import pallas as pl
from jax.experimental.pallas import tpu as pltpu
from jax.sharding import PartitionSpec as P

SUBSTEPS = 4
NS_ITERS = 6
LANES = 128
STRIP = 32
GATHER_BYTES = 4 << 20


def padded(block, sides, width):
    for axis, dim in sides:
        count = lax.axis_size(axis)
        forward = [(i, i + 1) for i in range(count - 1)]
        forward.append((count - 1, 0))
        backward = [(target, source) for source, target in forward]
        low = lax.ppermute(
            lax.slice_in_dim(block, block.shape[dim] - width, None, axis=dim), axis, forward
        )
        high = lax.ppermute(lax.slice_in_dim(block, 0, width, axis=dim), axis, backward)
        block = jnp.concatenate([low, block, high], axis=dim)
    return block


def tendency(center, east, west, wind_mid):
    pads = [(0, 0)] * (center.ndim - 2) + [(1, 1), (0, 0)]
    ypad = jnp.pad(center, pads)
    north = ypad[..., 2:, :]
    south = ypad[..., :-2, :]
    speed = wind_mid + 0.25 * jnp.tanh(center)
    return (
        center
        + 0.2 * (east - 2.0 * center + west)
        + 0.1 * (north - 2.0 * center + south)
        - 0.3 * speed * (east - west)
    )


def inverse_root(gram):
    order = gram.shape[0]
    ident = jnp.eye(order, dtype=jnp.float32)
    scale = jnp.sqrt(jnp.sum(gram * gram) + 1e-06)
    upper = gram / scale
    lower = ident
    for step in range(NS_ITERS):
        middle = 1.5 * ident - 0.5 * jnp.dot(lower, upper, precision=lax.Precision.HIGHEST)
        upper = jnp.dot(upper, middle, precision=lax.Precision.HIGHEST)
        lower = jnp.dot(middle, lower, precision=lax.Precision.HIGHEST)
    return lower / jnp.sqrt(scale)


def analyze(xb, cells, value, weight, count):
    order = xb.shape[0]
    slots = cells.shape[0]
    mean = jnp.sum(xb, axis=0) / order
    pert = xb - mean
    start_gram = (order - 1.0) * jnp.eye(order, dtype=jnp.float32)
    ypert = jnp.take(pert, cells, axis=1)
    ymean = jnp.take(mean, cells)
    live = (jnp.arange(slots, dtype=jnp.int32) < count).astype(jnp.float32)
    wts = weight * live
    gram = start_gram + jnp.dot(ypert * wts, ypert.T, precision=lax.Precision.HIGHEST)
    rhs = jnp.dot(ypert, wts * (value - ymean), precision=lax.Precision.HIGHEST)
    root = inverse_root(gram)
    wbar = jnp.dot(
        root, jnp.dot(root, rhs, precision=lax.Precision.HIGHEST), precision=lax.Precision.HIGHEST
    )
    trans = jnp.sqrt(order - 1.0) * root + wbar[:, None]
    return mean + jnp.dot(trans.T, pert, precision=lax.Precision.HIGHEST)


def exchanged(prior_ensemble, wind, obs_value, obs_weight, observed_cell_value, obs_count):
    stacked = jnp.concatenate([prior_ensemble, wind[None]], axis=0)
    extended = padded(stacked, (("space", 2),), SUBSTEPS)
    state = extended[:-1]
    wind_ext = extended[-1]
    for step in range(SUBSTEPS):
        edge = step + 1
        wind_mid = wind_ext[:, edge : wind_ext.shape[1] - edge]
        state = tendency(state[..., 1:-1], state[..., 2:], state[..., :-2], wind_mid)
    mem_here, latitude_lines, column_entries = state.shape
    groups = lax.axis_size("member")
    per_dev = obs_count.shape[0]
    cell_count = latitude_lines * column_entries // (groups * per_dev)
    blocks = state.reshape(mem_here, groups, per_dev, cell_count)
    arrived = lax.all_to_all(blocks, "member", split_axis=1, concat_axis=0, tiled=True)
    output_results = [
        analyze(arrived[:, 0, i], observed_cell_value[i], obs_value[i], obs_weight[i], obs_count[i])
        for i in range(per_dev)
    ]
    analysed_state = jnp.stack(output_results, axis=1)[:, None]
    returned = lax.all_to_all(analysed_state, "member", split_axis=0, concat_axis=1, tiled=True)
    return returned.reshape(mem_here, latitude_lines, column_entries)


def lane_of(shape):
    return lax.broadcasted_iota(jnp.int32, shape, 1)


def packet(u_ref, moved_wind, column):
    members, rows, _ = u_ref.shape
    lane = lane_of((8, LANES))
    beside = (lane - column) % LANES // SUBSTEPS == 1
    parts = []
    for m in range(members - 1):
        for g in range(rows // 8):
            at, to = slice(8 * g, 8 * g + 8), STRIP * m + 2 * SUBSTEPS * g
            both = jnp.where(beside, moved_wind[at], u_ref[m, at, :])
            moved = pltpu.roll(both, (to - column) % LANES, 1)
            parts.append(jnp.where(lane // (2 * SUBSTEPS) == to // (2 * SUBSTEPS), moved, 0.0))
    while len(parts) > 1:
        parts = [sum(parts[i : i + 2]) for i in range(0, len(parts), 2)]
    return parts[0]


def packets_kernel(u_hbm, wind_hbm, *refs):
    obs_hbm, (east_ref, west_ref, u_ref), obs_ref, sems = refs[:3], refs[3:6], refs[6:9], refs[9]
    members = u_hbm.shape[0]
    pairs = [(wind_hbm, u_ref.at[members])]
    pairs += [(u_hbm.at[m : m + 2], u_ref.at[m : m + 2]) for m in range(0, members, 2)]
    pairs += [*zip(obs_hbm, obs_ref)]
    copies = [pltpu.make_async_copy(a, b, sems.at[i]) for i, (a, b) in enumerate(pairs)]
    for copy in copies:
        copy.start()
    copies[0].wait()
    moved_wind = pltpu.roll(u_ref[members], SUBSTEPS, 1)
    for copy in copies[1 : 1 + members // 2]:
        copy.wait()
    east_ref[...] = packet(u_ref, moved_wind, LANES - SUBSTEPS)
    west_ref[...] = packet(u_ref, moved_wind, 0)
    for copy in copies[1 + members // 2 :]:
        copy.wait()


def unfolded(packet, rows, to):
    parts = [shifted(packet, 2 * SUBSTEPS * g - to) for g in range(rows // 8)]
    return jnp.concatenate(parts, axis=0)


def strips(block):
    lane = lane_of(block[0].shape)
    west = (lane % STRIP) < STRIP // 2
    parts = []
    for m, x in enumerate(block):
        low = pltpu.roll(x, (STRIP * m + SUBSTEPS) % LANES, 1)
        high = pltpu.roll(x, (STRIP * m + STRIP - SUBSTEPS) % LANES, 1)
        parts.append(jnp.where((lane // STRIP) == m, jnp.where(west, low, high), 0.0))
    return sum(parts)


def stencil(x, east, west, wind3):
    rows = x.shape[0]
    row = lax.broadcasted_iota(jnp.int32, x.shape, 0)
    north = jnp.where(row == rows - 1, 0.0, pltpu.roll(x, rows - 1, 0))
    south = jnp.where(row == 0, 0.0, pltpu.roll(x, 1, 0))
    speed = wind3 + 0.075 * jnp.tanh(x)
    return 0.4 * x + 0.2 * (east + west) + 0.1 * (north + south) - speed * (east - west)


def shifted(x, by):
    return pltpu.roll(x, -by % LANES, 1) if by else x


def substep(x, wind3):
    return stencil(x, shifted(x, 1), shifted(x, -1), wind3)


def substeps(x, wind3, count):
    at = {k: shifted(x, k) for k in range(-count, count + 1)}
    winds = {k: shifted(wind3, k) for k in range(1 - count, count)}
    for reach in range(count - 1, -1, -1):
        at = {
            k: stencil(at[k], at[k + 1], at[k - 1], winds[k]) for k in range(-reach, reach + 1)
        }
    return at[0]


def pieces(x, count):
    out = []
    for _ in range(count):
        part = x.astype(jnp.bfloat16)
        out.append(part)
        x = x - part.astype(jnp.float32)
    return out


def interior_kernel(count_ref, u_ref, cell_ref, value_ref, weight_ref, f_ref, q_ref):
    mem_here, rows = u_ref.shape[0] - 1, u_ref.shape[1]
    stride = f_ref.shape[0] // mem_here
    extra = stride - rows
    wind3 = 0.3 * u_ref[mem_here]
    slots = cell_ref.shape[1]
    slot = lax.broadcasted_iota(jnp.int32, (1, slots), 1)
    weight = jnp.where(slot < count_ref[0], weight_ref[...], 0.0)
    parts = pieces(weight, 3) + pieces(weight * value_ref[...], 3)
    sub = lax.broadcasted_iota(jnp.int32, (8, slots), 0)
    lhs = jnp.zeros((8, slots), jnp.float32)
    for k, part in enumerate(parts):
        lhs = jnp.where(sub == k, part.astype(jnp.float32), lhs)
    lhs = lhs.astype(jnp.bfloat16)
    patch_rows = extra * mem_here // 2
    for q in range(patch_rows):
        cell = lax.broadcasted_iota(jnp.int32, (LANES, slots), 0) + LANES * q
        hot = jnp.where(cell == cell_ref[...], 1.0, 0.0).astype(jnp.bfloat16)
        sums = lax.dot_general(
            lhs, hot, (((1,), (1,)), ((), ())), preferred_element_type=jnp.float32
        )
        for which in range(2):
            k = which * patch_rows + q
            line = sums[3 * which : 3 * which + 1] + sums[3 * which + 1 : 3 * which + 2]
            line = line + sums[3 * which + 2 : 3 * which + 3]
            at = (k // extra) * stride + rows + k % extra
            f_ref[at : at + 1, :] = line
    q_ref[0:rows, :] = strips([u_ref[m] for m in range(mem_here)])
    q_ref[rows : 2 * rows, :] = strips([u_ref[mem_here]] * mem_here)
    state = [u_ref[m] for m in range(mem_here)]
    for _ in range(SUBSTEPS):
        state = [substep(x, wind3) for x in state]
    for m, x in enumerate(state):
        f_ref[m * stride : m * stride + rows, :] = x


def edges_kernel(q_ref, west_ref, east_ref, f_in_ref, f_ref):
    rows = q_ref.shape[0] // 2
    lane = lane_of((rows, LANES))
    place = lane % STRIP
    full = []
    for k in range(2):
        own = q_ref[k * rows : (k + 1) * rows, :]
        west = unfolded(west_ref[...], rows, -SUBSTEPS * k)
        east = unfolded(east_ref[...], rows, STRIP - SUBSTEPS - SUBSTEPS * k)
        full.append(
            jnp.where(place < SUBSTEPS, west, jnp.where(place >= STRIP - SUBSTEPS, east, own))
        )
    x, wind3 = full[0], 0.3 * full[1]
    for _ in range(2):
        x = substeps(x, wind3, SUBSTEPS // 2)
    mem_here = LANES // STRIP
    stride = f_ref.shape[0] // mem_here
    for m in range(mem_here):
        low = pltpu.roll(x, (-STRIP * m - SUBSTEPS) % LANES, 1)
        high = pltpu.roll(x, (-STRIP * m - STRIP + SUBSTEPS) % LANES, 1)
        at = slice(m * stride, m * stride + rows)
        inside = f_in_ref[at, :]
        f_ref[at, :] = jnp.where(
            lane < SUBSTEPS, low, jnp.where(lane >= LANES - SUBSTEPS, high, inside)
        )
        at = slice(m * stride + rows, (m + 1) * stride)
        f_ref[at, :] = f_in_ref[at, :]


def visits(groups):
    chips = [groups - 2, *range(2, groups - 2, 2)]
    return [0, *[chip + (i + 1) % 2 for i, chip in enumerate(chips)]]


def analysis_kernel(dims, me_ref, cat_ref, sib_ref, o_ref, ob_ref, pert_ref, scaled_ref, mean_ref, done_ref, sems):
    mem_here, rows, groups = dims
    f32, bf16 = jnp.float32, jnp.bfloat16
    order = mem_here * groups
    height = rows // groups
    cells = height * LANES
    wide = order * groups
    stride = cat_ref.shape[0] * 2 // order
    per = LANES // order
    sets = range(groups // per)
    plain, turned = (((1,), (0,)), ((), ())), (((1,), (1,)), ((), ()))
    me = me_ref[0]

    def dot(x, y, how):
        return lax.dot_general(x, y, how, preferred_element_type=f32)

    def split(x):
        high = x.astype(bf16)
        return high, (x - high.astype(f32)).astype(bf16)

    for side, ref in enumerate((cat_ref, sib_ref)):
        for k in range(groups // 2):
            patch = me ^ (visits(groups)[k] ^ side)
            base = k * mem_here * stride
            lines = [
                ref[base + m * stride + rows : base + (m + 1) * stride, :] for m in range(mem_here)
            ]
            ob_ref[pl.ds(pl.multiple_of(patch * 2 * height, 2 * height), 2 * height), :] = (
                jnp.concatenate(lines, axis=0)
            )

    for p in range(groups):
        for q in range(height):
            at = pl.ds(p * height + q, order // 2, stride=stride)
            xb = jnp.concatenate([cat_ref[at, :], sib_ref[at, :]], axis=0)
            mean = jnp.sum(xb, axis=0, keepdims=True) * (1.0 / order)
            pert = xb - mean
            lanes = slice(q * LANES, (q + 1) * LANES)
            line = p * 2 * height + q
            pert_ref[p * order : (p + 1) * order, lanes] = pert
            scaled_ref[p * order : (p + 1) * order, lanes] = pert * ob_ref[line : line + 1, :]
            mean_ref[p : p + 1, lanes] = mean
    lift = []
    for q in range(height):
        weight = ob_ref[pl.ds(q, groups, stride=2 * height), :]
        lift.append(
            ob_ref[pl.ds(height + q, groups, stride=2 * height), :]
            - weight * mean_ref[:, q * LANES : (q + 1) * LANES]
        )
    lift = jnp.concatenate(lift, axis=1)
    lift = jnp.concatenate([lift] * (16 // groups), axis=0)
    lift_high, lift_low = split(lift)

    pert_high, pert_low = split(pert_ref[...])
    scaled_high, scaled_low = split(scaled_ref[...])
    own_row = lax.broadcasted_iota(jnp.int32, (order, LANES), 0)
    lane = lax.broadcasted_iota(jnp.int32, (order, LANES), 1)
    ident = jnp.where(own_row == lane % order, 1.0, 0.0)
    tail_row = lax.broadcasted_iota(jnp.int32, (16, LANES), 0)
    tail_block = lax.broadcasted_iota(jnp.int32, (16, LANES), 1) // order
    square_row = lax.broadcasted_iota(jnp.int32, (LANES, LANES), 0) // order
    square_lane = lax.broadcasted_iota(jnp.int32, (LANES, LANES), 1) // order
    diag = jnp.where(square_row == square_lane, 1.0, 0.0).astype(bf16)
    grams, prod, middle, lower, vec, inverse = [], [], [], [], [], []
    for t in sets:
        at = slice(t * LANES, (t + 1) * LANES)
        left_high = jnp.concatenate([scaled_high[at], lift_high], axis=0)
        left_low = jnp.concatenate([scaled_low[at], lift_low], axis=0)
        right = jnp.concatenate([pert_high[at], pert_low[at]], axis=0)
        out = dot(left_high, right, turned)
        full = out[:, :LANES] + out[:, LANES:] + dot(left_low, pert_high[at], turned)
        gram = (order - 1.0) * ident
        for p in range(per):
            gram = gram + jnp.where(lane // order == p, full[p * order : (p + 1) * order], 0.0)
        rhs = jnp.sum(
            jnp.where(tail_row == tail_block + per * t, full[LANES:], 0.0), axis=0, keepdims=True
        )
        grams.append(gram)
        vec.append(jnp.where(tail_row == 0, rhs, 0.0))

    def weights(x):
        high, low = (jnp.concatenate([part] * per, axis=0) * diag for part in split(x))
        return jnp.concatenate([high, high], axis=0), low

    def product(x, right):
        xh, xl = split(x)
        return dot(jnp.concatenate([xh, xl], axis=1), right[0], plain) + dot(xh, right[1], plain)

    twice = []
    for t in sets:
        twice.append(product(jnp.concatenate([grams[t], vec[t]], axis=0), weights(grams[t])))
    for t in sets:
        square = jnp.sum(grams[t] * grams[t], axis=0, keepdims=True)
        group = lane[0:1] // order
        total = jnp.zeros((1, LANES), f32)
        for p in range(per):
            mine = group == p
            total = jnp.where(mine, jnp.sum(jnp.where(mine, square, 0.0), axis=1, keepdims=True), total)
        inverse.append(1.0 / jnp.sqrt(total + 1e-06))
        first = grams[t] * inverse[t]
        middle.append(1.5 * ident - 0.5 * first)
        prod.append(1.5 * first - (0.5 * inverse[t]) * (twice[t][:order] * inverse[t]))
        vec[t] = 1.5 * vec[t] - (0.5 * inverse[t]) * twice[t][order:]
        lower.append(middle[t][0:8])
    for step in range(NS_ITERS):
        right = [weights(middle[t]) for t in sets]
        last = step == NS_ITERS - 1
        if step:
            for t in sets:
                left = ([] if last else [prod[t]]) + [vec[t][0:8], lower[t]]
                out = product(jnp.concatenate(left, axis=0), right[t])
                if not last:
                    prod[t], out = out[:order], out[order:]
                vec[t], lower[t] = out, out[8:16]
        for t in sets:
            left = [vec[t]] if last else [prod[t], vec[t]]
            out = product(jnp.concatenate(left, axis=0), right[t])
            if not last:
                prod[t], out = out[:order], out[order:]
                middle[t] = 1.5 * ident - 0.5 * prod[t]
            vec[t] = out
    pick = lax.broadcasted_iota(jnp.int32, (groups, LANES), 0)
    tall = []
    for t in sets:
        own = lower[t] * (jnp.sqrt(inverse[t]) * (order - 1.0) ** 0.5) + vec[t][0:1] * inverse[t]
        keep = pick == lax.broadcasted_iota(jnp.int32, (groups, LANES), 1) // order + per * t
        tall.append(
            jnp.concatenate(
                [jnp.where(keep, own[i : i + 1], 0.0) for i in range(mem_here)], axis=0
            )
        )

    tall_high, tall_low = split(jnp.concatenate(tall, axis=1))
    both = dot(jnp.concatenate([tall_high, tall_low], axis=0), pert_high, plain)
    count = groups * mem_here
    out = both[:count] + both[count:] + dot(tall_high, pert_low, plain)
    copies = []
    for i in range(mem_here):
        for q in range(height):
            lanes = slice(q * LANES, (q + 1) * LANES)
            done_ref[pl.ds(i * rows + q, groups, stride=height), :] = (
                out[i * groups : (i + 1) * groups, lanes] + mean_ref[:, lanes]
            )
        at = pl.ds(i * rows, rows)
        copies.append(pltpu.make_async_copy(done_ref.at[at], o_ref.at[at], sems.at[i]))
        copies[i].start()
    for copy in copies:
        copy.wait()


def typed(shape):
    shape, dtype = shape if isinstance(shape[0], tuple) else (shape, jnp.float32)
    return jax.ShapeDtypeStruct(shape, dtype)


def kernel_call(body, *out_shapes, scratch=(), smem=(), far=(), out_space=pltpu.VMEM):
    def call(*args):
        args = [
            pltpu.with_memory_space_constraint(x, pltpu.HBM) if i in far else x
            for i, x in enumerate(args)
        ]
        specs = [
            pl.BlockSpec(
                memory_space=pltpu.SMEM if i in smem else pl.ANY if i in far else pltpu.VMEM
            )
            for i in range(len(args))
        ]
        out = pl.pallas_call(
            body,
            out_shape=[typed(shape) for shape in out_shapes],
            in_specs=specs,
            out_specs=[pl.BlockSpec(memory_space=out_space) for _ in out_shapes],
            scratch_shapes=list(scratch),
            compiler_params=pltpu.CompilerParams(vmem_limit_bytes=32 << 20),
        )(*args)
        return out[0] if len(out_shapes) == 1 else out

    return call


def gathered(prior_ensemble, wind, obs_value, obs_weight, observed_cell_value, obs_count):
    mem_here, rows, _ = prior_ensemble.shape
    groups = lax.axis_size("member")
    count = lax.axis_size("space")
    order = mem_here * groups
    height = rows // groups
    stride = rows + 2 * height // mem_here
    wide, cells = order * groups, height * LANES
    f32 = jnp.float32

    forward = [(i, (i + 1) % count) for i in range(count)]
    backward = [(i, (i - 1) % count) for i in range(count)]
    observed = (observed_cell_value, obs_value, obs_weight)
    eastern, western, both, *observed = kernel_call(
        packets_kernel,
        (8, LANES),
        (8, LANES),
        (mem_here + 1, rows, LANES),
        *[(x.shape, x.dtype) for x in observed],
        scratch=[pltpu.SemaphoreType.DMA((mem_here + 1 + len(observed),))],
        far=range(5),
    )(prior_ensemble, wind, *observed)
    east = lax.ppermute(western, "space", backward)
    west = lax.ppermute(eastern, "space", forward)
    inside, near = kernel_call(
        interior_kernel, (mem_here * stride, LANES), (2 * rows, LANES), smem=(0,)
    )(obs_count, both, *observed)
    payload = kernel_call(edges_kernel, (mem_here * stride, LANES))(near, west, east, inside)

    def swap(x, k):
        return lax.ppermute(x, "member", [(i, i ^ k) for i in range(groups)])

    held = [payload] + [swap(payload, k) for k in visits(groups)[1:]]
    cat = jnp.concatenate(held, axis=0)
    first = jnp.concatenate(held[:2], axis=0)
    sibling = jnp.concatenate([swap(x, 1) for x in [first, *held[2:]]], axis=0)
    me = lax.axis_index("member").astype(jnp.int32).reshape(1)
    out = kernel_call(
        functools.partial(analysis_kernel, (mem_here, rows, groups)),
        (mem_here * rows, LANES),
        scratch=[
            pltpu.VMEM((groups * 2 * height, LANES), f32),
            pltpu.VMEM((wide, cells), f32),
            pltpu.VMEM((wide, cells), f32),
            pltpu.VMEM((groups, cells), f32),
            pltpu.VMEM((mem_here * rows, LANES), f32),
            pltpu.SemaphoreType.DMA((mem_here,)),
        ],
        smem=(0,),
        out_space=pl.ANY,
    )(me, cat, sibling)
    return out.reshape(mem_here, rows, LANES)


def local(prior_ensemble, *rest):
    mem_here, rows, columns = prior_ensemble.shape
    groups = lax.axis_size("member")
    whole_tile = 4 * mem_here * groups * rows * columns
    fits = (
        columns == LANES
        and mem_here * STRIP == LANES
        and rows % groups == 0
        and 2 * (rows // groups) % mem_here == 0
        and rows % 8 == 0
        and rows * 2 * SUBSTEPS <= 8 * STRIP
        and groups & (groups - 1) == 0
        and groups in (8, 16)
        and LANES % (mem_here * groups) == 0
        and lax.axis_size("space") % 2 == 0
        and rest[-1].shape[0] == 1
        and whole_tile <= GATHER_BYTES
    )
    return (gathered if fits else exchanged)(prior_ensemble, *rest)


def solution(mesh):
    in_specs = (
        P("member", None, "space"),
        P(None, "space"),
        P(("space", "member"), None),
        P(("space", "member"), None),
        P(("space", "member"), None),
        P(("space", "member")),
    )
    out_specs = P("member", None, "space")
    return jax.shard_map(local, mesh=mesh, in_specs=in_specs, out_specs=out_specs, check_vma=False)
```
